512 devices in a mesh: chain: 4 (over y), tp: 32 (over z, core), dec: 4 (over x).
Axes of the slice: x: 4, y: 4, z: 16, core: 2. Of those that a mesh axis runs over, the one named last changes fastest.
Arguments:
- query_comp: bfloat16 [4, 2048, 1536], P('dec', ('chain', 'tp')), may hold values from -6 to 6
- latent_rows: bfloat16 [4, 16, 128, 512], P('dec', 'chain', 'tp'), may hold values from -6 to 6
- rope_keys: bfloat16 [4, 16, 128, 64], P('dec', 'chain', 'tp'), may hold values from -6 to 6
- latent_gain: float32 [512], replicated, may hold values from 0.1 to 1.9
- query_up: bfloat16 [1536, 12288], P(None, 'tp'), may hold values from -0.15625 to 0.15625
- absorb_key: bfloat16 [64, 128, 512], P('tp'), may hold values from -17 to 17
- absorb_value: bfloat16 [64, 512, 128], P('tp'), may hold values from -0.25 to 0.25
- out_proj: bfloat16 [8192, 3584], P('tp'), may hold values from -0.0625 to 0.0625
- page_owner: int32 [4, 16], P('dec', 'chain'), may hold values from 0 to 3, as said below
- page_slot: int32 [4, 16], P('dec', 'chain'), may hold values from 0 to 7
Outputs:
- layer_output: bfloat16 [4, 2048, 3584], P('dec', ('chain', 'tp'))
- cache_latent: bfloat16 [4, 4, 8, 128, 512], P('dec', 'chain', None, 'tp')
- cache_rope: bfloat16 [4, 4, 8, 128, 64], P('dec', 'chain', None, 'tp')
The draws below stay inside these ranges and needn't reach their ends.
Inputs may be any that keep to these rules, and one draw needn't show every extreme that they name: `page_owner`: among the pages of one block index of all prompts, no two share an owner and a slot.
All inputs are finite; a program needn't handle non-finite values.
Results may differ from the reference program's by a relative error of at most 0.035.
Values may be sent and summed in bfloat16 or wider, within the bound.
No kernel may reach another device: no remote copies, remote signals or barrier semaphores. Data moves between devices by JAX's collectives and lax.ppermute only.
A program may use at most 64 MiB of HBM per device.

```python
import jax
import jax.numpy as jnp
from jax import lax

D = 3584
H_DEV = 2
HEADS = 64
QL = 1536
NOPE = 128
ROPE = 64
LAT = 512
VH = 128
PAGE = 128
PAGES_CH = 4
TOKENS = 2048
PAGES = 16
SEQS = 4
SLOTS = 8
N_CHAIN = 4
N_TP = 32
N_DEC = 4


def page_pairs(key):
    chosen = []
    for section_index in range(N_CHAIN):
        section_key = jax.random.fold_in(key, 100 + section_index)
        shuffle = jax.random.permutation(section_key, N_DEC * SLOTS)[:N_DEC * PAGES_CH]
        chosen.append(shuffle.reshape(N_DEC, PAGES_CH))
    return jnp.concatenate(chosen, axis=1).astype(jnp.int32)


def draw_page_owner(key, part):
    return (page_pairs(key) // SLOTS).astype(jnp.int32)


def draw_page_slot(key, part):
    return (page_pairs(key) % SLOTS).astype(jnp.int32)


def draw_absorb_key(key, part):
    key = jax.random.fold_in(key, 7)
    values = jax.random.truncated_normal(jax.random.fold_in(key, 1), -4.0, 4.0, (HEADS, NOPE, LAT), jnp.float32)
    values = values * NOPE ** (-0.5)
    return values.astype(jnp.bfloat16)


def shard_levels(stream_key, dims, split, low, high):
    gain, own = 1.0, jax.random.fold_in(stream_key, 6)
    for position, parts in split:
        steps = jnp.exp(jax.random.uniform(jax.random.fold_in(own, position), (parts,), jnp.float32, low / len(split), high / len(split)))
        gain = gain * jnp.repeat(steps, dims[position] // parts).reshape([-1 if axis == position else 1 for axis in range(len(dims))])
    return gain


def normal_values(key, dims, deviation, reach, cuts=(), held_as=jnp.bfloat16):
    entries = jax.random.normal(key, dims, jnp.float32) * deviation
    if len(cuts) > 0:
        entries = shard_levels(key, dims, cuts, -0.22, 0.18) * entries
    return jnp.clip(entries, min=-reach, max=reach).astype(held_as)


def setup_inputs(seed: int = 0) -> dict:
    key_list = jax.random.split(jax.random.key(seed), 11)
    return {
        "query_comp": normal_values(key_list[0], (SEQS, TOKENS, QL), 1.0, 6.0, ((0, 4), (1, 128))),
        "latent_rows": normal_values(key_list[1], (SEQS, PAGES, PAGE, LAT), 1.0, 6.0, ((0, 4), (1, 4), (2, 32))),
        "rope_keys": normal_values(key_list[2], (SEQS, PAGES, PAGE, ROPE), 1.0, 6.0, ((0, 4), (1, 4), (2, 32))),
        "latent_gain": jnp.clip(1.0 + 0.18 * jax.random.normal(key_list[3], (LAT,), jnp.float32), 0.1, 1.9),
        "query_up": normal_values(key_list[4], (QL, HEADS * (NOPE + ROPE)), QL ** -0.5, 0.15625, ((1, 32),)),
        "absorb_key": draw_absorb_key(jax.random.fold_in(key_list[10], 71), 0),
        "absorb_value": normal_values(key_list[6], (HEADS, LAT, VH), LAT ** -0.5, 0.25, ((0, 32),)),
        "out_proj": normal_values(key_list[7], (HEADS * VH, D), (HEADS * VH) ** -0.5, 0.0625, ((0, 32),)),
        "page_owner": draw_page_owner(jax.random.fold_in(key_list[10], 71), 0),
        "page_slot": draw_page_slot(jax.random.fold_in(key_list[10], 71), 0),
    }


def rotate(values, where_at):
    full_width = values.shape[-1]
    half_width = full_width // 2
    frequency = 10000.0 ** (-(jnp.arange(half_width).astype(jnp.float32) * 2.0 / full_width))
    angles = where_at.astype(jnp.float32)[:, None] * frequency[None, :]
    angles = angles.reshape((where_at.shape[0],) + (1,) * (values.ndim - 2) + (half_width,))
    cosine = jnp.cos(angles)
    sine_part = jnp.sin(angles)
    first_half = values[..., :half_width]
    second_half = values[..., half_width:]
    return jnp.concatenate([first_half * cosine - second_half * sine_part, second_half * cosine + first_half * sine_part], -1)

def reference(query_comp, latent_rows, rope_keys, latent_gain, query_up, absorb_key, absorb_value, out_proj, page_owner, page_slot):
    positions = jnp.arange(TOKENS, dtype=jnp.int32)
    latent = latent_rows.astype(jnp.float32)
    normed = (latent * lax.rsqrt(lax.optimization_barrier(jnp.mean(latent * latent, -1, keepdims=True)) + 1e-06) * latent_gain.astype(jnp.float32)).astype(jnp.bfloat16)
    rotated = jax.vmap(lambda block: rotate(block.reshape(TOKENS, ROPE).astype(jnp.float32), positions))(rope_keys).astype(jnp.bfloat16)
    flat_latent = normed.reshape(SEQS, TOKENS, LAT)
    scale = (NOPE + ROPE) ** (-0.5)
    causal = positions[None, :] <= positions[:, None]

    def one_sequence(items):
        compressed, keys_lat, keys_rope = items
        query = jnp.dot(compressed, query_up, preferred_element_type=jnp.float32).astype(jnp.bfloat16)
        query = query.reshape(TOKENS, HEADS, NOPE + ROPE)
        query_lat = jnp.einsum('thn,hnc->htc', query[..., :NOPE].astype(jnp.float32), absorb_key.astype(jnp.float32)).astype(jnp.bfloat16)
        query_rot = jnp.transpose(rotate(query[..., NOPE:].astype(jnp.float32), positions), (1, 0, 2)).astype(jnp.bfloat16)

        def one_head(triple):
            lat_head, rope_head, value_head = triple
            scores = (jnp.dot(lat_head, keys_lat.T, preferred_element_type=jnp.float32) + jnp.dot(rope_head, keys_rope.T, preferred_element_type=jnp.float32)) * scale
            highest = lax.optimization_barrier(jnp.max(jnp.where(causal, scores, -jnp.inf), -1, keepdims=True))
            weights = jnp.where(causal, jnp.exp(scores - highest), 0.0)
            totals = lax.optimization_barrier(jnp.sum(weights, -1, keepdims=True))
            mixed = (jnp.dot(weights.astype(jnp.bfloat16), keys_lat, preferred_element_type=jnp.float32) / totals).astype(jnp.bfloat16)
            return jnp.dot(mixed, value_head, preferred_element_type=jnp.float32).astype(jnp.bfloat16)
        heads_out = lax.map(one_head, (query_lat, query_rot, absorb_value))
        joined = jnp.transpose(heads_out, (1, 0, 2)).reshape(TOKENS, N_TP, H_DEV * VH)
        groups = jnp.transpose(joined, (1, 0, 2))
        group_proj = out_proj.reshape(N_TP, H_DEV * VH, D)

        def add_group(running, pair):
            group_rows, proj_rows = pair
            partial_sum = jnp.dot(group_rows, proj_rows, preferred_element_type=jnp.float32).astype(jnp.bfloat16)
            partial_sum = lax.optimization_barrier(partial_sum)
            return (running + partial_sum.astype(jnp.float32), None)
        summed, unused = lax.scan(add_group, jnp.zeros((TOKENS, D), jnp.float32), (groups, group_proj))
        return summed.astype(jnp.bfloat16)
    layer_output = lax.map(one_sequence, (query_comp, flat_latent, rotated))
    block_of = (jnp.arange(PAGES, dtype=jnp.int32) // PAGES_CH).astype(jnp.int32)
    rope_pages = rotated.reshape(SEQS, PAGES, PAGE, ROPE)
    cache_latent = jnp.zeros((N_DEC, N_CHAIN, SLOTS, PAGE, LAT), jnp.bfloat16).at[page_owner, block_of[None, :], page_slot].set(normed)
    cache_rope = jnp.zeros((N_DEC, N_CHAIN, SLOTS, PAGE, ROPE), jnp.bfloat16).at[page_owner, block_of[None, :], page_slot].set(rope_pages)
    return (layer_output, cache_latent, cache_rope)
```

```python
import functools

import jax
import jax.numpy as jnp
import numpy as np
from jax import lax
from jax.experimental import pallas as pl
from jax.experimental.pallas import tpu as pltpu
from jax.sharding import Mesh, PartitionSpec as P

BF = jnp.bfloat16
F32 = jnp.float32
LOG2E = 1.4426950408889634
Z = ("zh", "zl")
TP = ("zh", "zl", "core")
NEG = -1e30


def rope_tables(where_at, full_width):
    half = full_width // 2
    frequency = 10000.0 ** (-(jnp.arange(half).astype(F32) * 2.0 / full_width))
    angles = where_at.astype(F32)[:, None] * frequency[None, :]
    cosine, sine = jnp.cos(angles), jnp.sin(angles)
    return (
        jnp.concatenate([cosine, cosine], -1),
        jnp.concatenate([-sine, sine], -1),
    )


def swap_halves(v):
    half = v.shape[-1] // 2
    return jnp.concatenate([v[..., half:], v[..., :half]], -1)


def shift_z(x, step):
    n = lax.axis_size("zh") * lax.axis_size("zl")
    return lax.ppermute(x, Z, [(i, (i + step) % n) for i in range(n)])


def swap_core(x):
    return lax.ppermute(x, "core", [(0, 1), (1, 0)])


def spread(x, axis):
    n = lax.axis_size(axis)
    return lax.all_to_all(jnp.broadcast_to(x[None], (n,) + x.shape), axis, 0, 0, tiled=True)


def gather_classes(g):
    half = g.shape[0] // 2
    return (
        g,
        shift_z(g, -1),
        shift_z(g[:half], -2),
        shift_z(g[half:], 2),
        shift_z(g, 1),
    )


def query_kernel(g0, g1, g2a, g2b, g3, wq0, wq1, ak0, ak1, cos_ref, sin_ref, out_ref, x_ref, *, nope, rope):
    at = 0
    for g in (g0, g1, g2a, g2b, g3):
        n = g.shape[0]
        x_ref[at : at + n, :] = g[...]
        at += n
    x = x_ref[...]
    rows = x.shape[0]
    lat = ak0.shape[-1]
    head = 0
    for wq, ak in ((wq0, ak0), (wq1, ak1)):
        q = jnp.dot(x, wq[...], preferred_element_type=F32).astype(BF)
        for h in range(ak.shape[0]):
            base = h * (nope + rope)
            r0 = head * rows
            out_ref[r0 : r0 + rows, :lat] = jnp.dot(
                q[:, base : base + nope], ak[h], preferred_element_type=F32
            ).astype(BF)
            rot = q[:, base + nope : base + nope + rope].astype(F32)
            out_ref[r0 : r0 + rows, lat:] = (
                rot * cos_ref[...] + swap_halves(rot) * sin_ref[...]
            ).astype(BF)
            head += 1


def attend_kernel(
    where_ref, q_ref, kown, kown2, k1, k12, k2, k22, k3, k32, av0, av1, op0, op1, out_ref,
    m_ref, l_ref, acc_ref, ho_ref, *, rows, lat, scale, lay,
):
    chain, zl, core = where_ref[0], where_ref[1], where_ref[2]
    nzh, nzl, part, qrows, pages = lay
    s2 = scale * LOG2E
    vh = av0.shape[-1]
    heads = q_ref.shape[0] // rows
    half_keys = kown.shape[0]

    def key_pos(idx, kcore):
        d = idx // (nzh * pages * part)
        zh = (idx // (pages * part)) % nzh
        page = (idx // part) % pages
        r = idx % part
        z = zh * nzl + (zl + d) % nzl
        return page * (nzh * nzl * 2 * part) + z * (2 * part) + kcore * part + r

    def query_pos(idx):
        d = idx // (nzh * qrows)
        zh = (idx // qrows) % nzh
        j = idx % qrows
        z = zh * nzl + (zl + d) % nzl
        return z * (2 * qrows) + core * qrows + j

    qp = query_pos(lax.broadcasted_iota(jnp.int32, (rows, 1), 0))
    kidx = lax.broadcasted_iota(jnp.int32, (1, half_keys), 1)
    ok_a = key_pos(kidx, core) <= qp
    ok_b = key_pos(kidx, 1 - core) <= qp
    nt = (((1,), (1,)), ((), ()))

    def scores(q, ka, kb, masked):
        sa = lax.dot_general(q, ka, nt, preferred_element_type=F32)
        sb = lax.dot_general(q, kb, nt, preferred_element_type=F32)
        if masked:
            sa = jnp.where(ok_a, sa, NEG)
            sb = jnp.where(ok_b, sb, NEG)
        return sa, sb

    def step(q, kar, kbr, first):
        ka, kb = kar[...], kbr[...]
        sa, sb = scores(q, ka, kb, first)
        top = jnp.maximum(jnp.max(sa, -1, keepdims=True), jnp.max(sb, -1, keepdims=True))
        m = top if first else jnp.maximum(m_ref[...], top)
        pa = jnp.exp2((sa - m) * s2)
        pb = jnp.exp2((sb - m) * s2)
        total = jnp.sum(pa, -1, keepdims=True) + jnp.sum(pb, -1, keepdims=True)
        pv = jnp.dot(pa.astype(BF), ka[:, :lat], preferred_element_type=F32) + jnp.dot(
            pb.astype(BF), kb[:, :lat], preferred_element_type=F32
        )
        if first:
            l_ref[...] = total
            acc_ref[...] = pv
        else:
            fade = jnp.exp2((m_ref[...] - m) * s2)
            l_ref[...] = l_ref[...] * fade + total
            acc_ref[...] = acc_ref[...] * fade + pv
        m_ref[...] = m

    for h in range(heads):
        q = q_ref[h * rows : (h + 1) * rows, :]
        step(q, kown, kown2, True)
        for back, (ka, kb) in enumerate(((k1, k12), (k2, k22), (k3, k32)), 1):
            pl.when(chain >= back)(functools.partial(step, q, ka, kb, False))
        mixed = (acc_ref[...] / l_ref[...]).astype(BF)
        per = heads // 2
        av = (av0 if h < per else av1)[h % per]
        ho_ref[:, h * vh : (h + 1) * vh] = jnp.dot(mixed, av, preferred_element_type=F32).astype(BF)
    ho = ho_ref[...]
    k = op0.shape[0]
    width = out_ref.shape[1]
    cut = 512 if width % 512 == 0 else width
    for c in range(0, width, cut):
        out_ref[:, c : c + cut] = (
            jnp.dot(ho[:, :k], op0[:, c : c + cut], preferred_element_type=F32)
            + jnp.dot(ho[:, k:], op1[:, c : c + cut], preferred_element_type=F32)
        ).astype(BF)


def local(
    query_comp, latent_rows, rope_keys, latent_gain, query_up, absorb_key, absorb_value, out_proj,
    page_owner, page_slot,
):
    nzh, nzl, nch = lax.axis_size("zh"), lax.axis_size("zl"), lax.axis_size("chain")
    zh, zl, core = lax.axis_index("zh"), lax.axis_index("zl"), lax.axis_index("core")
    chain, dec = lax.axis_index("chain"), lax.axis_index("dec")
    pages, part, lat = latent_rows.shape[1:]
    rope = rope_keys.shape[3]
    heads_here, nope = absorb_key.shape[:2]
    vh = absorb_value.shape[2]
    qrows, ql = query_comp.shape[1:]
    width = out_proj.shape[1]
    tp_index = (zh * nzl + zl) * 2 + core
    tp_count = nzh * nzl * 2
    block_len = qrows * tp_count
    slots = 2 * pages

    key_where = (
        chain * block_len
        + jnp.arange(pages, dtype=jnp.int32)[:, None] * (part * tp_count)
        + tp_index * part
        + jnp.arange(part, dtype=jnp.int32)[None, :]
    ).reshape(-1)
    x = latent_rows[0].reshape(pages * part, lat).astype(F32)
    normed = (x * lax.rsqrt(jnp.mean(x * x, -1, keepdims=True) + 1e-06) * latent_gain).astype(BF)
    kcos, ksin = rope_tables(key_where, rope)
    kr = rope_keys[0].reshape(pages * part, rope).astype(F32)
    key_rot = (kr * kcos + swap_halves(kr) * ksin).astype(BF)
    keys = jnp.concatenate([normed, key_rot], -1)

    wq1 = swap_core(query_up)
    ak1 = swap_core(absorb_key)
    av1 = swap_core(absorb_value)
    op1 = swap_core(out_proj)

    kg = gather_classes(spread(keys, "zh"))
    qg = gather_classes(spread(query_comp[0], "zh"))
    own = jnp.concatenate([p.reshape(-1, lat + rope) for p in kg], 0)
    backs = [
        lax.ppermute(own, "chain", [(i, i + k) for i in range(nch - k)]) for k in range(1, nch)
    ]
    key_sets = []
    for a in [own] + backs:
        key_sets += [a, swap_core(a)]

    rows = qrows * nzh * nzl
    idx = jnp.arange(rows, dtype=jnp.int32)
    zq = (idx // qrows) % nzh * nzl + (zl + idx // (nzh * qrows)) % nzl
    query_where = chain * block_len + zq * (2 * qrows) + core * qrows + idx % qrows
    qcos, qsin = rope_tables(query_where, rope)
    heads = 2 * heads_here
    big = dict(vmem_limit_bytes=32 * 1024 * 1024)
    q = pl.pallas_call(
        functools.partial(query_kernel, nope=nope, rope=rope),
        out_shape=jax.ShapeDtypeStruct((heads * rows, lat + rope), BF),
        scratch_shapes=[pltpu.VMEM((rows, ql), BF)],
        compiler_params=pltpu.CompilerParams(**big),
        cost_estimate=pl.CostEstimate(
            flops=2 * rows * heads * (nope + rope) * ql + 2 * rows * heads * nope * lat,
            bytes_accessed=6000000, transcendentals=0,
        ),
        name="queries",
    )(*[p.reshape(-1, ql) for p in qg], query_up, wq1, absorb_key, ak1, qcos, qsin)

    vm = pl.BlockSpec(memory_space=pltpu.VMEM)
    partial = pl.pallas_call(
        functools.partial(
            attend_kernel, rows=rows, lat=lat, scale=(nope + rope) ** -0.5,
            lay=(nzh, nzl, part, qrows, pages),
        ),
        out_shape=jax.ShapeDtypeStruct((rows, width), BF),
        in_specs=[pl.BlockSpec(memory_space=pltpu.SMEM)] + [vm] * 13,
        out_specs=vm,
        scratch_shapes=[
            pltpu.VMEM((rows, 1), F32),
            pltpu.VMEM((rows, 1), F32),
            pltpu.VMEM((rows, lat), F32),
            pltpu.VMEM((rows, heads * vh), BF),
        ],
        compiler_params=pltpu.CompilerParams(**big),
        cost_estimate=pl.CostEstimate(
            flops=4 * rows * heads * nch * block_len * lat, bytes_accessed=9000000,
            transcendentals=rows * heads * nch * block_len,
        ),
        name="attend",
    )(
        jnp.stack([chain, zl, core]).astype(jnp.int32), q, *key_sets,
        absorb_value, av1, out_proj, op1,
    )

    sums = partial.reshape(nzl, nzh, qrows, width)
    half = nzh // 2
    up = shift_z(sums[1], 1)
    down = shift_z(sums[3], -1)
    up2 = shift_z(sums[2, :half], 2)
    down2 = shift_z(sums[2, half:], -2)
    near = (
        sums[0].astype(F32) + up.astype(F32) + down.astype(F32)
        + jnp.concatenate([up2, down2], 0).astype(F32)
    ).astype(BF)
    got = lax.all_to_all(near, "zh", 0, 0, tiled=True)
    layer_output = jnp.sum(got.astype(F32), 0).astype(BF)[None]

    code = (page_owner[0] * slots + page_slot[0]).astype(BF)
    tail = jnp.broadcast_to(code[:, None, None], (pages, part, 128 - rope))
    page = jnp.concatenate([keys.reshape(pages, part, lat + rope), tail], -1)
    page = spread(page, "dec")
    came = page[:, :, 0, lat + rope].reshape(-1).astype(jnp.int32)
    take = (came[None, :] == dec * slots + jnp.arange(slots, dtype=jnp.int32)[:, None]).astype(BF)
    placed = jnp.einsum(
        "sp,pjc->sjc", take, page.reshape(-1, part, page.shape[-1]), preferred_element_type=F32
    ).astype(BF)
    cache_latent = placed[..., :lat][None, None]
    cache_rope = placed[..., lat : lat + rope][None, None]
    return (layer_output, cache_latent, cache_rope)


def solution(mesh):
    shape = mesh.shape
    chips = shape["tp"] // 2
    nzl = 4
    fine = Mesh(
        np.asarray(mesh.devices).reshape(shape["chain"], chips // nzl, nzl, 2, shape["dec"]),
        ("chain", "zh", "zl", "core", "dec"),
    )
    row = ("chain",) + TP
    return jax.shard_map(
        local,
        mesh=fine,
        in_specs=(
            P("dec", row, None),
            P("dec", "chain", TP, None),
            P("dec", "chain", TP, None),
            P(),
            P(None, TP),
            P(TP, None, None),
            P(TP, None, None),
            P(TP, None),
            P("dec", "chain"),
            P("dec", "chain"),
        ),
        out_specs=(
            P("dec", row, None),
            P("dec", "chain", None, TP, None),
            P("dec", "chain", None, TP, None),
        ),
        check_vma=False,
    )
```

```python
import functools

import jax
import jax.numpy as jnp
import numpy as np
from jax import lax
from jax.experimental import pallas as pl
from jax.experimental.pallas import tpu as pltpu
from jax.sharding import Mesh, PartitionSpec as P

BF = jnp.bfloat16
F32 = jnp.float32
LOG2E = 1.4426950408889634
Z = ("zh", "zl")
TP = ("zh", "zl", "core")
NEG = -1e30


def rope_tables(where_at, full_width):
    half = full_width // 2
    frequency = 10000.0 ** (-(jnp.arange(half).astype(F32) * 2.0 / full_width))
    angles = where_at.astype(F32)[:, None] * frequency[None, :]
    cosine, sine = jnp.cos(angles), jnp.sin(angles)
    return (
        jnp.concatenate([cosine, cosine], -1),
        jnp.concatenate([-sine, sine], -1),
    )


def swap_halves(v):
    half = v.shape[-1] // 2
    return jnp.concatenate([v[..., half:], v[..., :half]], -1)


def shift_z(x, step):
    n = lax.axis_size("zh") * lax.axis_size("zl")
    return lax.ppermute(x, Z, [(i, (i + step) % n) for i in range(n)])


def swap_core(x):
    return lax.ppermute(x, "core", [(0, 1), (1, 0)])


def spread(x, axis):
    n = lax.axis_size(axis)
    return lax.all_to_all(jnp.broadcast_to(x[None], (n,) + x.shape), axis, 0, 0, tiled=True)


def frequencies(width):
    half = width // 2
    f = 10000.0 ** (-(np.arange(half) * 2.0 / width))
    return jnp.asarray(np.concatenate([f, f]).astype(np.float32))[None]


def key_kernel(base_ref, x_ref, gain_ref, freq_ref, out_ref, *, lat, part, page_len):
    x = x_ref[...].astype(F32)
    n = x.shape[0]
    latent, rot = x[:, :lat], x[:, lat:]
    norm = lax.rsqrt(jnp.mean(latent * latent, -1, keepdims=True) + 1e-06)
    out_ref[:, :lat] = (latent * norm * gain_ref[...]).astype(BF)
    row = lax.broadcasted_iota(jnp.int32, rot.shape, 0)
    lane = lax.broadcasted_iota(jnp.int32, rot.shape, 1)
    where_at = base_ref[0] + row // part * page_len + row % part
    angle = where_at.astype(F32) * freq_ref[...]
    sine = jnp.sin(angle)
    sine = jnp.where(lane < rot.shape[1] // 2, -sine, sine)
    out_ref[:, lat:] = (rot * jnp.cos(angle) + swap_halves(rot) * sine).astype(BF)


def query_kernel(where_ref, g, wq0, wq1, ak0, ak1, cos_ref, sin_ref, out_ref, x_ref, *, nope, rope, qrows, nzh, nzl):
    zl = where_ref[1]
    for d in range(nzl):
        for zh in range(nzh):
            z = zh * nzl + lax.rem(zl + d, nzl)
            at = (d * nzh + zh) * qrows
            x_ref[at : at + qrows, :] = g[pl.ds(pl.multiple_of(z * qrows, qrows), qrows), :]
    x = x_ref[...]
    rows = x.shape[0]
    lat = ak0.shape[-1]
    head = 0
    for wq, ak in ((wq0, ak0), (wq1, ak1)):
        q = jnp.dot(x, wq[...], preferred_element_type=F32).astype(BF)
        for h in range(ak.shape[0]):
            base = h * (nope + rope)
            r0 = head * rows
            out_ref[r0 : r0 + rows, :lat] = jnp.dot(
                q[:, base : base + nope], ak[h], preferred_element_type=F32
            ).astype(BF)
            rot = q[:, base + nope : base + nope + rope].astype(F32)
            out_ref[r0 : r0 + rows, lat:] = (
                rot * cos_ref[...] + swap_halves(rot) * sin_ref[...]
            ).astype(BF)
            head += 1


def attend_kernel(
    where_ref, q_ref, ka_ref, kb_ref, av0, av1, op0, op1, out_ref,
    s_ref, top_ref, l_ref, acc_ref, ho_ref, *, rows, lat, scale, lay,
):
    chain, zl, core = where_ref[0], where_ref[1], where_ref[2]
    nch, nzh, nzl, part, qrows, pages = lay
    s2 = scale * LOG2E
    vh = av0.shape[-1]
    heads = q_ref.shape[0] // rows
    n = ka_ref.shape[0] // nch
    nt = (((1,), (1,)), ((), ()))

    def key_pos(idx, kcore):
        z = idx // (pages * part)
        page = (idx // part) % pages
        return page * (nzh * nzl * 2 * part) + z * (2 * part) + kcore * part + idx % part

    def query_pos(idx):
        d = idx // (nzh * qrows)
        z = (idx // qrows) % nzh * nzl + (zl + d) % nzl
        return z * (2 * qrows) + core * qrows + idx % qrows

    def lanes(x, op):
        out = x[:, :128]
        for c in range(128, x.shape[1], 128):
            out = op(out, x[:, c : c + 128])
        return out

    def score(back):
        if back == 0:
            qp = query_pos(lax.broadcasted_iota(jnp.int32, (rows, 1), 0))
            kidx = lax.broadcasted_iota(jnp.int32, (1, n), 1)
            ok = (key_pos(kidx, core) <= qp, key_pos(kidx, 1 - core) <= qp)
        for h in range(heads):
            q = q_ref[h * rows : (h + 1) * rows, :]
            for i, k_ref in enumerate((ka_ref, kb_ref)):
                s = lax.dot_general(q, k_ref[back * n : (back + 1) * n, :], nt, preferred_element_type=F32)
                if back == 0:
                    s = jnp.where(ok[i], s, NEG)
                at = (2 * back + i) * n
                s_ref[h, :, at : at + n] = s
                top = lanes(s, jnp.maximum)
                if back or i:
                    top = jnp.maximum(top, top_ref[h])
                top_ref[h] = top

    def mix(back):
        for h in range(heads):
            m = top_ref[h][:, :1]
            pv = None
            for i, k_ref in enumerate((ka_ref, kb_ref)):
                at = (2 * back + i) * n
                p = jnp.exp2(s_ref[h, :, at : at + n] * s2 - m)
                total = lanes(p, jnp.add)
                if back or i:
                    total += l_ref[h]
                l_ref[h] = total
                part_pv = jnp.dot(
                    p.astype(BF), k_ref[back * n : (back + 1) * n, :lat], preferred_element_type=F32
                )
                pv = part_pv if pv is None else pv + part_pv
            acc_ref[h] = acc_ref[h] + pv if back else pv

    score(0)
    for back in range(1, nch):
        pl.when(chain >= back)(functools.partial(score, back))
    for h in range(heads):
        m = jnp.max(top_ref[h], -1, keepdims=True) * s2
        top_ref[h] = jnp.broadcast_to(m, top_ref.shape[1:])
    mix(0)
    for back in range(1, nch):
        pl.when(chain >= back)(functools.partial(mix, back))
    per = heads // 2
    for h in range(heads):
        total = jnp.sum(l_ref[h], -1, keepdims=True)
        mixed = (acc_ref[h] / total).astype(BF)
        av = (av0 if h < per else av1)[h % per]
        ho_ref[:, h * vh : (h + 1) * vh] = jnp.dot(mixed, av, preferred_element_type=F32).astype(BF)
    ho = ho_ref[...]
    k = op0.shape[0]
    width = out_ref.shape[1]
    cut = 512 if width % 512 == 0 else width
    for c in range(0, width, cut):
        out_ref[:, c : c + cut] = (
            jnp.dot(ho[:, :k], op0[:, c : c + cut], preferred_element_type=F32)
            + jnp.dot(ho[:, k:], op1[:, c : c + cut], preferred_element_type=F32)
        ).astype(BF)


def local(
    query_comp, latent_rows, rope_keys, latent_gain, query_up, absorb_key, absorb_value, out_proj,
    page_owner, page_slot,
):
    nzh, nzl, nch = lax.axis_size("zh"), lax.axis_size("zl"), lax.axis_size("chain")
    zh, zl, core = lax.axis_index("zh"), lax.axis_index("zl"), lax.axis_index("core")
    chain, dec = lax.axis_index("chain"), lax.axis_index("dec")
    pages, part, lat = latent_rows.shape[1:]
    rope = rope_keys.shape[3]
    heads_here, nope = absorb_key.shape[:2]
    vh = absorb_value.shape[2]
    qrows, ql = query_comp.shape[1:]
    width = out_proj.shape[1]
    tp_index = (zh * nzl + zl) * 2 + core
    tp_count = nzh * nzl * 2
    block_len = qrows * tp_count
    slots = 2 * pages
    smem = pl.BlockSpec(memory_space=pltpu.SMEM)
    vm = pl.BlockSpec(memory_space=pltpu.VMEM)
    big = pltpu.CompilerParams(vmem_limit_bytes=40 * 1024 * 1024)

    raw = jnp.concatenate(
        [latent_rows[0].reshape(pages * part, lat), rope_keys[0].reshape(pages * part, rope)], -1
    )
    keys = pl.pallas_call(
        functools.partial(key_kernel, lat=lat, part=part, page_len=part * tp_count),
        out_shape=jax.ShapeDtypeStruct(raw.shape, BF),
        in_specs=[smem, vm, vm, vm],
        out_specs=vm,
        compiler_params=big,
        name="keys",
    )((chain * block_len + tp_index * part).astype(jnp.int32)[None], raw, latent_gain[None], frequencies(rope))

    own = lax.all_gather(keys, Z, axis=0, tiled=True)
    qg = lax.all_gather(query_comp[0], Z, axis=0, tiled=True)
    backs = [
        lax.ppermute(own, "chain", [(i, i + k) for i in range(nch - k)]) for k in range(1, nch)
    ]
    mine = jnp.concatenate([own] + backs, 0)
    other = swap_core(mine)

    wq1 = swap_core(query_up)
    ak1 = swap_core(absorb_key)
    av1 = swap_core(absorb_value)
    op1 = swap_core(out_proj)

    rows = qrows * nzh * nzl
    idx = jnp.arange(rows, dtype=jnp.int32)
    zq = (idx // qrows) % nzh * nzl + (zl + idx // (nzh * qrows)) % nzl
    query_where = chain * block_len + zq * (2 * qrows) + core * qrows + idx % qrows
    qcos, qsin = rope_tables(query_where, rope)
    heads = 2 * heads_here
    where = jnp.stack([chain, zl, core]).astype(jnp.int32)
    q = pl.pallas_call(
        functools.partial(query_kernel, nope=nope, rope=rope, qrows=qrows, nzh=nzh, nzl=nzl),
        out_shape=jax.ShapeDtypeStruct((heads * rows, lat + rope), BF),
        in_specs=[smem] + [vm] * 7,
        out_specs=vm,
        scratch_shapes=[pltpu.VMEM((rows, ql), BF)],
        compiler_params=big,
        cost_estimate=pl.CostEstimate(
            flops=2 * rows * heads * (nope + rope) * ql + 2 * rows * heads * nope * lat,
            bytes_accessed=6000000, transcendentals=0,
        ),
        name="queries",
    )(where, qg, query_up, wq1, absorb_key, ak1, qcos, qsin)

    partial = pl.pallas_call(
        functools.partial(
            attend_kernel, rows=rows, lat=lat, scale=(nope + rope) ** -0.5,
            lay=(nch, nzh, nzl, part, qrows, pages),
        ),
        out_shape=jax.ShapeDtypeStruct((rows, width), BF),
        in_specs=[smem] + [vm] * 7,
        out_specs=vm,
        scratch_shapes=[
            pltpu.VMEM((heads, rows, nch * block_len), F32),
            pltpu.VMEM((heads, rows, 128), F32),
            pltpu.VMEM((heads, rows, 128), F32),
            pltpu.VMEM((heads, rows, lat), F32),
            pltpu.VMEM((rows, heads * vh), BF),
        ],
        compiler_params=big,
        cost_estimate=pl.CostEstimate(
            flops=4 * rows * heads * nch * block_len * lat, bytes_accessed=9000000,
            transcendentals=rows * heads * nch * block_len,
        ),
        name="attend",
    )(where, q, mine, other, absorb_value, av1, out_proj, op1)

    sums = partial.reshape(nzl, nzh, qrows, width)
    half = nzh // 2
    up2 = shift_z(sums[2, :half], 2)
    down2 = shift_z(sums[2, half:], -2)
    up = shift_z(sums[1], 1)
    down = shift_z(sums[3], -1)
    near = (
        sums[0].astype(F32) + up.astype(F32) + down.astype(F32)
        + jnp.concatenate([up2, down2], 0).astype(F32)
    ).astype(BF)
    cut = width // 2

    def chunk(steps):
        return lax.dynamic_index_in_dim(near, lax.rem(zh + steps, nzh), 0, keepdims=False)

    far = chunk(2)
    around = shift_z(far[:, cut:], -nzl)
    direct = shift_z(far[:, :cut], 2 * nzl)
    ahead = shift_z(chunk(1), nzl)
    behind = chunk(3).astype(F32)
    behind = jnp.concatenate([behind[:, :cut], behind[:, cut:] + around.astype(F32)], -1).astype(BF)
    behind = shift_z(behind, -nzl)
    total = chunk(0).astype(F32) + ahead.astype(F32) + behind.astype(F32)
    total = jnp.concatenate([total[:, :cut] + direct.astype(F32), total[:, cut:]], -1)
    layer_output = total.astype(BF)[None]

    code = (page_owner[0] * slots + page_slot[0]).astype(BF)
    tail = jnp.broadcast_to(code[:, None, None], (pages, part, 128 - rope))
    page = jnp.concatenate([keys.reshape(pages, part, lat + rope), tail], -1)
    page = spread(page, "dec")
    came = page[:, :, 0, lat + rope].reshape(-1).astype(jnp.int32)
    take = (came[None, :] == dec * slots + jnp.arange(slots, dtype=jnp.int32)[:, None]).astype(BF)
    placed = jnp.einsum(
        "sp,pjc->sjc", take, page.reshape(-1, part, page.shape[-1]), preferred_element_type=F32
    ).astype(BF)
    cache_latent = placed[..., :lat][None, None]
    cache_rope = placed[..., lat : lat + rope][None, None]
    return (layer_output, cache_latent, cache_rope)


def solution(mesh):
    shape = mesh.shape
    chips = shape["tp"] // 2
    nzl = 4
    fine = Mesh(
        np.asarray(mesh.devices).reshape(shape["chain"], chips // nzl, nzl, 2, shape["dec"]),
        ("chain", "zh", "zl", "core", "dec"),
    )
    row = ("chain",) + TP
    return jax.shard_map(
        local,
        mesh=fine,
        in_specs=(
            P("dec", row, None),
            P("dec", "chain", TP, None),
            P("dec", "chain", TP, None),
            P(),
            P(None, TP),
            P(TP, None, None),
            P(TP, None, None),
            P(TP, None),
            P("dec", "chain"),
            P("dec", "chain"),
        ),
        out_specs=(
            P("dec", row, None),
            P("dec", "chain", None, TP, None),
            P("dec", "chain", None, TP, None),
        ),
        check_vma=False,
    )
```

```python
import functools

import jax
import jax.numpy as jnp
import numpy as np
from jax import lax
from jax.experimental import pallas as pl
from jax.experimental.pallas import tpu as pltpu
from jax.sharding import Mesh, PartitionSpec as P

BF = jnp.bfloat16
F32 = jnp.float32
LOG2E = 1.4426950408889634
Z = ("zh", "zl")
TP = ("zh", "zl", "core")
NEG = -1e30


def rope_tables(where_at, full_width):
    half = full_width // 2
    frequency = 10000.0 ** (-(jnp.arange(half).astype(F32) * 2.0 / full_width))
    angles = where_at.astype(F32)[:, None] * frequency[None, :]
    cosine, sine = jnp.cos(angles), jnp.sin(angles)
    return (
        jnp.concatenate([cosine, cosine], -1),
        jnp.concatenate([-sine, sine], -1),
    )


def swap_halves(v):
    half = v.shape[-1] // 2
    return jnp.concatenate([v[..., half:], v[..., :half]], -1)


def shift_z(x, step):
    n = lax.axis_size("zh") * lax.axis_size("zl")
    return lax.ppermute(x, Z, [(i, (i + step) % n) for i in range(n)])


def swap_core(x):
    return lax.ppermute(x, "core", [(0, 1), (1, 0)])


def spread(x, axis):
    n = lax.axis_size(axis)
    return lax.all_to_all(jnp.broadcast_to(x[None], (n,) + x.shape), axis, 0, 0, tiled=True)


def frequencies(width):
    half = width // 2
    f = 10000.0 ** (-(np.arange(half) * 2.0 / width))
    return jnp.asarray(np.concatenate([f, f]).astype(np.float32))[None]


def key_kernel(base_ref, owner_ref, slot_ref, q_ref, x_ref, gain_ref, freq_ref, all_ref, out_ref, *, lat, part, page_len, slots):
    x = x_ref[...].astype(F32)
    n = x.shape[0]
    latent, rot = x[:, :lat], x[:, lat:]
    norm = lax.rsqrt(jnp.mean(latent * latent, -1, keepdims=True) + 1e-06)
    out_ref[:, :lat] = (latent * norm * gain_ref[...]).astype(BF)
    row = lax.broadcasted_iota(jnp.int32, rot.shape, 0)
    lane = lax.broadcasted_iota(jnp.int32, rot.shape, 1)
    where_at = base_ref[0] + row // part * page_len + row % part
    angle = where_at.astype(F32) * freq_ref[...]
    sine = jnp.sin(angle)
    sine = jnp.where(lane < rot.shape[1] // 2, -sine, sine)
    code = jnp.zeros(rot.shape, F32)
    for p in range(n // part):
        here = (owner_ref[0, p] * slots + slot_ref[0, p]).astype(F32)
        code = jnp.where(row // part == p, here, code)
    turned = rot * jnp.cos(angle) + swap_halves(rot) * sine
    out_ref[:, lat:] = jnp.concatenate([turned, code], -1).astype(BF)
    ql = q_ref.shape[1]
    all_ref[:, :ql] = q_ref[...]
    all_ref[:, ql:] = out_ref[...]


def query_kernel(g, wq0, wq1, ak0, ak1, cos_ref, sin_ref, out_ref, *, nope, rope):
    x = g[:, : wq0.shape[0]]
    rows = x.shape[0]
    lat = ak0.shape[-1]
    head = 0
    for wq, ak in ((wq0, ak0), (wq1, ak1)):
        q = jnp.dot(x, wq[...], preferred_element_type=F32).astype(BF)
        for h in range(ak.shape[0]):
            base = h * (nope + rope)
            r0 = head * rows
            out_ref[r0 : r0 + rows, :lat] = jnp.dot(
                q[:, base : base + nope], ak[h], preferred_element_type=F32
            ).astype(BF)
            rot = q[:, base + nope : base + nope + rope].astype(F32)
            turned = rot * cos_ref[...] + swap_halves(rot) * sin_ref[...]
            out_ref[r0 : r0 + rows, lat:] = jnp.concatenate(
                [turned, jnp.zeros_like(turned)], -1
            ).astype(BF)
            head += 1


def attend_kernel(
    where_ref, q_ref, ka_ref, kb_ref, av0, av1, op0, op1, out_ref,
    s_ref, top_ref, l_ref, acc_ref, ho_ref, *, rows, lat, scale, lay,
):
    chain, core = where_ref[0], where_ref[1]
    nch, nzh, nzl, part, qrows, pages = lay
    s2 = scale * LOG2E
    vh = av0.shape[-1]
    heads = q_ref.shape[0] // rows
    n = ka_ref.shape[0] // nch
    nt = (((1,), (1,)), ((), ()))

    def key_pos(idx, kcore):
        z = idx // (pages * part)
        page = (idx // part) % pages
        return page * (nzh * nzl * 2 * part) + z * (2 * part) + kcore * part + idx % part

    def query_pos(idx):
        return idx // qrows * (2 * qrows) + core * qrows + idx % qrows

    def lanes(x, op):
        out = x[:, :128]
        for c in range(128, x.shape[1], 128):
            out = op(out, x[:, c : c + 128])
        return out

    def score(back):
        if back == 0:
            qp = query_pos(lax.broadcasted_iota(jnp.int32, (rows, 1), 0))
            kidx = lax.broadcasted_iota(jnp.int32, (1, n), 1)
            ok = (key_pos(kidx, core) <= qp, key_pos(kidx, 1 - core) <= qp)
        for h in range(heads):
            q = q_ref[h * rows : (h + 1) * rows, :]
            for i, k_ref in enumerate((ka_ref, kb_ref)):
                s = lax.dot_general(q, k_ref[back * n : (back + 1) * n, :], nt, preferred_element_type=F32)
                if back == 0:
                    s = jnp.where(ok[i], s, NEG)
                at = (2 * back + i) * n
                s_ref[h, :, at : at + n] = s
                top = lanes(s, jnp.maximum)
                if back or i:
                    top = jnp.maximum(top, top_ref[h])
                top_ref[h] = top

    def mix(back):
        for h in range(heads):
            m = top_ref[h][:, :1]
            pv = None
            for i, k_ref in enumerate((ka_ref, kb_ref)):
                at = (2 * back + i) * n
                p = jnp.exp2(s_ref[h, :, at : at + n] * s2 - m)
                total = lanes(p, jnp.add)
                if back or i:
                    total += l_ref[h]
                l_ref[h] = total
                part_pv = jnp.dot(
                    p.astype(BF), k_ref[back * n : (back + 1) * n, :lat], preferred_element_type=F32
                )
                pv = part_pv if pv is None else pv + part_pv
            acc_ref[h] = acc_ref[h] + pv if back else pv

    score(0)
    for back in range(1, nch):
        pl.when(chain >= back)(functools.partial(score, back))
    for h in range(heads):
        m = jnp.max(top_ref[h], -1, keepdims=True) * s2
        top_ref[h] = jnp.broadcast_to(m, top_ref.shape[1:])
    mix(0)
    for back in range(1, nch):
        pl.when(chain >= back)(functools.partial(mix, back))
    per = heads // 2
    for h in range(heads):
        total = jnp.sum(l_ref[h], -1, keepdims=True)
        mixed = (acc_ref[h] / total).astype(BF)
        av = (av0 if h < per else av1)[h % per]
        ho_ref[:, h * vh : (h + 1) * vh] = jnp.dot(mixed, av, preferred_element_type=F32).astype(BF)
    ho = ho_ref[...]
    k = op0.shape[0]
    width = out_ref.shape[1]
    cut = 512 if width % 512 == 0 else width
    for c in range(0, width, cut):
        out_ref[:, c : c + cut] = (
            jnp.dot(ho[:, :k], op0[:, c : c + cut], preferred_element_type=F32)
            + jnp.dot(ho[:, k:], op1[:, c : c + cut], preferred_element_type=F32)
        ).astype(BF)


def local(
    query_comp, latent_rows, rope_keys, latent_gain, query_up, absorb_key, absorb_value, out_proj,
    page_owner, page_slot,
):
    nzh, nzl, nch = lax.axis_size("zh"), lax.axis_size("zl"), lax.axis_size("chain")
    zh, zl, core = lax.axis_index("zh"), lax.axis_index("zl"), lax.axis_index("core")
    chain, dec = lax.axis_index("chain"), lax.axis_index("dec")
    pages, part, lat = latent_rows.shape[1:]
    rope = rope_keys.shape[3]
    heads_here, nope = absorb_key.shape[:2]
    vh = absorb_value.shape[2]
    qrows, ql = query_comp.shape[1:]
    width = out_proj.shape[1]
    tp_index = (zh * nzl + zl) * 2 + core
    tp_count = nzh * nzl * 2
    block_len = qrows * tp_count
    slots = 2 * pages
    smem = pl.BlockSpec(memory_space=pltpu.SMEM)
    vm = pl.BlockSpec(memory_space=pltpu.VMEM)

    def room(mib):
        return pltpu.CompilerParams(vmem_limit_bytes=mib * 1024 * 1024)

    raw = jnp.concatenate(
        [latent_rows[0].reshape(pages * part, lat), rope_keys[0].reshape(pages * part, rope)], -1
    )
    merged, keys = pl.pallas_call(
        functools.partial(key_kernel, lat=lat, part=part, page_len=part * tp_count, slots=slots),
        out_shape=(
            jax.ShapeDtypeStruct((qrows, ql + lat + 2 * rope), BF),
            jax.ShapeDtypeStruct((pages * part, lat + 2 * rope), BF),
        ),
        in_specs=[smem] * 3 + [vm] * 4,
        out_specs=(vm, vm),
        compiler_params=room(4),
        name="keys",
    )(
        (chain * block_len + tp_index * part).astype(jnp.int32)[None],
        page_owner, page_slot, query_comp[0], raw, latent_gain[None], frequencies(rope),
    )

    whole = lax.all_gather(merged, Z, axis=0, tiled=True)
    own = whole[:, ql:]
    backs = [
        lax.ppermute(own, "chain", [(i, i + k) for i in range(nch - k)]) for k in range(1, nch)
    ]
    mine = jnp.concatenate([own] + backs, 0)
    other = swap_core(mine)

    wq1 = swap_core(query_up)
    ak1 = swap_core(absorb_key)
    av1 = swap_core(absorb_value)
    op1 = swap_core(out_proj)

    rows = qrows * nzh * nzl
    idx = jnp.arange(rows, dtype=jnp.int32)
    query_where = chain * block_len + idx // qrows * (2 * qrows) + core * qrows + idx % qrows
    qcos, qsin = rope_tables(query_where, rope)
    heads = 2 * heads_here
    where = jnp.stack([chain, core]).astype(jnp.int32)
    q = pl.pallas_call(
        functools.partial(query_kernel, nope=nope, rope=rope),
        out_shape=jax.ShapeDtypeStruct((heads * rows, lat + 2 * rope), BF),
        in_specs=[vm] * 7,
        out_specs=vm,
        compiler_params=room(12),
        cost_estimate=pl.CostEstimate(
            flops=2 * rows * heads * (nope + rope) * ql + 2 * rows * heads * nope * lat,
            bytes_accessed=6000000, transcendentals=0,
        ),
        name="queries",
    )(whole, query_up, wq1, absorb_key, ak1, qcos, qsin)

    partial = pl.pallas_call(
        functools.partial(
            attend_kernel, rows=rows, lat=lat, scale=(nope + rope) ** -0.5,
            lay=(nch, nzh, nzl, part, qrows, pages),
        ),
        out_shape=jax.ShapeDtypeStruct((rows, width), BF),
        in_specs=[smem] + [vm] * 7,
        out_specs=vm,
        scratch_shapes=[
            pltpu.VMEM((heads, rows, nch * block_len), F32),
            pltpu.VMEM((heads, rows, 128), F32),
            pltpu.VMEM((heads, rows, 128), F32),
            pltpu.VMEM((heads, rows, lat), F32),
            pltpu.VMEM((rows, heads * vh), BF),
        ],
        compiler_params=room(24),
        cost_estimate=pl.CostEstimate(
            flops=4 * rows * heads * nch * block_len * lat, bytes_accessed=9000000,
            transcendentals=rows * heads * nch * block_len,
        ),
        name="attend",
    )(where, q, mine, other, absorb_value, av1, out_proj, op1)

    layer_output = lax.psum_scatter(partial, Z, scatter_dimension=0, tiled=True)[None]

    page = spread(keys.reshape(pages, part, -1), "dec")
    came = page[:, :, 0, lat + rope].reshape(-1).astype(jnp.int32)
    take = (came[None, :] == dec * slots + jnp.arange(slots, dtype=jnp.int32)[:, None]).astype(BF)
    placed = jnp.einsum(
        "sp,pjc->sjc", take, page.reshape(-1, part, page.shape[-1]), preferred_element_type=F32
    ).astype(BF)
    cache_latent = placed[..., :lat][None, None]
    cache_rope = placed[..., lat : lat + rope][None, None]
    return (layer_output, cache_latent, cache_rope)


def solution(mesh):
    shape = mesh.shape
    chips = shape["tp"] // 2
    nzl = 4
    fine = Mesh(
        np.asarray(mesh.devices).reshape(shape["chain"], chips // nzl, nzl, 2, shape["dec"]),
        ("chain", "zh", "zl", "core", "dec"),
    )
    row = ("chain",) + TP
    return jax.shard_map(
        local,
        mesh=fine,
        in_specs=(
            P("dec", row, None),
            P("dec", "chain", TP, None),
            P("dec", "chain", TP, None),
            P(),
            P(None, TP),
            P(TP, None, None),
            P(TP, None, None),
            P(TP, None),
            P("dec", "chain"),
            P("dec", "chain"),
        ),
        out_specs=(
            P("dec", row, None),
            P("dec", "chain", None, TP, None),
            P("dec", "chain", None, TP, None),
        ),
        check_vma=False,
    )
```

```python
import functools

import jax
import jax.numpy as jnp
import numpy as np
from jax import lax
from jax.experimental import pallas as pl
from jax.experimental.pallas import tpu as pltpu
from jax.sharding import Mesh, PartitionSpec as P

BF = jnp.bfloat16
F32 = jnp.float32
LOG2E = 1.4426950408889634
Z = ("zh", "zl")
TP = ("zh", "zl", "core")
NEG = -1e30


def rope_tables(where_at, full_width):
    half = full_width // 2
    frequency = 10000.0 ** (-(jnp.arange(half).astype(F32) * 2.0 / full_width))
    angles = where_at.astype(F32)[:, None] * frequency[None, :]
    cosine, sine = jnp.cos(angles), jnp.sin(angles)
    return (
        jnp.concatenate([cosine, cosine], -1),
        jnp.concatenate([-sine, sine], -1),
    )


def swap_halves(v):
    half = v.shape[-1] // 2
    return jnp.concatenate([v[..., half:], v[..., :half]], -1)


def shift_z(x, step):
    n = lax.axis_size("zh") * lax.axis_size("zl")
    return lax.ppermute(x, Z, [(i, (i + step) % n) for i in range(n)])


def swap_core(x):
    return lax.ppermute(x, "core", [(0, 1), (1, 0)])


def spread(x, axis):
    n = lax.axis_size(axis)
    return lax.all_to_all(jnp.broadcast_to(x[None], (n,) + x.shape), axis, 0, 0, tiled=True)


def frequencies(width):
    half = width // 2
    f = 10000.0 ** (-(np.arange(half) * 2.0 / width))
    return jnp.asarray(np.concatenate([f, f]).astype(np.float32))[None]


def key_kernel(base_ref, owner_ref, slot_ref, q_ref, x_ref, gain_ref, freq_ref, all_ref, out_ref, *, lat, part, page_len, slots):
    x = x_ref[...].astype(F32)
    n = x.shape[0]
    latent, rot = x[:, :lat], x[:, lat:]
    norm = lax.rsqrt(jnp.mean(latent * latent, -1, keepdims=True) + 1e-06)
    out_ref[:, :lat] = (latent * norm * gain_ref[...]).astype(BF)
    row = lax.broadcasted_iota(jnp.int32, rot.shape, 0)
    lane = lax.broadcasted_iota(jnp.int32, rot.shape, 1)
    where_at = base_ref[0] + row // part * page_len + row % part
    angle = where_at.astype(F32) * freq_ref[...]
    sine = jnp.sin(angle)
    sine = jnp.where(lane < rot.shape[1] // 2, -sine, sine)
    code = jnp.zeros(rot.shape, F32)
    for p in range(n // part):
        here = (owner_ref[0, p] * slots + slot_ref[0, p]).astype(F32)
        code = jnp.where(row // part == p, here, code)
    turned = rot * jnp.cos(angle) + swap_halves(rot) * sine
    out_ref[:, lat:] = jnp.concatenate([turned, code], -1).astype(BF)
    ql = q_ref.shape[1]
    all_ref[:, :ql] = q_ref[...]
    all_ref[:, ql:] = out_ref[...]


def own_kernel(g0, g1, g2, g3, g4, own_ref, *, ql):
    at = 0
    for g in (g0, g1, g2, g3, g4):
        n = g.shape[0]
        own_ref[at : at + n, :] = g[:, ql:]
        at += n


def query_kernel(g0, g1, g2, g3, g4, wq0, wq1, ak0, ak1, cos_ref, sin_ref, out_ref, x_ref, *, nope, rope):
    at = 0
    for g in (g0, g1, g2, g3, g4):
        n = g.shape[0]
        x_ref[at : at + n, :] = g[:, : wq0.shape[0]]
        at += n
    x = x_ref[...]
    rows = x.shape[0]
    lat = ak0.shape[-1]
    head = 0
    for wq, ak in ((wq0, ak0), (wq1, ak1)):
        q = jnp.dot(x, wq[...], preferred_element_type=F32).astype(BF)
        for h in range(ak.shape[0]):
            base = h * (nope + rope)
            r0 = head * rows
            out_ref[r0 : r0 + rows, :lat] = jnp.dot(
                q[:, base : base + nope], ak[h], preferred_element_type=F32
            ).astype(BF)
            rot = q[:, base + nope : base + nope + rope].astype(F32)
            turned = rot * cos_ref[...] + swap_halves(rot) * sin_ref[...]
            out_ref[r0 : r0 + rows, lat:] = jnp.concatenate(
                [turned, jnp.zeros_like(turned)], -1
            ).astype(BF)
            head += 1


def attend_kernel(
    where_ref, qpos_ref, kpos_ref, q_ref, ka_ref, kb_ref, av0, av1, op0, op1, out_ref,
    s_ref, top_ref, l_ref, acc_ref, ho_ref, *, rows, lat, scale, nch,
):
    chain = where_ref[0]
    s2 = scale * LOG2E
    vh = av0.shape[-1]
    heads = q_ref.shape[0] // rows
    n = ka_ref.shape[0] // nch
    nt = (((1,), (1,)), ((), ()))

    def lanes(x, op):
        out = x[:, :128]
        for c in range(128, x.shape[1], 128):
            out = op(out, x[:, c : c + 128])
        return out

    def score(back):
        if back == 0:
            ok = [kpos_ref[i : i + 1, :] <= qpos_ref[...] for i in range(2)]
        for h in range(heads):
            q = q_ref[h * rows : (h + 1) * rows, :]
            for i, k_ref in enumerate((ka_ref, kb_ref)):
                s = lax.dot_general(q, k_ref[back * n : (back + 1) * n, :], nt, preferred_element_type=F32)
                if back == 0:
                    s = jnp.where(ok[i], s, NEG)
                at = (2 * back + i) * n
                s_ref[h, :, at : at + n] = s
                top = lanes(s, jnp.maximum)
                if back or i:
                    top = jnp.maximum(top, top_ref[h])
                top_ref[h] = top

    def mix(back):
        for h in range(heads):
            m = top_ref[h][:, :1]
            pv = None
            for i, k_ref in enumerate((ka_ref, kb_ref)):
                at = (2 * back + i) * n
                p = jnp.exp2(s_ref[h, :, at : at + n] * s2 - m)
                total = lanes(p, jnp.add)
                if back or i:
                    total += l_ref[h]
                l_ref[h] = total
                part_pv = jnp.dot(
                    p.astype(BF), k_ref[back * n : (back + 1) * n, :lat], preferred_element_type=F32
                )
                pv = part_pv if pv is None else pv + part_pv
            acc_ref[h] = acc_ref[h] + pv if back else pv

    score(0)
    for back in range(1, nch):
        pl.when(chain >= back)(functools.partial(score, back))
    for h in range(heads):
        m = jnp.max(top_ref[h], -1, keepdims=True) * s2
        top_ref[h] = jnp.broadcast_to(m, top_ref.shape[1:])
    mix(0)
    for back in range(1, nch):
        pl.when(chain >= back)(functools.partial(mix, back))
    per = heads // 2
    for h in range(heads):
        total = jnp.sum(l_ref[h], -1, keepdims=True)
        mixed = (acc_ref[h] / total).astype(BF)
        av = (av0 if h < per else av1)[h % per]
        ho_ref[:, h * vh : (h + 1) * vh] = jnp.dot(mixed, av, preferred_element_type=F32).astype(BF)
    ho = ho_ref[...]
    k = op0.shape[0]
    width = out_ref.shape[1]
    cut = 512 if width % 512 == 0 else width
    for c in range(0, width, cut):
        out_ref[:, c : c + cut] = (
            jnp.dot(ho[:, :k], op0[:, c : c + cut], preferred_element_type=F32)
            + jnp.dot(ho[:, k:], op1[:, c : c + cut], preferred_element_type=F32)
        ).astype(BF)


def local(
    query_comp, latent_rows, rope_keys, latent_gain, query_up, absorb_key, absorb_value, out_proj,
    page_owner, page_slot,
):
    nzh, nzl, nch = lax.axis_size("zh"), lax.axis_size("zl"), lax.axis_size("chain")
    zh, zl, core = lax.axis_index("zh"), lax.axis_index("zl"), lax.axis_index("core")
    chain, dec = lax.axis_index("chain"), lax.axis_index("dec")
    pages, part, lat = latent_rows.shape[1:]
    rope = rope_keys.shape[3]
    heads_here, nope = absorb_key.shape[:2]
    vh = absorb_value.shape[2]
    qrows, ql = query_comp.shape[1:]
    width = out_proj.shape[1]
    tp_index = (zh * nzl + zl) * 2 + core
    tp_count = nzh * nzl * 2
    block_len = qrows * tp_count
    slots = 2 * pages
    smem = pl.BlockSpec(memory_space=pltpu.SMEM)
    vm = pl.BlockSpec(memory_space=pltpu.VMEM)

    def room(mib):
        return pltpu.CompilerParams(vmem_limit_bytes=mib * 1024 * 1024)

    raw = jnp.concatenate(
        [latent_rows[0].reshape(pages * part, lat), rope_keys[0].reshape(pages * part, rope)], -1
    )
    merged, keys = pl.pallas_call(
        functools.partial(key_kernel, lat=lat, part=part, page_len=part * tp_count, slots=slots),
        out_shape=(
            jax.ShapeDtypeStruct((qrows, ql + lat + 2 * rope), BF),
            jax.ShapeDtypeStruct((pages * part, lat + 2 * rope), BF),
        ),
        in_specs=[smem] * 3 + [vm] * 4,
        out_specs=(vm, vm),
        compiler_params=room(4),
        name="keys",
    )(
        (chain * block_len + tp_index * part).astype(jnp.int32)[None],
        page_owner, page_slot, query_comp[0], raw, latent_gain[None], frequencies(rope),
    )

    group = jnp.concatenate(
        [shift_z(merged, nzl), merged, shift_z(merged, -nzl), shift_z(merged, -2 * nzl)], 0
    )
    parts = [
        group,
        shift_z(group, -1),
        shift_z(group, 1),
        shift_z(group[qrows : 3 * qrows], -2),
        shift_z(group[: 2 * qrows], 2),
    ]
    rows = qrows * nzh * nzl
    kw = lat + 2 * rope
    own = pl.pallas_call(
        functools.partial(own_kernel, ql=ql),
        out_shape=jax.ShapeDtypeStruct((rows, kw), BF),
        in_specs=[vm] * 5,
        out_specs=vm,
        compiler_params=room(4),
        name="own",
    )(*parts)

    half = rows // 2
    before = lax.ppermute(own, "chain", [(0, 1), (1, 2), (2, 3)])
    across = lax.ppermute(own, "chain", [(0, 3), (1, 0)])
    second = lax.ppermute(before[:half], "chain", [(1, 2), (2, 3)])
    second2 = lax.ppermute(across[half:], "chain", [(3, 2), (0, 3)])
    mine = jnp.concatenate([own, before, second, second2, across], 0)
    other = swap_core(mine)

    wq1 = swap_core(query_up)
    ak1 = swap_core(absorb_key)
    av1 = swap_core(absorb_value)
    op1 = swap_core(out_proj)

    steps = [4 * e + d for d in (0, 1, -1) for e in (-1, 0, 1, 2)] + [2, 6, -6, -2]
    z = (zh * nzl + zl + jnp.asarray(np.array(steps, np.int32))) % (nzh * nzl)
    lane = jnp.arange(qrows, dtype=jnp.int32)
    qpos = (z[:, None] * (2 * qrows) + core * qrows + lane[None]).reshape(rows)
    lane = lane // part * (part * tp_count) + lane % part
    kpos = (z[:, None] * (2 * part) + lane[None]).reshape(1, rows)
    kpos = kpos + jnp.stack([core, 1 - core])[:, None] * part
    query_where = chain * block_len + qpos
    qcos, qsin = rope_tables(query_where, rope)
    heads = 2 * heads_here
    where = chain.astype(jnp.int32)[None]
    q = pl.pallas_call(
        functools.partial(query_kernel, nope=nope, rope=rope),
        out_shape=jax.ShapeDtypeStruct((heads * rows, kw), BF),
        in_specs=[vm] * 11,
        out_specs=vm,
        scratch_shapes=[pltpu.VMEM((rows, ql), BF)],
        compiler_params=room(12),
        cost_estimate=pl.CostEstimate(
            flops=2 * rows * heads * (nope + rope) * ql + 2 * rows * heads * nope * lat,
            bytes_accessed=6000000, transcendentals=0,
        ),
        name="queries",
    )(*parts, query_up, wq1, absorb_key, ak1, qcos, qsin)

    partial = pl.pallas_call(
        functools.partial(
            attend_kernel, rows=rows, lat=lat, scale=(nope + rope) ** -0.5,
            nch=nch,
        ),
        out_shape=jax.ShapeDtypeStruct((rows, width), BF),
        in_specs=[smem] + [vm] * 9,
        out_specs=vm,
        scratch_shapes=[
            pltpu.VMEM((heads, rows, nch * block_len), F32),
            pltpu.VMEM((heads, rows, 128), F32),
            pltpu.VMEM((heads, rows, 128), F32),
            pltpu.VMEM((heads, rows, lat), F32),
            pltpu.VMEM((rows, heads * vh), BF),
        ],
        compiler_params=room(24),
        cost_estimate=pl.CostEstimate(
            flops=4 * rows * heads * nch * block_len * lat, bytes_accessed=9000000,
            transcendentals=rows * heads * nch * block_len,
        ),
        name="attend",
    )(where, qpos[:, None], kpos, q, mine, other, absorb_value, av1, out_proj, op1)

    n = nzh * qrows
    up = shift_z(partial[n : 2 * n], 1)
    down = shift_z(partial[2 * n : 3 * n], -1)
    up2 = shift_z(partial[3 * n : 3 * n + n // 2], 2)
    down2 = shift_z(partial[3 * n + n // 2 :], -2)

    def near(e):
        at = slice((e + 1) * qrows, (e + 2) * qrows)
        return partial[at].astype(F32) + up[at].astype(F32) + down[at].astype(F32)

    cut = width // 2
    far = near(2).astype(BF)
    around = shift_z(far[:, cut:], -nzl)
    direct = shift_z(far[:, :cut], 2 * nzl)
    ahead = shift_z((near(1) + up2[qrows:].astype(F32)).astype(BF), nzl)
    behind = near(-1) + down2[:qrows].astype(F32)
    behind = jnp.concatenate([behind[:, :cut], behind[:, cut:] + around.astype(F32)], -1)
    behind = shift_z(behind.astype(BF), -nzl)
    total = near(0) + up2[:qrows].astype(F32) + down2[qrows:].astype(F32)
    total = total + ahead.astype(F32) + behind.astype(F32)
    total = jnp.concatenate([total[:, :cut] + direct.astype(F32), total[:, cut:]], -1)
    layer_output = total.astype(BF)[None]

    page = spread(keys.reshape(pages, part, -1), "dec")
    came = page[:, :, 0, lat + rope].reshape(-1).astype(jnp.int32)
    take = (came[None, :] == dec * slots + jnp.arange(slots, dtype=jnp.int32)[:, None]).astype(BF)
    placed = jnp.einsum(
        "sp,pjc->sjc", take, page.reshape(-1, part, page.shape[-1]), preferred_element_type=F32
    ).astype(BF)
    cache_latent = placed[..., :lat][None, None]
    cache_rope = placed[..., lat : lat + rope][None, None]
    return (layer_output, cache_latent, cache_rope)


def solution(mesh):
    shape = mesh.shape
    chips = shape["tp"] // 2
    nzl = 4
    fine = Mesh(
        np.asarray(mesh.devices).reshape(shape["chain"], chips // nzl, nzl, 2, shape["dec"]),
        ("chain", "zh", "zl", "core", "dec"),
    )
    row = ("chain",) + TP
    return jax.shard_map(
        local,
        mesh=fine,
        in_specs=(
            P("dec", row, None),
            P("dec", "chain", TP, None),
            P("dec", "chain", TP, None),
            P(),
            P(None, TP),
            P(TP, None, None),
            P(TP, None, None),
            P(TP, None),
            P("dec", "chain"),
            P("dec", "chain"),
        ),
        out_specs=(
            P("dec", row, None),
            P("dec", "chain", None, TP, None),
            P("dec", "chain", None, TP, None),
        ),
        check_vma=False,
    )
```

```python
import functools

import jax
import jax.numpy as jnp
import numpy as np
from jax import lax
from jax.experimental import pallas as pl
from jax.experimental.pallas import tpu as pltpu
from jax.sharding import Mesh, PartitionSpec as P

BF = jnp.bfloat16
F32 = jnp.float32
LOG2E = 1.4426950408889634
Z = ("zh", "zl")
TP = ("zh", "zl", "core")
NEG = -1e30
STEPS = [4 * e + d for d in (0, 1, -1) for e in (-1, 0, 1, 2)] + [2, 6, -6, -2]


def swap_halves(v):
    half = v.shape[-1] // 2
    return jnp.concatenate([v[..., half:], v[..., :half]], -1)


def shift_z(x, step):
    n = lax.axis_size("zh") * lax.axis_size("zl")
    return lax.ppermute(x, Z, [(i, (i + step) % n) for i in range(n)])


def swap_core(x):
    return lax.ppermute(x, "core", [(0, 1), (1, 0)])


def spread(x, axis):
    n = lax.axis_size(axis)
    return lax.all_to_all(jnp.broadcast_to(x[None], (n,) + x.shape), axis, 0, 0, tiled=True)


def frequencies(width):
    half = width // 2
    f = 10000.0 ** (-(np.arange(half) * 2.0 / width))
    return jnp.asarray(np.concatenate([f, f]).astype(np.float32))[None]


def turn(v, where_at, freq):
    angle = where_at.astype(F32) * freq
    lane = lax.broadcasted_iota(jnp.int32, v.shape, 1)
    sine = jnp.sin(angle)
    sine = jnp.where(lane < v.shape[1] // 2, -sine, sine)
    return v * jnp.cos(angle) + swap_halves(v) * sine


def key_kernel(base_ref, owner_ref, slot_ref, x_ref, gain_ref, freq_ref, out_ref, *, lat, part, page_len, slots):
    x = x_ref[...].astype(F32)
    n = x.shape[0]
    latent, rot = x[:, :lat], x[:, lat:]
    norm = lax.rsqrt(jnp.mean(latent * latent, -1, keepdims=True) + 1e-06)
    out_ref[:, :lat] = (latent * norm * gain_ref[...]).astype(BF)
    row = lax.broadcasted_iota(jnp.int32, rot.shape, 0)
    where_at = base_ref[0] + row // part * page_len + row % part
    turned = turn(rot, where_at, freq_ref[...])
    code = jnp.zeros(rot.shape, F32)
    for p in range(n // part):
        here = (owner_ref[0, p] * slots + slot_ref[0, p]).astype(F32)
        code = jnp.where(row // part == p, here, code)
    out_ref[:, lat:] = jnp.concatenate([turned, code], -1).astype(BF)


def query_where(idx, z, core, qrows, chips):
    blk = idx // qrows
    off = jnp.zeros_like(idx)
    for i, step in enumerate(STEPS):
        off = jnp.where(blk == i, step % chips, off)
    return lax.rem(z + off, chips) * (2 * qrows) + core * qrows + idx % qrows


def pack_kernel(*refs):
    out_ref, at = refs[-1], 0
    for r in refs[:-1]:
        n = r.shape[0]
        out_ref[at : at + n, :] = r[...]
        at += n


def query_kernel(
    where_ref, g_ref, wq_ref, ak0, ak1, freq_ref, out_ref, x_ref, *, nope, rope, qrows, chips
):
    chain, z, core = where_ref[0], where_ref[1], where_ref[2]
    for i, step in enumerate(STEPS):
        at = lax.rem(z + step % chips, chips)
        x_ref[i * qrows : (i + 1) * qrows, :] = g_ref[pl.ds(pl.multiple_of(at * qrows, qrows), qrows), :]
    x = x_ref[...]
    rows = x.shape[0]
    lat = ak0.shape[-1]
    idx = lax.broadcasted_iota(jnp.int32, (rows, rope), 0)
    place = chain * (chips * 2 * qrows) + query_where(idx, z, core, qrows, chips)
    angle = place.astype(F32) * freq_ref[...]
    lane = lax.broadcasted_iota(jnp.int32, angle.shape, 1)
    sine = jnp.sin(angle)
    sine = jnp.where(lane < rope // 2, -sine, sine)
    cosine = jnp.cos(angle)
    head = 0
    for side, ak in ((core, ak0), (1 - core, ak1)):
        q = jnp.dot(x, wq_ref[side], preferred_element_type=F32).astype(BF)
        for h in range(ak.shape[0]):
            base = h * (nope + rope)
            r0 = head * rows
            out_ref[r0 : r0 + rows, :lat] = jnp.dot(
                q[:, base : base + nope], ak[h], preferred_element_type=F32
            ).astype(BF)
            rot = q[:, base + nope : base + nope + rope].astype(F32)
            turned = rot * cosine + swap_halves(rot) * sine
            out_ref[r0 : r0 + rows, lat:] = jnp.concatenate(
                [turned, jnp.zeros_like(turned)], -1
            ).astype(BF)
            head += 1


def attend_kernel(
    where_ref, q_ref, ka_ref, kb_ref, av0, av1, op_ref, out_ref,
    s_ref, top_ref, l_ref, acc_ref, ho_ref, *, rows, lat, scale, nch, chips, qrows, part,
):
    chain, z, core = where_ref[0], where_ref[1], where_ref[2]
    s2 = scale * LOG2E
    vh = av0.shape[-1]
    heads = q_ref.shape[0] // rows
    n = ka_ref.shape[0] // nch
    nt = (((1,), (1,)), ((), ()))

    def lanes(x, op):
        out = x[:, :128]
        for c in range(128, x.shape[1], 128):
            out = op(out, x[:, c : c + 128])
        return out

    def score(back):
        if back == 0:
            idx = lax.broadcasted_iota(jnp.int32, (rows, 1), 0)
            qpos = query_where(idx, z, core, qrows, chips)
            idx = lax.broadcasted_iota(jnp.int32, (1, n), 1)
            kpos = (idx % qrows) // part * (chips * 2 * part) + idx // qrows * (2 * part) + idx % part
            ok = [kpos + i * part <= qpos for i in (core, 1 - core)]
        for h in range(heads):
            q = q_ref[h * rows : (h + 1) * rows, :]
            for i, k_ref in enumerate((ka_ref, kb_ref)):
                s = lax.dot_general(q, k_ref[back * n : (back + 1) * n, :], nt, preferred_element_type=F32)
                if back == 0:
                    s = jnp.where(ok[i], s, NEG)
                at = (2 * back + i) * n
                s_ref[h, :, at : at + n] = s
                top = lanes(s, jnp.maximum)
                if back or i:
                    top = jnp.maximum(top, top_ref[h])
                top_ref[h] = top

    def mix(back):
        for h in range(heads):
            m = top_ref[h][:, :1]
            pv = None
            for i, k_ref in enumerate((ka_ref, kb_ref)):
                at = (2 * back + i) * n
                p = jnp.exp2(s_ref[h, :, at : at + n] * s2 - m)
                total = lanes(p, jnp.add)
                if back or i:
                    total += l_ref[h]
                l_ref[h] = total
                part_pv = jnp.dot(
                    p.astype(BF), k_ref[back * n : (back + 1) * n, :lat], preferred_element_type=F32
                )
                pv = part_pv if pv is None else pv + part_pv
            acc_ref[h] = acc_ref[h] + pv if back else pv

    score(0)
    for back in range(1, nch):
        pl.when(chain >= back)(functools.partial(score, back))
    for h in range(heads):
        m = jnp.max(top_ref[h], -1, keepdims=True) * s2
        top_ref[h] = jnp.broadcast_to(m, top_ref.shape[1:])
    mix(0)
    for back in range(1, nch):
        pl.when(chain >= back)(functools.partial(mix, back))
    per = heads // 2
    for h in range(heads):
        total = jnp.sum(l_ref[h], -1, keepdims=True)
        mixed = (acc_ref[h] / total).astype(BF)
        av = (av0 if h < per else av1)[h % per]
        ho_ref[:, h * vh : (h + 1) * vh] = jnp.dot(mixed, av, preferred_element_type=F32).astype(BF)
    ho = ho_ref[...]
    k = op_ref.shape[1]
    width = out_ref.shape[1]
    cut = 512 if width % 512 == 0 else width
    for c in range(0, width, cut):
        out_ref[:, c : c + cut] = (
            jnp.dot(ho[:, :k], op_ref[core, :, c : c + cut], preferred_element_type=F32)
            + jnp.dot(ho[:, k:], op_ref[1 - core, :, c : c + cut], preferred_element_type=F32)
        ).astype(BF)


def local(
    query_comp, latent_rows, rope_keys, latent_gain, query_up, absorb_key, absorb_value, out_proj,
    page_owner, page_slot,
):
    nzh, nzl, nch = lax.axis_size("zh"), lax.axis_size("zl"), lax.axis_size("chain")
    zh, zl, core = lax.axis_index("zh"), lax.axis_index("zl"), lax.axis_index("core")
    chain, dec = lax.axis_index("chain"), lax.axis_index("dec")
    pages, part, lat = latent_rows.shape[1:]
    rope = rope_keys.shape[3]
    heads_here, nope = absorb_key.shape[:2]
    vh = absorb_value.shape[2]
    qrows, ql = query_comp.shape[1:]
    width = out_proj.shape[1]
    tp_index = (zh * nzl + zl) * 2 + core
    tp_count = nzh * nzl * 2
    block_len = qrows * tp_count
    slots = 2 * pages
    smem = pl.BlockSpec(memory_space=pltpu.SMEM)
    vm = pl.BlockSpec(memory_space=pltpu.VMEM)

    def room(mib):
        return pltpu.CompilerParams(vmem_limit_bytes=mib * 1024 * 1024)

    raw = jnp.concatenate(
        [latent_rows[0].reshape(pages * part, lat), rope_keys[0].reshape(pages * part, rope)], -1
    )
    rows = qrows * nzh * nzl
    kw = lat + 2 * rope
    heads = 2 * heads_here
    z = zh * nzl + zl
    where = jnp.stack([chain, z, core]).astype(jnp.int32)
    keys = pl.pallas_call(
        functools.partial(key_kernel, lat=lat, part=part, page_len=part * tp_count, slots=slots),
        out_shape=jax.ShapeDtypeStruct((pages * part, kw), BF),
        in_specs=[smem] * 3 + [vm] * 3,
        out_specs=vm,
        compiler_params=room(4),
        name="keys",
    )(
        (chain * block_len + tp_index * part).astype(jnp.int32)[None],
        page_owner, page_slot, raw, latent_gain[None], frequencies(rope),
    )

    wq = lax.all_gather(query_up, "core", axis=0, tiled=False)
    op = lax.all_gather(out_proj, "core", axis=0, tiled=False)
    ak1 = swap_core(absorb_key)
    av1 = swap_core(absorb_value)

    own = lax.all_gather(keys, Z, axis=0, tiled=True)
    backs = [
        lax.ppermute(own, "chain", [(i, i + k) for i in range(nch - k)]) for k in range(1, nch)
    ]
    held = lax.optimization_barrier((query_comp[0], own))[0]
    qg = lax.all_gather(held, Z, axis=0, tiled=True)
    qg, *backs = lax.optimization_barrier((qg, *backs))
    mine = pl.pallas_call(
        pack_kernel,
        out_shape=jax.ShapeDtypeStruct((nch * rows, kw), BF),
        in_specs=[vm] * nch,
        out_specs=vm,
        compiler_params=room(4),
        name="pack",
    )(own, *backs)
    other = swap_core(mine)

    q = pl.pallas_call(
        functools.partial(query_kernel, nope=nope, rope=rope, qrows=qrows, chips=nzh * nzl),
        out_shape=jax.ShapeDtypeStruct((heads * rows, kw), BF),
        in_specs=[smem] + [vm] * 5,
        out_specs=vm,
        scratch_shapes=[pltpu.VMEM((rows, ql), BF)],
        compiler_params=room(12),
        cost_estimate=pl.CostEstimate(
            flops=2 * rows * heads * (nope + rope) * ql + 2 * rows * heads * nope * lat,
            bytes_accessed=6000000, transcendentals=0,
        ),
        name="queries",
    )(where, qg, wq, absorb_key, ak1, frequencies(rope))

    partial = pl.pallas_call(
        functools.partial(
            attend_kernel, rows=rows, lat=lat, scale=(nope + rope) ** -0.5,
            nch=nch, chips=nzh * nzl, qrows=qrows, part=part,
        ),
        out_shape=jax.ShapeDtypeStruct((rows, width), BF),
        in_specs=[smem] + [vm] * 6,
        out_specs=vm,
        scratch_shapes=[
            pltpu.VMEM((heads, rows, nch * block_len), F32),
            pltpu.VMEM((heads, rows, 128), F32),
            pltpu.VMEM((heads, rows, 128), F32),
            pltpu.VMEM((heads, rows, lat), F32),
            pltpu.VMEM((rows, heads * vh), BF),
        ],
        compiler_params=room(24),
        cost_estimate=pl.CostEstimate(
            flops=4 * rows * heads * nch * block_len * lat, bytes_accessed=9000000,
            transcendentals=rows * heads * nch * block_len,
        ),
        name="attend",
    )(where, q, mine, other, absorb_value, av1, op)

    n = nzh * qrows
    up2 = shift_z(partial[3 * n : 3 * n + n // 2], 2)
    down2 = shift_z(partial[3 * n + n // 2 :], -2)
    up = shift_z(partial[n : 2 * n], 1)
    down = shift_z(partial[2 * n : 3 * n], -1)

    def near(e):
        at = slice((e + 1) * qrows, (e + 2) * qrows)
        return partial[at].astype(F32) + up[at].astype(F32) + down[at].astype(F32)

    cut = width // 2
    far = near(2).astype(BF)
    around = shift_z(far[:, cut:], -nzl)
    direct = shift_z(far[:, :cut], 2 * nzl)
    ahead = shift_z((near(1) + up2[qrows:].astype(F32)).astype(BF), nzl)
    behind = near(-1) + down2[:qrows].astype(F32)
    behind = jnp.concatenate([behind[:, :cut], behind[:, cut:] + around.astype(F32)], -1)
    behind = shift_z(behind.astype(BF), -nzl)
    total = near(0) + up2[:qrows].astype(F32) + down2[qrows:].astype(F32)
    total = total + ahead.astype(F32) + behind.astype(F32)
    total = jnp.concatenate([total[:, :cut] + direct.astype(F32), total[:, cut:]], -1)
    layer_output = total.astype(BF)[None]

    keys = lax.optimization_barrier((keys, partial))[0]
    page = spread(keys.reshape(pages, part, -1), "dec")
    came = page[:, :, 0, lat + rope].reshape(-1).astype(jnp.int32)
    take = (came[None, :] == dec * slots + jnp.arange(slots, dtype=jnp.int32)[:, None]).astype(BF)
    placed = jnp.einsum(
        "sp,pjc->sjc", take, page.reshape(-1, part, page.shape[-1]), preferred_element_type=F32
    ).astype(BF)
    cache_latent = placed[..., :lat][None, None]
    cache_rope = placed[..., lat : lat + rope][None, None]
    return (layer_output, cache_latent, cache_rope)


def solution(mesh):
    shape = mesh.shape
    chips = shape["tp"] // 2
    nzl = 4
    fine = Mesh(
        np.asarray(mesh.devices).reshape(shape["chain"], chips // nzl, nzl, 2, shape["dec"]),
        ("chain", "zh", "zl", "core", "dec"),
    )
    row = ("chain",) + TP
    return jax.shard_map(
        local,
        mesh=fine,
        in_specs=(
            P("dec", row, None),
            P("dec", "chain", TP, None),
            P("dec", "chain", TP, None),
            P(),
            P(None, TP),
            P(TP, None, None),
            P(TP, None, None),
            P(TP, None),
            P("dec", "chain"),
            P("dec", "chain"),
        ),
        out_specs=(
            P("dec", row, None),
            P("dec", "chain", None, TP, None),
            P("dec", "chain", None, TP, None),
        ),
        check_vma=False,
    )
```

```python
import functools

import jax
import jax.numpy as jnp
import numpy as np
from jax import lax
from jax.experimental import pallas as pl
from jax.experimental.pallas import tpu as pltpu
from jax.sharding import Mesh, PartitionSpec as P

BF = jnp.bfloat16
F32 = jnp.float32
LOG2E = 1.4426950408889634
Z = ("zh", "zl")
TP = ("zh", "zl", "core")
NEG = -1e30
STEPS = [4 * e + d for d in (0, 1, -1) for e in (-1, 0, 1, 2)] + [2, 6, -6, -2]


def swap_halves(v):
    half = v.shape[-1] // 2
    return jnp.concatenate([v[..., half:], v[..., :half]], -1)


def shift_z(x, step):
    n = lax.axis_size("zh") * lax.axis_size("zl")
    return lax.ppermute(x, Z, [(i, (i + step) % n) for i in range(n)])


def swap_core(x):
    return lax.ppermute(x, "core", [(0, 1), (1, 0)])


def spread(x, axis):
    n = lax.axis_size(axis)
    return lax.all_to_all(jnp.broadcast_to(x[None], (n,) + x.shape), axis, 0, 0, tiled=True)


def frequencies(width):
    half = width // 2
    f = 10000.0 ** (-(np.arange(half) * 2.0 / width))
    return jnp.asarray(np.concatenate([f, f]).astype(np.float32))[None]


def turn(v, where_at, freq):
    angle = where_at.astype(F32) * freq
    lane = lax.broadcasted_iota(jnp.int32, v.shape, 1)
    sine = jnp.sin(angle)
    sine = jnp.where(lane < v.shape[1] // 2, -sine, sine)
    return v * jnp.cos(angle) + swap_halves(v) * sine


def key_kernel(base_ref, owner_ref, slot_ref, x_ref, gain_ref, freq_ref, out_ref, *, lat, part, page_len, slots):
    x = x_ref[...].astype(F32)
    n = x.shape[0]
    latent, rot = x[:, :lat], x[:, lat:]
    norm = lax.rsqrt(jnp.mean(latent * latent, -1, keepdims=True) + 1e-06)
    out_ref[:, :lat] = (latent * norm * gain_ref[...]).astype(BF)
    row = lax.broadcasted_iota(jnp.int32, rot.shape, 0)
    where_at = base_ref[0] + row // part * page_len + row % part
    turned = turn(rot, where_at, freq_ref[...])
    code = jnp.zeros(rot.shape, F32)
    for p in range(n // part):
        here = (owner_ref[0, p] * slots + slot_ref[0, p]).astype(F32)
        code = jnp.where(row // part == p, here, code)
    out_ref[:, lat:] = jnp.concatenate([turned, code], -1).astype(BF)


def query_where(idx, z, core, qrows, chips):
    blk = idx // qrows
    off = jnp.zeros_like(idx)
    for i, step in enumerate(STEPS):
        off = jnp.where(blk == i, step % chips, off)
    return lax.rem(z + off, chips) * (2 * qrows) + core * qrows + idx % qrows


def pack_kernel(*refs):
    out_ref, at = refs[-1], 0
    for r in refs[:-1]:
        n = r.shape[0]
        out_ref[at : at + n, :] = r[...]
        at += n


def query_kernel(
    where_ref, g_ref, wq0, wq1, ak0, ak1, freq_ref, out_ref, x_ref, *, nope, rope, qrows, chips, nzl
):
    chain, z, core = where_ref[0], where_ref[1], where_ref[2]
    for i, step in enumerate(STEPS):
        at = lax.rem(z + step % chips, chips)
        at = lax.rem(at, nzl) * (chips // nzl) + at // nzl
        x_ref[i * qrows : (i + 1) * qrows, :] = g_ref[pl.ds(pl.multiple_of(at * qrows, qrows), qrows), :]
    x = x_ref[...]
    rows = x.shape[0]
    lat = ak0.shape[-1]
    idx = lax.broadcasted_iota(jnp.int32, (rows, rope), 0)
    place = chain * (chips * 2 * qrows) + query_where(idx, z, core, qrows, chips)
    angle = place.astype(F32) * freq_ref[...]
    lane = lax.broadcasted_iota(jnp.int32, angle.shape, 1)
    sine = jnp.sin(angle)
    sine = jnp.where(lane < rope // 2, -sine, sine)
    cosine = jnp.cos(angle)
    head = 0
    for wq, ak in ((wq0, ak0), (wq1, ak1)):
        q = jnp.dot(x, wq[...], preferred_element_type=F32).astype(BF)
        for h in range(ak.shape[0]):
            base = h * (nope + rope)
            r0 = head * rows
            out_ref[r0 : r0 + rows, :lat] = jnp.dot(
                q[:, base : base + nope], ak[h], preferred_element_type=F32
            ).astype(BF)
            rot = q[:, base + nope : base + nope + rope].astype(F32)
            turned = rot * cosine + swap_halves(rot) * sine
            out_ref[r0 : r0 + rows, lat:] = jnp.concatenate(
                [turned, jnp.zeros_like(turned)], -1
            ).astype(BF)
            head += 1


def attend_kernel(
    where_ref, q_ref, ka_ref, kb_ref, av0, av1, op0, op1, o0, o1, o2, o3, o4,
    s_ref, top_ref, l_ref, acc_ref, ho_ref, *, rows, lat, scale, nch, chips, qrows, part,
):
    chain, z, core = where_ref[0], where_ref[1], where_ref[2]
    s2 = scale * LOG2E
    vh = av0.shape[-1]
    heads = q_ref.shape[0] // rows
    n = ka_ref.shape[0] // nch
    nt = (((1,), (1,)), ((), ()))

    def lanes(x, op):
        out = x[:, :128]
        for c in range(128, x.shape[1], 128):
            out = op(out, x[:, c : c + 128])
        return out

    def score(back):
        if back == 0:
            idx = lax.broadcasted_iota(jnp.int32, (rows, 1), 0)
            qpos = query_where(idx, z, core, qrows, chips)
            idx = lax.broadcasted_iota(jnp.int32, (1, n), 1)
            kpos = (idx % qrows) // part * (chips * 2 * part) + idx // qrows * (2 * part) + idx % part
            ok = [kpos + i * part <= qpos for i in (core, 1 - core)]
        for h in range(heads):
            q = q_ref[h * rows : (h + 1) * rows, :]
            for i, k_ref in enumerate((ka_ref, kb_ref)):
                s = lax.dot_general(q, k_ref[back * n : (back + 1) * n, :], nt, preferred_element_type=F32)
                if back == 0:
                    s = jnp.where(ok[i], s, NEG)
                at = (2 * back + i) * n
                s_ref[h, :, at : at + n] = s
                top = lanes(s, jnp.maximum)
                if back or i:
                    top = jnp.maximum(top, top_ref[h])
                top_ref[h] = top

    def mix(back):
        for h in range(heads):
            m = top_ref[h][:, :1]
            pv = None
            for i, k_ref in enumerate((ka_ref, kb_ref)):
                at = (2 * back + i) * n
                p = jnp.exp2(s_ref[h, :, at : at + n] * s2 - m)
                total = lanes(p, jnp.add)
                if back or i:
                    total += l_ref[h]
                l_ref[h] = total
                part_pv = jnp.dot(
                    p.astype(BF), k_ref[back * n : (back + 1) * n, :lat], preferred_element_type=F32
                )
                pv = part_pv if pv is None else pv + part_pv
            acc_ref[h] = acc_ref[h] + pv if back else pv

    score(0)
    for back in range(1, nch):
        pl.when(chain >= back)(functools.partial(score, back))
    for h in range(heads):
        m = jnp.max(top_ref[h], -1, keepdims=True) * s2
        top_ref[h] = jnp.broadcast_to(m, top_ref.shape[1:])
    mix(0)
    for back in range(1, nch):
        pl.when(chain >= back)(functools.partial(mix, back))
    per = heads // 2
    for h in range(heads):
        total = jnp.sum(l_ref[h], -1, keepdims=True)
        mixed = (acc_ref[h] / total).astype(BF)
        av = (av0 if h < per else av1)[h % per]
        ho_ref[:, h * vh : (h + 1) * vh] = jnp.dot(mixed, av, preferred_element_type=F32).astype(BF)
    ho = ho_ref[...]
    k = op0.shape[0]
    width = op0.shape[1]
    cut = 512 if width % 512 == 0 else width
    for c in range(0, width, cut):
        part_out = (
            jnp.dot(ho[:, :k], op0[:, c : c + cut], preferred_element_type=F32)
            + jnp.dot(ho[:, k:], op1[:, c : c + cut], preferred_element_type=F32)
        ).astype(BF)
        at = 0
        for out_ref in (o0, o1, o2, o3, o4):
            out_ref[:, c : c + cut] = part_out[at : at + out_ref.shape[0]]
            at += out_ref.shape[0]


def local(
    query_comp, latent_rows, rope_keys, latent_gain, query_up, absorb_key, absorb_value, out_proj,
    page_owner, page_slot,
):
    nzh, nzl, nch = lax.axis_size("zh"), lax.axis_size("zl"), lax.axis_size("chain")
    zh, zl, core = lax.axis_index("zh"), lax.axis_index("zl"), lax.axis_index("core")
    chain, dec = lax.axis_index("chain"), lax.axis_index("dec")
    pages, part, lat = latent_rows.shape[1:]
    rope = rope_keys.shape[3]
    heads_here, nope = absorb_key.shape[:2]
    vh = absorb_value.shape[2]
    qrows, ql = query_comp.shape[1:]
    width = out_proj.shape[1]
    tp_index = (zh * nzl + zl) * 2 + core
    tp_count = nzh * nzl * 2
    block_len = qrows * tp_count
    slots = 2 * pages
    smem = pl.BlockSpec(memory_space=pltpu.SMEM)
    vm = pl.BlockSpec(memory_space=pltpu.VMEM)

    def room(mib):
        return pltpu.CompilerParams(vmem_limit_bytes=mib * 1024 * 1024)

    raw = jnp.concatenate(
        [latent_rows[0].reshape(pages * part, lat), rope_keys[0].reshape(pages * part, rope)], -1
    )
    rows = qrows * nzh * nzl
    kw = lat + 2 * rope
    heads = 2 * heads_here
    z = zh * nzl + zl
    where = jnp.stack([chain, z, core]).astype(jnp.int32)
    keys = pl.pallas_call(
        functools.partial(key_kernel, lat=lat, part=part, page_len=part * tp_count, slots=slots),
        out_shape=jax.ShapeDtypeStruct((pages * part, kw), BF),
        in_specs=[smem] * 3 + [vm] * 3,
        out_specs=vm,
        compiler_params=room(4),
        name="keys",
    )(
        (chain * block_len + tp_index * part).astype(jnp.int32)[None],
        page_owner, page_slot, raw, latent_gain[None], frequencies(rope),
    )

    qz = spread(query_comp[0], "zh")
    own = lax.all_gather(keys, Z, axis=0, tiled=True)
    backs = [
        lax.ppermute(own, "chain", [(i, i + k) for i in range(nch - k)]) for k in range(1, nch)
    ]
    qz, *weights, _ = lax.optimization_barrier(
        (qz, query_up, absorb_key, absorb_value, out_proj, own)
    )
    qg = spread(qz, "zl").reshape(rows, ql)
    wq1, ak1, av1, op1 = [swap_core(w) for w in weights]
    mine = pl.pallas_call(
        pack_kernel,
        out_shape=jax.ShapeDtypeStruct((nch * rows, kw), BF),
        in_specs=[vm] * nch,
        out_specs=vm,
        compiler_params=room(4),
        name="pack",
    )(own, *backs)
    other = swap_core(mine)

    q = pl.pallas_call(
        functools.partial(query_kernel, nope=nope, rope=rope, qrows=qrows, chips=nzh * nzl, nzl=nzl),
        out_shape=jax.ShapeDtypeStruct((heads * rows, kw), BF),
        in_specs=[smem] + [vm] * 6,
        out_specs=vm,
        scratch_shapes=[pltpu.VMEM((rows, ql), BF)],
        compiler_params=room(12),
        cost_estimate=pl.CostEstimate(
            flops=2 * rows * heads * (nope + rope) * ql + 2 * rows * heads * nope * lat,
            bytes_accessed=6000000, transcendentals=0,
        ),
        name="queries",
    )(where, qg, query_up, wq1, absorb_key, ak1, frequencies(rope))

    n = nzh * qrows
    sums = pl.pallas_call(
        functools.partial(
            attend_kernel, rows=rows, lat=lat, scale=(nope + rope) ** -0.5,
            nch=nch, chips=nzh * nzl, qrows=qrows, part=part,
        ),
        out_shape=[jax.ShapeDtypeStruct((r, width), BF) for r in (n, n, n, n // 2, n // 2)],
        in_specs=[smem] + [vm] * 7,
        out_specs=[vm] * 5,
        scratch_shapes=[
            pltpu.VMEM((heads, rows, nch * block_len), F32),
            pltpu.VMEM((heads, rows, 128), F32),
            pltpu.VMEM((heads, rows, 128), F32),
            pltpu.VMEM((heads, rows, lat), F32),
            pltpu.VMEM((rows, heads * vh), BF),
        ],
        compiler_params=room(24),
        cost_estimate=pl.CostEstimate(
            flops=4 * rows * heads * nch * block_len * lat, bytes_accessed=9000000,
            transcendentals=rows * heads * nch * block_len,
        ),
        name="attend",
    )(where, q, mine, other, absorb_value, av1, out_proj, op1)

    up2 = shift_z(sums[3], 2)
    down2 = shift_z(sums[4], -2)
    up = shift_z(sums[1], 1)
    down = shift_z(sums[2], -1)

    def near(e):
        at = slice((e + 1) * qrows, (e + 2) * qrows)
        return sums[0][at].astype(F32) + up[at].astype(F32) + down[at].astype(F32)

    cut = width // 2
    far = near(2).astype(BF)
    around = shift_z(far[:, cut:], -nzl)
    direct = shift_z(far[:, :cut], 2 * nzl)
    ahead = shift_z((near(1) + up2[qrows:].astype(F32)).astype(BF), nzl)
    behind = near(-1) + down2[:qrows].astype(F32)
    behind = jnp.concatenate([behind[:, :cut], behind[:, cut:] + around.astype(F32)], -1)
    behind = shift_z(behind.astype(BF), -nzl)
    total = near(0) + up2[:qrows].astype(F32) + down2[qrows:].astype(F32)
    total = total + ahead.astype(F32) + behind.astype(F32)
    total = jnp.concatenate([total[:, :cut] + direct.astype(F32), total[:, cut:]], -1)
    layer_output = total.astype(BF)[None]

    keys = lax.optimization_barrier((keys, up2))[0]
    page = spread(keys.reshape(pages, part, -1), "dec")
    came = page[:, :, 0, lat + rope].reshape(-1).astype(jnp.int32)
    take = (came[None, :] == dec * slots + jnp.arange(slots, dtype=jnp.int32)[:, None]).astype(BF)
    placed = jnp.einsum(
        "sp,pjc->sjc", take, page.reshape(-1, part, page.shape[-1]), preferred_element_type=F32
    ).astype(BF)
    cache_latent = placed[..., :lat][None, None]
    cache_rope = placed[..., lat : lat + rope][None, None]
    return (layer_output, cache_latent, cache_rope)


def solution(mesh):
    shape = mesh.shape
    chips = shape["tp"] // 2
    nzl = 4
    fine = Mesh(
        np.asarray(mesh.devices).reshape(shape["chain"], chips // nzl, nzl, 2, shape["dec"]),
        ("chain", "zh", "zl", "core", "dec"),
    )
    row = ("chain",) + TP
    return jax.shard_map(
        local,
        mesh=fine,
        in_specs=(
            P("dec", row, None),
            P("dec", "chain", TP, None),
            P("dec", "chain", TP, None),
            P(),
            P(None, TP),
            P(TP, None, None),
            P(TP, None, None),
            P(TP, None),
            P("dec", "chain"),
            P("dec", "chain"),
        ),
        out_specs=(
            P("dec", row, None),
            P("dec", "chain", None, TP, None),
            P("dec", "chain", None, TP, None),
        ),
        check_vma=False,
    )
```

```python
import functools

import jax
import jax.numpy as jnp
import numpy as np
from jax import lax
from jax.experimental import pallas as pl
from jax.experimental.pallas import tpu as pltpu
from jax.sharding import Mesh, PartitionSpec as P

BF = jnp.bfloat16
F32 = jnp.float32
LOG2E = 1.4426950408889634
Z = ("zh", "zl")
TP = ("zh", "zl", "core")
NEG = -1e30
STEPS = [4 * e + d for d in (0, 1, -1) for e in (-1, 0, 1, 2)] + [2, 6, -6, -2]


def swap_halves(v):
    half = v.shape[-1] // 2
    return jnp.concatenate([v[..., half:], v[..., :half]], -1)


def shift_z(x, step):
    n = lax.axis_size("zh") * lax.axis_size("zl")
    return lax.ppermute(x, Z, [(i, (i + step) % n) for i in range(n)])


def swap_core(x):
    return lax.ppermute(x, "core", [(0, 1), (1, 0)])


def spread(x, axis):
    n = lax.axis_size(axis)
    return lax.all_to_all(jnp.broadcast_to(x[None], (n,) + x.shape), axis, 0, 0, tiled=True)


def frequencies(width):
    half = width // 2
    f = 10000.0 ** (-(np.arange(half) * 2.0 / width))
    return jnp.asarray(np.concatenate([f, f]).astype(np.float32))[None]


def turn(v, where_at, freq):
    angle = where_at.astype(F32) * freq
    lane = lax.broadcasted_iota(jnp.int32, v.shape, 1)
    sine = jnp.sin(angle)
    sine = jnp.where(lane < v.shape[1] // 2, -sine, sine)
    return v * jnp.cos(angle) + swap_halves(v) * sine


def key_kernel(base_ref, owner_ref, slot_ref, x_ref, gain_ref, freq_ref, out_ref, *, lat, part, page_len, slots):
    x = x_ref[...].astype(F32)
    n = x.shape[0]
    latent, rot = x[:, :lat], x[:, lat:]
    norm = lax.rsqrt(jnp.mean(latent * latent, -1, keepdims=True) + 1e-06)
    out_ref[:, :lat] = (latent * norm * gain_ref[...]).astype(BF)
    row = lax.broadcasted_iota(jnp.int32, rot.shape, 0)
    where_at = base_ref[0] + row // part * page_len + row % part
    turned = turn(rot, where_at, freq_ref[...])
    code = jnp.zeros(rot.shape, F32)
    for p in range(n // part):
        here = (owner_ref[0, p] * slots + slot_ref[0, p]).astype(F32)
        code = jnp.where(row // part == p, here, code)
    out_ref[:, lat:] = jnp.concatenate([turned, code], -1).astype(BF)


def query_where(idx, z, core, qrows, chips):
    blk = idx // qrows
    off = jnp.zeros_like(idx)
    for i, step in enumerate(STEPS):
        off = jnp.where(blk == i, step % chips, off)
    return lax.rem(z + off, chips) * (2 * qrows) + core * qrows + idx % qrows


def pack_kernel(*refs):
    out_ref, at = refs[-1], 0
    for r in refs[:-1]:
        n = r.shape[0]
        out_ref[at : at + n, :] = r[...]
        at += n


def query_kernel(
    where_ref, g_ref, freq_ref, wq0, wq1, ak0, ak1, out_ref, x_ref, wq_ref, ak_ref, sems,
    *, nope, rope, qrows, chips, nzl,
):
    loads = [
        pltpu.make_async_copy(src, dst.at[i], sems.at[2 * j + i])
        for j, (pair, dst) in enumerate((((wq0, wq1), wq_ref), ((ak0, ak1), ak_ref)))
        for i, src in enumerate(pair)
    ]
    for load in loads:
        load.start()
    chain, z, core = where_ref[0], where_ref[1], where_ref[2]
    for i, step in enumerate(STEPS):
        at = lax.rem(z + step % chips, chips)
        at = lax.rem(at, nzl) * (chips // nzl) + at // nzl
        x_ref[i * qrows : (i + 1) * qrows, :] = g_ref[pl.ds(pl.multiple_of(at * qrows, qrows), qrows), :]
    x = x_ref[...]
    rows = x.shape[0]
    lat = ak_ref.shape[-1]
    idx = lax.broadcasted_iota(jnp.int32, (rows, rope), 0)
    place = chain * (chips * 2 * qrows) + query_where(idx, z, core, qrows, chips)
    angle = place.astype(F32) * freq_ref[...]
    lane = lax.broadcasted_iota(jnp.int32, angle.shape, 1)
    sine = jnp.sin(angle)
    sine = jnp.where(lane < rope // 2, -sine, sine)
    cosine = jnp.cos(angle)
    head = 0
    for load in loads:
        load.wait()
    for side in range(2):
        ak = ak_ref.at[side]
        q = jnp.dot(x, wq_ref[side], preferred_element_type=F32).astype(BF)
        for h in range(ak.shape[0]):
            base = h * (nope + rope)
            r0 = head * rows
            out_ref[r0 : r0 + rows, :lat] = jnp.dot(
                q[:, base : base + nope], ak[h], preferred_element_type=F32
            ).astype(BF)
            rot = q[:, base + nope : base + nope + rope].astype(F32)
            turned = rot * cosine + swap_halves(rot) * sine
            out_ref[r0 : r0 + rows, lat:] = jnp.concatenate(
                [turned, jnp.zeros_like(turned)], -1
            ).astype(BF)
            head += 1


def attend_kernel(
    where_ref, q_ref, ka_ref, kb_ref, av0, av1, op0, op1, o0, o1, o2, o3, o4,
    s_ref, top_ref, l_ref, acc_ref, ho_ref, av_ref, op_ref, sems, *, rows, lat, scale, nch, chips, qrows, part,
):
    chain, z, core = where_ref[0], where_ref[1], where_ref[2]
    s2 = scale * LOG2E
    loads = [
        pltpu.make_async_copy(src, dst.at[i], sems.at[2 * j + i])
        for j, (pair, dst) in enumerate((((av0, av1), av_ref), ((op0, op1), op_ref)))
        for i, src in enumerate(pair)
    ]
    for load in loads:
        load.start()
    vh = av_ref.shape[-1]
    heads = q_ref.shape[0] // rows
    n = ka_ref.shape[0] // nch
    nt = (((1,), (1,)), ((), ()))

    def lanes(x, op):
        out = x[:, :128]
        for c in range(128, x.shape[1], 128):
            out = op(out, x[:, c : c + 128])
        return out

    def score(back):
        if back == 0:
            idx = lax.broadcasted_iota(jnp.int32, (rows, 1), 0)
            qpos = query_where(idx, z, core, qrows, chips)
            idx = lax.broadcasted_iota(jnp.int32, (1, n), 1)
            kpos = (idx % qrows) // part * (chips * 2 * part) + idx // qrows * (2 * part) + idx % part
            ok = [kpos + i * part <= qpos for i in (core, 1 - core)]
        for h in range(heads):
            q = q_ref[h * rows : (h + 1) * rows, :]
            for i, k_ref in enumerate((ka_ref, kb_ref)):
                s = lax.dot_general(q, k_ref[back * n : (back + 1) * n, :], nt, preferred_element_type=F32)
                if back == 0:
                    s = jnp.where(ok[i], s, NEG)
                at = (2 * back + i) * n
                s_ref[h, :, at : at + n] = s
                top = lanes(s, jnp.maximum)
                if back or i:
                    top = jnp.maximum(top, top_ref[h])
                top_ref[h] = top

    def mix(back):
        for h in range(heads):
            m = top_ref[h][:, :1]
            pv = None
            for i, k_ref in enumerate((ka_ref, kb_ref)):
                at = (2 * back + i) * n
                p = jnp.exp2(s_ref[h, :, at : at + n] * s2 - m)
                total = lanes(p, jnp.add)
                if back or i:
                    total += l_ref[h]
                l_ref[h] = total
                part_pv = jnp.dot(
                    p.astype(BF), k_ref[back * n : (back + 1) * n, :lat], preferred_element_type=F32
                )
                pv = part_pv if pv is None else pv + part_pv
            acc_ref[h] = acc_ref[h] + pv if back else pv

    score(0)
    for back in range(1, nch):
        pl.when(chain >= back)(functools.partial(score, back))
    for h in range(heads):
        m = jnp.max(top_ref[h], -1, keepdims=True) * s2
        top_ref[h] = jnp.broadcast_to(m, top_ref.shape[1:])
    mix(0)
    for back in range(1, nch):
        pl.when(chain >= back)(functools.partial(mix, back))
    for load in loads:
        load.wait()
    per = heads // 2
    for h in range(heads):
        total = jnp.sum(l_ref[h], -1, keepdims=True)
        mixed = (acc_ref[h] / total).astype(BF)
        av = av_ref[h // per, h % per]
        ho_ref[:, h * vh : (h + 1) * vh] = jnp.dot(mixed, av, preferred_element_type=F32).astype(BF)
    ho = ho_ref[...]
    k, width = op_ref.shape[1:]
    cut = 512 if width % 512 == 0 else width
    for c in range(0, width, cut):
        part_out = (
            jnp.dot(ho[:, :k], op_ref[0, :, c : c + cut], preferred_element_type=F32)
            + jnp.dot(ho[:, k:], op_ref[1, :, c : c + cut], preferred_element_type=F32)
        ).astype(BF)
        at = 0
        for out_ref in (o0, o1, o2, o3, o4):
            out_ref[:, c : c + cut] = part_out[at : at + out_ref.shape[0]]
            at += out_ref.shape[0]


def local(
    query_comp, latent_rows, rope_keys, latent_gain, query_up, absorb_key, absorb_value, out_proj,
    page_owner, page_slot,
):
    nzh, nzl, nch = lax.axis_size("zh"), lax.axis_size("zl"), lax.axis_size("chain")
    zh, zl, core = lax.axis_index("zh"), lax.axis_index("zl"), lax.axis_index("core")
    chain, dec = lax.axis_index("chain"), lax.axis_index("dec")
    pages, part, lat = latent_rows.shape[1:]
    rope = rope_keys.shape[3]
    heads_here, nope = absorb_key.shape[:2]
    vh = absorb_value.shape[2]
    qrows, ql = query_comp.shape[1:]
    width = out_proj.shape[1]
    tp_index = (zh * nzl + zl) * 2 + core
    tp_count = nzh * nzl * 2
    block_len = qrows * tp_count
    slots = 2 * pages
    smem = pl.BlockSpec(memory_space=pltpu.SMEM)
    vm = pl.BlockSpec(memory_space=pltpu.VMEM)
    hbm = pl.BlockSpec(memory_space=pl.ANY)

    def room(mib):
        return pltpu.CompilerParams(vmem_limit_bytes=mib * 1024 * 1024)

    raw = jnp.concatenate(
        [latent_rows[0].reshape(pages * part, lat), rope_keys[0].reshape(pages * part, rope)], -1
    )
    rows = qrows * nzh * nzl
    kw = lat + 2 * rope
    heads = 2 * heads_here
    z = zh * nzl + zl
    where = jnp.stack([chain, z, core]).astype(jnp.int32)
    keys = pl.pallas_call(
        functools.partial(key_kernel, lat=lat, part=part, page_len=part * tp_count, slots=slots),
        out_shape=jax.ShapeDtypeStruct((pages * part, kw), BF),
        in_specs=[smem] * 3 + [vm] * 3,
        out_specs=vm,
        compiler_params=room(4),
        name="keys",
    )(
        (chain * block_len + tp_index * part).astype(jnp.int32)[None],
        page_owner, page_slot, raw, latent_gain[None], frequencies(rope),
    )

    qz = spread(query_comp[0], "zh")
    own = lax.all_gather(keys, Z, axis=0, tiled=True)
    backs = [
        lax.ppermute(own, "chain", [(i, i + k) for i in range(nch - k)]) for k in range(1, nch)
    ]
    qz, _ = lax.optimization_barrier((qz, own))
    *weights, page, _ = lax.optimization_barrier(
        (query_up, absorb_key, absorb_value, out_proj, keys, backs[0])
    )
    qg = spread(qz, "zl").reshape(rows, ql)
    wq1, ak1, av1, op1 = [swap_core(w) for w in weights]
    mine = pl.pallas_call(
        pack_kernel,
        out_shape=jax.ShapeDtypeStruct((nch * rows, kw), BF),
        in_specs=[vm] * nch,
        out_specs=vm,
        compiler_params=room(4),
        name="pack",
    )(own, *backs)
    other = swap_core(mine)

    q = pl.pallas_call(
        functools.partial(query_kernel, nope=nope, rope=rope, qrows=qrows, chips=nzh * nzl, nzl=nzl),
        out_shape=jax.ShapeDtypeStruct((heads * rows, kw), BF),
        in_specs=[smem] + [vm] * 2 + [hbm] * 4,
        out_specs=vm,
        scratch_shapes=[
            pltpu.VMEM((rows, ql), BF),
            pltpu.VMEM((2,) + query_up.shape, BF),
            pltpu.VMEM((2,) + absorb_key.shape, BF),
            pltpu.SemaphoreType.DMA((4,)),
        ],
        compiler_params=room(12),
        cost_estimate=pl.CostEstimate(
            flops=2 * rows * heads * (nope + rope) * ql + 2 * rows * heads * nope * lat,
            bytes_accessed=6000000, transcendentals=0,
        ),
        name="queries",
    )(where, qg, frequencies(rope), query_up, wq1, absorb_key, ak1)

    n = nzh * qrows
    sums = pl.pallas_call(
        functools.partial(
            attend_kernel, rows=rows, lat=lat, scale=(nope + rope) ** -0.5,
            nch=nch, chips=nzh * nzl, qrows=qrows, part=part,
        ),
        out_shape=[jax.ShapeDtypeStruct((r, width), BF) for r in (n, n, n, n // 2, n // 2)],
        in_specs=[smem] + [vm] * 3 + [hbm] * 4,
        out_specs=[vm] * 5,
        scratch_shapes=[
            pltpu.VMEM((heads, rows, nch * block_len), F32),
            pltpu.VMEM((heads, rows, 128), F32),
            pltpu.VMEM((heads, rows, 128), F32),
            pltpu.VMEM((heads, rows, lat), F32),
            pltpu.VMEM((rows, heads * vh), BF),
            pltpu.VMEM((2,) + absorb_value.shape, BF),
            pltpu.VMEM((2,) + out_proj.shape, BF),
            pltpu.SemaphoreType.DMA((4,)),
        ],
        compiler_params=room(28),
        cost_estimate=pl.CostEstimate(
            flops=4 * rows * heads * nch * block_len * lat, bytes_accessed=9000000,
            transcendentals=rows * heads * nch * block_len,
        ),
        name="attend",
    )(where, q, mine, other, absorb_value, av1, out_proj, op1)

    up = shift_z(sums[1], 1)
    down = shift_z(sums[2], -1)
    up2 = shift_z(sums[3], 2)
    down2 = shift_z(sums[4], -2)
    cut = width // 2

    def near(e, up, down):
        at = slice((e + 1) * qrows, (e + 2) * qrows)
        return sums[0][at].astype(F32) + up[at].astype(F32) + down[at].astype(F32)

    far = near(2, up, down).astype(BF)
    far, up, down = lax.optimization_barrier((far, up, down))
    left = shift_z(far[:, :cut], nzl).astype(F32)
    right = shift_z(far[:, cut:], -nzl).astype(F32)
    ahead = near(1, up, down) + up2[qrows:].astype(F32)
    ahead = jnp.concatenate([ahead[:, :cut] + left, ahead[:, cut:]], -1)
    ahead = shift_z(ahead.astype(BF), nzl)
    behind = near(-1, up, down) + down2[:qrows].astype(F32)
    behind = jnp.concatenate([behind[:, :cut], behind[:, cut:] + right], -1)
    behind = shift_z(behind.astype(BF), -nzl)
    total = near(0, up, down) + up2[:qrows].astype(F32) + down2[qrows:].astype(F32)
    total = total + ahead.astype(F32) + behind.astype(F32)
    layer_output = total.astype(BF)[None]

    page = spread(page.reshape(pages, part, -1), "dec")
    came = page[:, :, 0, lat + rope].reshape(-1).astype(jnp.int32)
    take = (came[None, :] == dec * slots + jnp.arange(slots, dtype=jnp.int32)[:, None]).astype(BF)
    placed = jnp.einsum(
        "sp,pjc->sjc", take, page.reshape(-1, part, page.shape[-1]), preferred_element_type=F32
    ).astype(BF)
    cache_latent = placed[..., :lat][None, None]
    cache_rope = placed[..., lat : lat + rope][None, None]
    return (layer_output, cache_latent, cache_rope)


def solution(mesh):
    shape = mesh.shape
    chips = shape["tp"] // 2
    nzl = 4
    fine = Mesh(
        np.asarray(mesh.devices).reshape(shape["chain"], chips // nzl, nzl, 2, shape["dec"]),
        ("chain", "zh", "zl", "core", "dec"),
    )
    row = ("chain",) + TP
    return jax.shard_map(
        local,
        mesh=fine,
        in_specs=(
            P("dec", row, None),
            P("dec", "chain", TP, None),
            P("dec", "chain", TP, None),
            P(),
            P(None, TP),
            P(TP, None, None),
            P(TP, None, None),
            P(TP, None),
            P("dec", "chain"),
            P("dec", "chain"),
        ),
        out_specs=(
            P("dec", row, None),
            P("dec", "chain", None, TP, None),
            P("dec", "chain", None, TP, None),
        ),
        check_vma=False,
    )
```

```python
import functools

import jax
import jax.numpy as jnp
import numpy as np
from jax import lax
from jax.experimental import pallas as pl
from jax.experimental.pallas import tpu as pltpu
from jax.sharding import Mesh, PartitionSpec as P

BF = jnp.bfloat16
F32 = jnp.float32
LOG2E = 1.4426950408889634
Z = ("zh", "zl")
TP = ("zh", "zl", "core")
NEG = -1e30
STEPS = [4 * e + d for d in (0, 1, -1) for e in (-1, 0, 1, 2)] + [2, 6, -6, -2]


def swap_halves(v):
    half = v.shape[-1] // 2
    return jnp.concatenate([v[..., half:], v[..., :half]], -1)


def shift_z(x, step):
    n = lax.axis_size("zh") * lax.axis_size("zl")
    return lax.ppermute(x, Z, [(i, (i + step) % n) for i in range(n)])


def swap_core(x):
    return lax.ppermute(x, "core", [(0, 1), (1, 0)])


def spread(x, axis):
    n = lax.axis_size(axis)
    return lax.all_to_all(jnp.broadcast_to(x[None], (n,) + x.shape), axis, 0, 0, tiled=True)


def frequencies(width):
    half = width // 2
    f = 10000.0 ** (-(np.arange(half) * 2.0 / width))
    return jnp.asarray(np.concatenate([f, f]).astype(np.float32))[None]


def turn(v, where_at, freq):
    angle = where_at.astype(F32) * freq
    lane = lax.broadcasted_iota(jnp.int32, v.shape, 1)
    sine = jnp.sin(angle)
    sine = jnp.where(lane < v.shape[1] // 2, -sine, sine)
    return v * jnp.cos(angle) + swap_halves(v) * sine


def key_kernel(base_ref, owner_ref, slot_ref, x_ref, gain_ref, freq_ref, out_ref, *, lat, part, page_len, slots):
    x = x_ref[...].astype(F32)
    n = x.shape[0]
    latent, rot = x[:, :lat], x[:, lat:]
    norm = lax.rsqrt(jnp.mean(latent * latent, -1, keepdims=True) + 1e-06)
    out_ref[:, :lat] = (latent * norm * gain_ref[...]).astype(BF)
    row = lax.broadcasted_iota(jnp.int32, rot.shape, 0)
    where_at = base_ref[0] + row // part * page_len + row % part
    turned = turn(rot, where_at, freq_ref[...])
    code = jnp.zeros(rot.shape, F32)
    for p in range(n // part):
        here = (owner_ref[0, p] * slots + slot_ref[0, p]).astype(F32)
        code = jnp.where(row // part == p, here, code)
    out_ref[:, lat:] = jnp.concatenate([turned, code], -1).astype(BF)


def query_where(idx, z, core, qrows, chips):
    blk = idx // qrows
    off = jnp.zeros_like(idx)
    for i, step in enumerate(STEPS):
        off = jnp.where(blk == i, step % chips, off)
    return lax.rem(z + off, chips) * (2 * qrows) + core * qrows + idx % qrows


def query_kernel(
    where_ref, g_ref, freq_ref, wq0, wq1, ak0, ak1, out_ref, x_ref, wq_ref, ak_ref, sems,
    *, nope, rope, qrows, chips,
):
    loads = [
        pltpu.make_async_copy(src, dst.at[i], sems.at[2 * j + i])
        for j, (pair, dst) in enumerate((((wq0, wq1), wq_ref), ((ak0, ak1), ak_ref)))
        for i, src in enumerate(pair)
    ]
    for load in loads:
        load.start()
    chain, z, core = where_ref[0], where_ref[1], where_ref[2]
    for i, step in enumerate(STEPS):
        at = lax.rem(z + step % chips, chips)
        x_ref[i * qrows : (i + 1) * qrows, :] = g_ref[pl.ds(pl.multiple_of(at * qrows, qrows), qrows), :]
    x = x_ref[...]
    rows = x.shape[0]
    lat = ak_ref.shape[-1]
    idx = lax.broadcasted_iota(jnp.int32, (rows, rope), 0)
    place = chain * (chips * 2 * qrows) + query_where(idx, z, core, qrows, chips)
    angle = place.astype(F32) * freq_ref[...]
    lane = lax.broadcasted_iota(jnp.int32, angle.shape, 1)
    sine = jnp.sin(angle)
    sine = jnp.where(lane < rope // 2, -sine, sine)
    cosine = jnp.cos(angle)
    head = 0
    for load in loads:
        load.wait()
    for side in range(2):
        ak = ak_ref.at[side]
        q = jnp.dot(x, wq_ref[side], preferred_element_type=F32).astype(BF)
        for h in range(ak.shape[0]):
            base = h * (nope + rope)
            r0 = head * rows
            out_ref[r0 : r0 + rows, :lat] = jnp.dot(
                q[:, base : base + nope], ak[h], preferred_element_type=F32
            ).astype(BF)
            rot = q[:, base + nope : base + nope + rope].astype(F32)
            turned = rot * cosine + swap_halves(rot) * sine
            out_ref[r0 : r0 + rows, lat:] = jnp.concatenate(
                [turned, jnp.zeros_like(turned)], -1
            ).astype(BF)
            head += 1


def attend_kernel(
    where_ref, q_ref, ka_ref, kb_ref, av0, av1, op0, op1, o0, o1, o2, o3, o4,
    s_ref, top_ref, l_ref, acc_ref, ho_ref, av_ref, op_ref, sems, *, rows, lat, scale, nch, chips, qrows, part,
):
    chain, z, core = where_ref[0], where_ref[1], where_ref[2]
    s2 = scale * LOG2E
    loads = [
        pltpu.make_async_copy(src, dst.at[i], sems.at[2 * j + i])
        for j, (pair, dst) in enumerate((((av0, av1), av_ref), ((op0, op1), op_ref)))
        for i, src in enumerate(pair)
    ]
    for load in loads:
        load.start()
    vh = av_ref.shape[-1]
    heads = q_ref.shape[0] // rows
    n = ka_ref.shape[0] // nch
    nt = (((1,), (1,)), ((), ()))

    def lanes(x, op):
        out = x[:, :128]
        for c in range(128, x.shape[1], 128):
            out = op(out, x[:, c : c + 128])
        return out

    def block(back):
        return pl.ds(pl.multiple_of(jnp.maximum(chain - back, 0) * n, n), n)

    def score(back):
        if back == 0:
            idx = lax.broadcasted_iota(jnp.int32, (rows, 1), 0)
            qpos = query_where(idx, z, core, qrows, chips)
            idx = lax.broadcasted_iota(jnp.int32, (1, n), 1)
            kpos = (idx % qrows) // part * (chips * 2 * part) + idx // qrows * (2 * part) + idx % part
            ok = [kpos + i * part <= qpos for i in (core, 1 - core)]
        for h in range(heads):
            q = q_ref[h * rows : (h + 1) * rows, :]
            for i, k_ref in enumerate((ka_ref, kb_ref)):
                s = lax.dot_general(q, k_ref[block(back), :], nt, preferred_element_type=F32)
                if back == 0:
                    s = jnp.where(ok[i], s, NEG)
                at = (2 * back + i) * n
                s_ref[h, :, at : at + n] = s
                top = lanes(s, jnp.maximum)
                if back or i:
                    top = jnp.maximum(top, top_ref[h])
                top_ref[h] = top

    def mix(back):
        for h in range(heads):
            m = top_ref[h][:, :1]
            pv = None
            for i, k_ref in enumerate((ka_ref, kb_ref)):
                at = (2 * back + i) * n
                p = jnp.exp2(s_ref[h, :, at : at + n] * s2 - m)
                total = lanes(p, jnp.add)
                if back or i:
                    total += l_ref[h]
                l_ref[h] = total
                part_pv = jnp.dot(
                    p.astype(BF), k_ref[block(back), :lat], preferred_element_type=F32
                )
                pv = part_pv if pv is None else pv + part_pv
            acc_ref[h] = acc_ref[h] + pv if back else pv

    score(0)
    for back in range(1, nch):
        pl.when(chain >= back)(functools.partial(score, back))
    for h in range(heads):
        m = jnp.max(top_ref[h], -1, keepdims=True) * s2
        top_ref[h] = jnp.broadcast_to(m, top_ref.shape[1:])
    mix(0)
    for back in range(1, nch):
        pl.when(chain >= back)(functools.partial(mix, back))
    for load in loads:
        load.wait()
    per = heads // 2
    for h in range(heads):
        total = jnp.sum(l_ref[h], -1, keepdims=True)
        mixed = (acc_ref[h] / total).astype(BF)
        av = av_ref[h // per, h % per]
        ho_ref[:, h * vh : (h + 1) * vh] = jnp.dot(mixed, av, preferred_element_type=F32).astype(BF)
    ho = ho_ref[...]
    k, width = op_ref.shape[1:]
    cut = 512 if width % 512 == 0 else width
    for c in range(0, width, cut):
        part_out = (
            jnp.dot(ho[:, :k], op_ref[0, :, c : c + cut], preferred_element_type=F32)
            + jnp.dot(ho[:, k:], op_ref[1, :, c : c + cut], preferred_element_type=F32)
        ).astype(BF)
        at = 0
        for out_ref in (o0, o1, o2, o3, o4):
            out_ref[:, c : c + cut] = part_out[at : at + out_ref.shape[0]]
            at += out_ref.shape[0]


def local(
    query_comp, latent_rows, rope_keys, latent_gain, query_up, absorb_key, absorb_value, out_proj,
    page_owner, page_slot,
):
    nzh, nzl, nch = lax.axis_size("zh"), lax.axis_size("zl"), lax.axis_size("chain")
    zh, zl, core = lax.axis_index("zh"), lax.axis_index("zl"), lax.axis_index("core")
    chain, dec = lax.axis_index("chain"), lax.axis_index("dec")
    pages, part, lat = latent_rows.shape[1:]
    rope = rope_keys.shape[3]
    heads_here, nope = absorb_key.shape[:2]
    vh = absorb_value.shape[2]
    qrows, ql = query_comp.shape[1:]
    width = out_proj.shape[1]
    tp_index = (zh * nzl + zl) * 2 + core
    tp_count = nzh * nzl * 2
    block_len = qrows * tp_count
    slots = 2 * pages
    smem = pl.BlockSpec(memory_space=pltpu.SMEM)
    vm = pl.BlockSpec(memory_space=pltpu.VMEM)
    hbm = pl.BlockSpec(memory_space=pltpu.HBM)

    def room(mib):
        return pltpu.CompilerParams(vmem_limit_bytes=mib * 1024 * 1024)

    raw = jnp.concatenate(
        [latent_rows[0].reshape(pages * part, lat), rope_keys[0].reshape(pages * part, rope)], -1
    )
    rows = qrows * nzh * nzl
    kw = lat + 2 * rope
    heads = 2 * heads_here
    z = zh * nzl + zl
    where = jnp.stack([chain, z, core]).astype(jnp.int32)
    keys = pl.pallas_call(
        functools.partial(key_kernel, lat=lat, part=part, page_len=part * tp_count, slots=slots),
        out_shape=jax.ShapeDtypeStruct((pages * part, kw), BF),
        in_specs=[smem] * 3 + [vm] * 3,
        out_specs=vm,
        compiler_params=room(4),
        name="keys",
    )(
        (chain * block_len + tp_index * part).astype(jnp.int32)[None],
        page_owner, page_slot, raw, latent_gain[None], frequencies(rope),
    )

    own = lax.all_gather(keys, Z, axis=0, tiled=True)
    mine = spread(own, "chain").reshape(nch * rows, kw)
    held = lax.optimization_barrier((query_comp[0], own))[0]
    qg = lax.all_gather(held, Z, axis=0, tiled=True)
    wq1, ak1, av1, op1 = [swap_core(w) for w in (query_up, absorb_key, absorb_value, out_proj)]
    qg, mine = lax.optimization_barrier((qg, mine))
    other = swap_core(mine)

    q = pl.pallas_call(
        functools.partial(query_kernel, nope=nope, rope=rope, qrows=qrows, chips=nzh * nzl),
        out_shape=jax.ShapeDtypeStruct((heads * rows, kw), BF),
        in_specs=[smem] + [vm] * 2 + [hbm] * 4,
        out_specs=vm,
        scratch_shapes=[
            pltpu.VMEM((rows, ql), BF),
            pltpu.VMEM((2,) + query_up.shape, BF),
            pltpu.VMEM((2,) + absorb_key.shape, BF),
            pltpu.SemaphoreType.DMA((4,)),
        ],
        compiler_params=room(12),
        cost_estimate=pl.CostEstimate(
            flops=2 * rows * heads * (nope + rope) * ql + 2 * rows * heads * nope * lat,
            bytes_accessed=6000000, transcendentals=0,
        ),
        name="queries",
    )(where, qg, frequencies(rope), query_up, wq1, absorb_key, ak1)

    n = nzh * qrows
    sums = pl.pallas_call(
        functools.partial(
            attend_kernel, rows=rows, lat=lat, scale=(nope + rope) ** -0.5,
            nch=nch, chips=nzh * nzl, qrows=qrows, part=part,
        ),
        out_shape=[jax.ShapeDtypeStruct((r, width), BF) for r in (n, n, n, n // 2, n // 2)],
        in_specs=[smem] + [vm] * 3 + [hbm] * 4,
        out_specs=[vm] * 5,
        scratch_shapes=[
            pltpu.VMEM((heads, rows, nch * block_len), F32),
            pltpu.VMEM((heads, rows, 128), F32),
            pltpu.VMEM((heads, rows, 128), F32),
            pltpu.VMEM((heads, rows, lat), F32),
            pltpu.VMEM((rows, heads * vh), BF),
            pltpu.VMEM((2,) + absorb_value.shape, BF),
            pltpu.VMEM((2,) + out_proj.shape, BF),
            pltpu.SemaphoreType.DMA((4,)),
        ],
        compiler_params=room(28),
        cost_estimate=pl.CostEstimate(
            flops=4 * rows * heads * nch * block_len * lat, bytes_accessed=9000000,
            transcendentals=rows * heads * nch * block_len,
        ),
        name="attend",
    )(where, q, mine, other, absorb_value, av1, out_proj, op1)

    up = shift_z(sums[1], 1)
    down = shift_z(sums[2], -1)
    up2 = shift_z(sums[3], 2)
    down2 = shift_z(sums[4], -2)
    cut = width // 2

    def near(e, up, down):
        at = slice((e + 1) * qrows, (e + 2) * qrows)
        return sums[0][at].astype(F32) + up[at].astype(F32) + down[at].astype(F32)

    far = near(2, up, down).astype(BF)
    far, up, down = lax.optimization_barrier((far, up, down))
    left = shift_z(far[:, :cut], nzl).astype(F32)
    right = shift_z(far[:, cut:], -nzl).astype(F32)
    ahead = near(1, up, down) + up2[qrows:].astype(F32)
    ahead = jnp.concatenate([ahead[:, :cut] + left, ahead[:, cut:]], -1)
    ahead = shift_z(ahead.astype(BF), nzl)
    behind = near(-1, up, down) + down2[:qrows].astype(F32)
    behind = jnp.concatenate([behind[:, :cut], behind[:, cut:] + right], -1)
    behind = shift_z(behind.astype(BF), -nzl)
    total = near(0, up, down) + up2[:qrows].astype(F32) + down2[qrows:].astype(F32)
    total = total + ahead.astype(F32) + behind.astype(F32)
    layer_output = total.astype(BF)[None]

    page = lax.optimization_barrier((keys, far))[0]
    page = spread(page.reshape(pages, part, -1), "dec")
    came = page[:, :, 0, lat + rope].reshape(-1).astype(jnp.int32)
    take = (came[None, :] == dec * slots + jnp.arange(slots, dtype=jnp.int32)[:, None]).astype(BF)
    placed = jnp.einsum(
        "sp,pjc->sjc", take, page.reshape(-1, part, page.shape[-1]), preferred_element_type=F32
    ).astype(BF)
    cache_latent = placed[..., :lat][None, None]
    cache_rope = placed[..., lat : lat + rope][None, None]
    return (layer_output, cache_latent, cache_rope)


def solution(mesh):
    shape = mesh.shape
    chips = shape["tp"] // 2
    nzl = 4
    fine = Mesh(
        np.asarray(mesh.devices).reshape(shape["chain"], chips // nzl, nzl, 2, shape["dec"]),
        ("chain", "zh", "zl", "core", "dec"),
    )
    row = ("chain",) + TP
    return jax.shard_map(
        local,
        mesh=fine,
        in_specs=(
            P("dec", row, None),
            P("dec", "chain", TP, None),
            P("dec", "chain", TP, None),
            P(),
            P(None, TP),
            P(TP, None, None),
            P(TP, None, None),
            P(TP, None),
            P("dec", "chain"),
            P("dec", "chain"),
        ),
        out_specs=(
            P("dec", row, None),
            P("dec", "chain", None, TP, None),
            P("dec", "chain", None, TP, None),
        ),
        check_vma=False,
    )
```

```python
import functools

import jax
import jax.numpy as jnp
import numpy as np
from jax import lax
from jax.experimental import pallas as pl
from jax.experimental.pallas import tpu as pltpu
from jax.sharding import Mesh, PartitionSpec as P

BF = jnp.bfloat16
F32 = jnp.float32
LOG2E = 1.4426950408889634
Z = ("zh", "zl")
TP = ("zh", "zl", "core")
NEG = -1e30
STEPS = [4 * e + d for d in (0, 1, -1) for e in (-1, 0, 1, 2)] + [2, 6, -6, -2]


def swap_halves(v):
    half = v.shape[-1] // 2
    return jnp.concatenate([v[..., half:], v[..., :half]], -1)


def shift_z(x, step):
    n = lax.axis_size("zh") * lax.axis_size("zl")
    return lax.ppermute(x, Z, [(i, (i + step) % n) for i in range(n)])


def swap_core(x):
    return lax.ppermute(x, "core", [(0, 1), (1, 0)])


def spread(x, axis):
    n = lax.axis_size(axis)
    return lax.all_to_all(jnp.broadcast_to(x[None], (n,) + x.shape), axis, 0, 0, tiled=True)


def frequencies(width):
    half = width // 2
    lane = lax.broadcasted_iota(jnp.int32, (1, width), 1)
    out = jnp.ones((1, width), F32)
    for i in range(1, half):
        out = jnp.where(lane % half == i, np.float32(10000.0 ** (-2.0 * i / width)), out)
    return out


def rope_factors(where_at):
    width = where_at.shape[1]
    angle = where_at.astype(F32) * frequencies(width)
    lane = lax.broadcasted_iota(jnp.int32, where_at.shape, 1)
    sine = jnp.sin(angle)
    return jnp.cos(angle), jnp.where(lane < width // 2, -sine, sine)


def key_kernel(base_ref, x_ref, gain_ref, out_ref, *, lat, part, page_len):
    x = x_ref[...].astype(F32)
    latent, rot = x[:, :lat], x[:, lat:]
    norm = lax.rsqrt(jnp.mean(latent * latent, -1, keepdims=True) + 1e-06)
    out_ref[:, :lat] = (latent * norm * gain_ref[...]).astype(BF)
    row = lax.broadcasted_iota(jnp.int32, rot.shape, 0)
    cosine, sine = rope_factors(base_ref[0] + row // part * page_len + row % part)
    turned = rot * cosine + swap_halves(rot) * sine
    out_ref[:, lat:] = jnp.concatenate([turned, jnp.zeros_like(turned)], -1).astype(BF)


def page_kernel(owner_ref, slot_ref, key_ref, out_ref, *, lat, part, slots):
    tail = key_ref[:, lat:].astype(F32)
    row = lax.broadcasted_iota(jnp.int32, tail.shape, 0)
    lane = lax.broadcasted_iota(jnp.int32, tail.shape, 1)
    code = jnp.zeros(tail.shape, F32)
    for p in range(tail.shape[0] // part):
        here = (owner_ref[0, p] * slots + slot_ref[0, p]).astype(F32)
        code = jnp.where(row // part == p, here, code)
    tail = jnp.where(lane < tail.shape[1] // 2, tail, code).astype(BF)
    for i in range(out_ref.shape[0]):
        out_ref[i, :, :lat] = key_ref[:, :lat]
        out_ref[i, :, lat:] = tail


def blocks(shapes):
    at = 0
    for w, shape in enumerate(shapes):
        for lead in range(int(np.prod(shape[:-2]))):
            for c in range(0, shape[-1], 128):
                yield at, w, lead, c, shape[-2]
                at += shape[-2]


def packed_rows(shapes):
    return sum(int(np.prod(shape)) for shape in shapes) // 128


def block_of(ref, lead, c):
    if len(ref.shape) == 3:
        return ref.at[lead, :, pl.ds(c, 128)]
    return ref.at[:, pl.ds(c, 128)]


def pack_kernel(*refs, shapes):
    ins, out_ref, sems = refs[: len(shapes)], refs[-2], refs[-1]
    loads = [
        pltpu.make_async_copy(block_of(ins[w], lead, c), out_ref.at[pl.ds(at, n), :], sems.at[i])
        for i, (at, w, lead, c, n) in enumerate(blocks(shapes))
    ]
    for load in loads:
        load.start()
    for load in loads:
        load.wait()


def weight_loads(own, packed, dst, which, shapes, sems):
    loads = [(src, d.at[0]) for src, d in zip(own, dst)]
    for at, w, lead, c, n in blocks(shapes):
        if w in which:
            to = block_of(dst[which.index(w)].at[1], lead, c)
            loads.append((packed.at[pl.ds(at, n), :], to))
    return [pltpu.make_async_copy(src, to, sems.at[i]) for i, (src, to) in enumerate(loads)]


def load_count(which, shapes):
    return len(which) + sum(1 for b in blocks(shapes) if b[1] in which)


def query_where(idx, z, core, qrows, chips):
    blk = idx // qrows
    off = jnp.zeros_like(idx)
    for i, step in enumerate(STEPS):
        off = jnp.where(blk == i, step % chips, off)
    return lax.rem(z + off, chips) * (2 * qrows) + core * qrows + idx % qrows


def query_kernel(
    where_ref, g_ref, wq0, ak0, packed, out_ref, x_ref, wq_ref, ak_ref, sems,
    *, nope, rope, qrows, chips, shapes,
):
    loads = weight_loads((wq0, ak0), packed, (wq_ref, ak_ref), (0, 1), shapes, sems)
    for load in loads:
        load.start()
    chain, z, core = where_ref[0], where_ref[1], where_ref[2]
    for i, step in enumerate(STEPS):
        at = lax.rem(z + step % chips, chips)
        x_ref[i * qrows : (i + 1) * qrows, :] = g_ref[pl.ds(pl.multiple_of(at * qrows, qrows), qrows), :]
    x = x_ref[...]
    rows = x.shape[0]
    lat = ak_ref.shape[-1]
    idx = lax.broadcasted_iota(jnp.int32, (rows, rope), 0)
    place = chain * (chips * 2 * qrows) + query_where(idx, z, core, qrows, chips)
    cosine, sine = rope_factors(place)
    head = 0
    for load in loads:
        load.wait()
    for side in range(2):
        ak = ak_ref.at[side]
        q = jnp.dot(x, wq_ref[side], preferred_element_type=F32).astype(BF)
        for h in range(ak.shape[0]):
            base = h * (nope + rope)
            r0 = head * rows
            out_ref[r0 : r0 + rows, :lat] = jnp.dot(
                q[:, base : base + nope], ak[h], preferred_element_type=F32
            ).astype(BF)
            rot = q[:, base + nope : base + nope + rope].astype(F32)
            turned = rot * cosine + swap_halves(rot) * sine
            out_ref[r0 : r0 + rows, lat:] = jnp.concatenate(
                [turned, jnp.zeros_like(turned)], -1
            ).astype(BF)
            head += 1


def attend_kernel(
    where_ref, q_ref, ka_ref, kb_ref, av0, op0, packed, o0, o1, o2, o3, o4,
    s_ref, top_ref, l_ref, acc_ref, ho_ref, av_ref, op_ref, sems, *, rows, lat, scale, nch, chips, qrows, part, shapes,
):
    chain, z, core = where_ref[0], where_ref[1], where_ref[2]
    s2 = scale * LOG2E
    loads = weight_loads((av0, op0), packed, (av_ref, op_ref), (2, 3), shapes, sems)
    for load in loads:
        load.start()
    vh = av_ref.shape[-1]
    heads = q_ref.shape[0] // rows
    n = ka_ref.shape[0] // nch
    nt = (((1,), (1,)), ((), ()))

    def lanes(x, op):
        out = x[:, :128]
        for c in range(128, x.shape[1], 128):
            out = op(out, x[:, c : c + 128])
        return out

    def block(back):
        return pl.ds(pl.multiple_of(jnp.maximum(chain - back, 0) * n, n), n)

    def score(back):
        if back == 0:
            idx = lax.broadcasted_iota(jnp.int32, (rows, 1), 0)
            qpos = query_where(idx, z, core, qrows, chips)
            idx = lax.broadcasted_iota(jnp.int32, (1, n), 1)
            kpos = (idx % qrows) // part * (chips * 2 * part) + idx // qrows * (2 * part) + idx % part
            ok = [kpos + i * part <= qpos for i in (core, 1 - core)]
        for h in range(heads):
            q = q_ref[h * rows : (h + 1) * rows, :]
            for i, k_ref in enumerate((ka_ref, kb_ref)):
                s = lax.dot_general(q, k_ref[block(back), :], nt, preferred_element_type=F32)
                if back == 0:
                    s = jnp.where(ok[i], s, NEG)
                at = (2 * back + i) * n
                s_ref[h, :, at : at + n] = s
                top = lanes(s, jnp.maximum)
                if back or i:
                    top = jnp.maximum(top, top_ref[h])
                top_ref[h] = top

    def mix(back):
        for h in range(heads):
            m = top_ref[h][:, :1]
            pv = None
            for i, k_ref in enumerate((ka_ref, kb_ref)):
                at = (2 * back + i) * n
                p = jnp.exp2(s_ref[h, :, at : at + n] * s2 - m)
                total = lanes(p, jnp.add)
                if back or i:
                    total += l_ref[h]
                l_ref[h] = total
                part_pv = jnp.dot(
                    p.astype(BF), k_ref[block(back), :lat], preferred_element_type=F32
                )
                pv = part_pv if pv is None else pv + part_pv
            acc_ref[h] = acc_ref[h] + pv if back else pv

    score(0)
    for back in range(1, nch):
        pl.when(chain >= back)(functools.partial(score, back))
    for h in range(heads):
        m = jnp.max(top_ref[h], -1, keepdims=True) * s2
        top_ref[h] = jnp.broadcast_to(m, top_ref.shape[1:])
    mix(0)
    for back in range(1, nch):
        pl.when(chain >= back)(functools.partial(mix, back))
    for load in loads:
        load.wait()
    per = heads // 2
    for h in range(heads):
        total = jnp.sum(l_ref[h], -1, keepdims=True)
        mixed = (acc_ref[h] / total).astype(BF)
        av = av_ref[h // per, h % per]
        ho_ref[:, h * vh : (h + 1) * vh] = jnp.dot(mixed, av, preferred_element_type=F32).astype(BF)
    ho = ho_ref[...]
    k, width = op_ref.shape[1:]
    cut = 512 if width % 512 == 0 else width
    for c in range(0, width, cut):
        part_out = (
            jnp.dot(ho[:, :k], op_ref[0, :, c : c + cut], preferred_element_type=F32)
            + jnp.dot(ho[:, k:], op_ref[1, :, c : c + cut], preferred_element_type=F32)
        ).astype(BF)
        at = 0
        for out_ref in (o0, o1, o2, o3, o4):
            out_ref[:, c : c + cut] = part_out[at : at + out_ref.shape[0]]
            at += out_ref.shape[0]


def local(
    query_comp, latent_rows, rope_keys, latent_gain, query_up, absorb_key, absorb_value, out_proj,
    page_owner, page_slot,
):
    nzh, nzl, nch = lax.axis_size("zh"), lax.axis_size("zl"), lax.axis_size("chain")
    zh, zl, core = lax.axis_index("zh"), lax.axis_index("zl"), lax.axis_index("core")
    chain, dec = lax.axis_index("chain"), lax.axis_index("dec")
    pages, part, lat = latent_rows.shape[1:]
    rope = rope_keys.shape[3]
    heads_here, nope = absorb_key.shape[:2]
    vh = absorb_value.shape[2]
    qrows, ql = query_comp.shape[1:]
    width = out_proj.shape[1]
    tp_index = (zh * nzl + zl) * 2 + core
    tp_count = nzh * nzl * 2
    block_len = qrows * tp_count
    slots = 2 * pages
    smem = pl.BlockSpec(memory_space=pltpu.SMEM)
    vm = pl.BlockSpec(memory_space=pltpu.VMEM)
    hbm = pl.BlockSpec(memory_space=pltpu.HBM)

    def room(mib):
        return pltpu.CompilerParams(vmem_limit_bytes=mib * 1024 * 1024)

    raw = jnp.concatenate(
        [latent_rows[0].reshape(pages * part, lat), rope_keys[0].reshape(pages * part, rope)], -1
    )
    rows = qrows * nzh * nzl
    kw = lat + 2 * rope
    heads = 2 * heads_here
    z = zh * nzl + zl
    where = jnp.stack([chain, z, core]).astype(jnp.int32)
    keys = pl.pallas_call(
        functools.partial(key_kernel, lat=lat, part=part, page_len=part * tp_count),
        out_shape=jax.ShapeDtypeStruct((pages * part, kw), BF),
        in_specs=[smem, vm, vm],
        out_specs=vm,
        compiler_params=room(4),
        name="keys",
    )((chain * block_len + tp_index * part).astype(jnp.int32)[None], raw, latent_gain[None])

    weights = (query_up, absorb_key, absorb_value, out_proj)
    shapes = tuple(w.shape for w in weights)
    count = len(list(blocks(shapes)))
    packed = pl.pallas_call(
        functools.partial(pack_kernel, shapes=shapes),
        out_shape=jax.ShapeDtypeStruct((packed_rows(shapes), 128), BF),
        in_specs=[hbm] * 4,
        out_specs=vm,
        scratch_shapes=[pltpu.SemaphoreType.DMA((count,))],
        compiler_params=room(8),
        name="pack",
    )(*weights)
    packed = swap_core(packed)

    own = lax.all_gather(keys, Z, axis=0, tiled=True)
    mine = spread(own, "chain").reshape(nch * rows, kw)
    held = lax.optimization_barrier((query_comp[0], own))[0]
    qg = lax.all_gather(held, Z, axis=0, tiled=True)
    qg, mine = lax.optimization_barrier((qg, mine))
    other = swap_core(mine)

    q = pl.pallas_call(
        functools.partial(query_kernel, nope=nope, rope=rope, qrows=qrows, chips=nzh * nzl, shapes=shapes),
        out_shape=jax.ShapeDtypeStruct((heads * rows, kw), BF),
        in_specs=[smem, vm] + [hbm] * 3,
        out_specs=vm,
        scratch_shapes=[
            pltpu.VMEM((rows, ql), BF),
            pltpu.VMEM((2,) + query_up.shape, BF),
            pltpu.VMEM((2,) + absorb_key.shape, BF),
            pltpu.SemaphoreType.DMA((load_count((0, 1), shapes),)),
        ],
        compiler_params=room(12),
        cost_estimate=pl.CostEstimate(
            flops=2 * rows * heads * (nope + rope) * ql + 2 * rows * heads * nope * lat,
            bytes_accessed=6000000, transcendentals=0,
        ),
        name="queries",
    )(where, qg, query_up, absorb_key, packed)

    n = nzh * qrows
    sums = pl.pallas_call(
        functools.partial(
            attend_kernel, rows=rows, lat=lat, scale=(nope + rope) ** -0.5,
            nch=nch, chips=nzh * nzl, qrows=qrows, part=part, shapes=shapes,
        ),
        out_shape=[jax.ShapeDtypeStruct((r, width), BF) for r in (n, n, n, n // 2, n // 2)],
        in_specs=[smem] + [vm] * 3 + [hbm] * 3,
        out_specs=[vm] * 5,
        scratch_shapes=[
            pltpu.VMEM((heads, rows, nch * block_len), F32),
            pltpu.VMEM((heads, rows, 128), F32),
            pltpu.VMEM((heads, rows, 128), F32),
            pltpu.VMEM((heads, rows, lat), F32),
            pltpu.VMEM((rows, heads * vh), BF),
            pltpu.VMEM((2,) + absorb_value.shape, BF),
            pltpu.VMEM((2,) + out_proj.shape, BF),
            pltpu.SemaphoreType.DMA((load_count((2, 3), shapes),)),
        ],
        compiler_params=room(28),
        cost_estimate=pl.CostEstimate(
            flops=4 * rows * heads * nch * block_len * lat, bytes_accessed=9000000,
            transcendentals=rows * heads * nch * block_len,
        ),
        name="attend",
    )(where, q, mine, other, absorb_value, out_proj, packed)

    up = shift_z(sums[1], 1)
    down = shift_z(sums[2], -1)
    up2 = shift_z(sums[3], 2)
    down2 = shift_z(sums[4], -2)
    cut = width // 2

    def near(e, up, down):
        at = slice((e + 1) * qrows, (e + 2) * qrows)
        return sums[0][at].astype(F32) + up[at].astype(F32) + down[at].astype(F32)

    far = near(2, up, down).astype(BF)
    far, up, down = lax.optimization_barrier((far, up, down))
    left = shift_z(far[:, :cut], nzl).astype(F32)
    right = shift_z(far[:, cut:], -nzl).astype(F32)
    ahead = near(1, up, down) + up2[qrows:].astype(F32)
    ahead = jnp.concatenate([ahead[:, :cut] + left, ahead[:, cut:]], -1)
    ahead = shift_z(ahead.astype(BF), nzl)
    behind = near(-1, up, down) + down2[:qrows].astype(F32)
    behind = jnp.concatenate([behind[:, :cut], behind[:, cut:] + right], -1)
    behind = shift_z(behind.astype(BF), -nzl)
    total = near(0, up, down) + up2[:qrows].astype(F32) + down2[qrows:].astype(F32)
    total = total + ahead.astype(F32) + behind.astype(F32)
    layer_output = total.astype(BF)[None]

    page = lax.optimization_barrier((keys, up))[0]
    page = pl.pallas_call(
        functools.partial(page_kernel, lat=lat, part=part, slots=slots),
        out_shape=jax.ShapeDtypeStruct((lax.axis_size("dec"),) + keys.shape, BF),
        in_specs=[smem, smem, vm],
        out_specs=vm,
        compiler_params=room(4),
        name="pages",
    )(page_owner, page_slot, page)
    page = lax.all_to_all(page, "dec", 0, 0, tiled=True).reshape(-1, pages, part, kw)
    came = page[:, :, 0, lat + rope].reshape(-1).astype(jnp.int32)
    take = (came[None, :] == dec * slots + jnp.arange(slots, dtype=jnp.int32)[:, None]).astype(BF)
    placed = jnp.einsum(
        "sp,pjc->sjc", take, page.reshape(-1, part, page.shape[-1]), preferred_element_type=F32
    ).astype(BF)
    cache_latent = placed[..., :lat][None, None]
    cache_rope = placed[..., lat : lat + rope][None, None]
    return (layer_output, cache_latent, cache_rope)


def solution(mesh):
    shape = mesh.shape
    chips = shape["tp"] // 2
    nzl = 4
    fine = Mesh(
        np.asarray(mesh.devices).reshape(shape["chain"], chips // nzl, nzl, 2, shape["dec"]),
        ("chain", "zh", "zl", "core", "dec"),
    )
    row = ("chain",) + TP
    return jax.shard_map(
        local,
        mesh=fine,
        in_specs=(
            P("dec", row, None),
            P("dec", "chain", TP, None),
            P("dec", "chain", TP, None),
            P(),
            P(None, TP),
            P(TP, None, None),
            P(TP, None, None),
            P(TP, None),
            P("dec", "chain"),
            P("dec", "chain"),
        ),
        out_specs=(
            P("dec", row, None),
            P("dec", "chain", None, TP, None),
            P("dec", "chain", None, TP, None),
        ),
        check_vma=False,
    )
```

```python
import functools

import jax
import jax.numpy as jnp
import numpy as np
from jax import lax
from jax.experimental import pallas as pl
from jax.experimental.pallas import tpu as pltpu
from jax.sharding import Mesh, PartitionSpec as P

BF = jnp.bfloat16
F32 = jnp.float32
LOG2E = 1.4426950408889634
Z = ("zh", "zl")
TP = ("zh", "zl", "core")
NEG = -1e30
STEPS = [4 * e + d for d in (0, 1, -1) for e in (-1, 0, 1, 2)] + [2, 6, -6, -2]


def swap_halves(v):
    half = v.shape[-1] // 2
    return jnp.concatenate([v[..., half:], v[..., :half]], -1)


def shift_z(x, step):
    n = lax.axis_size("zh") * lax.axis_size("zl")
    return lax.ppermute(x, Z, [(i, (i + step) % n) for i in range(n)])


def swap_core(x):
    return lax.ppermute(x, "core", [(0, 1), (1, 0)])


def spread(x, axis):
    n = lax.axis_size(axis)
    return lax.all_to_all(jnp.broadcast_to(x[None], (n,) + x.shape), axis, 0, 0, tiled=True)


def frequencies(width):
    half = width // 2
    lane = lax.broadcasted_iota(jnp.int32, (1, width), 1)
    out = jnp.ones((1, width), F32)
    for i in range(1, half):
        out = jnp.where(lane % half == i, np.float32(10000.0 ** (-2.0 * i / width)), out)
    return out


def rope_factors(where_at):
    width = where_at.shape[1]
    angle = where_at.astype(F32) * frequencies(width)
    lane = lax.broadcasted_iota(jnp.int32, where_at.shape, 1)
    sine = jnp.sin(angle)
    return jnp.cos(angle), jnp.where(lane < width // 2, -sine, sine)


def page_kernel(owner_ref, slot_ref, key_ref, out_ref, *, lat, part, slots):
    tail = key_ref[:, lat:].astype(F32)
    row = lax.broadcasted_iota(jnp.int32, tail.shape, 0)
    lane = lax.broadcasted_iota(jnp.int32, tail.shape, 1)
    code = jnp.zeros(tail.shape, F32)
    for p in range(tail.shape[0] // part):
        here = (owner_ref[0, p] * slots + slot_ref[0, p]).astype(F32)
        code = jnp.where(row // part == p, here, code)
    tail = jnp.where(lane < tail.shape[1] // 2, tail, code).astype(BF)
    for i in range(out_ref.shape[0]):
        out_ref[i, :, :lat] = key_ref[:, :lat]
        out_ref[i, :, lat:] = tail


def blocks(shapes):
    at = 0
    for w, shape in enumerate(shapes):
        for lead in range(int(np.prod(shape[:-2]))):
            for c in range(0, shape[-1], 128):
                yield at, w, lead, c, shape[-2]
                at += shape[-2]


def packed_rows(shapes):
    return sum(int(np.prod(shape)) for shape in shapes) // 128


def block_of(ref, lead, c):
    if len(ref.shape) == 3:
        return ref.at[lead, :, pl.ds(c, 128)]
    return ref.at[:, pl.ds(c, 128)]


def key_kernel(base_ref, x_ref, gain_ref, *refs, lat, part, page_len, shapes):
    ins, out_ref, packed, sems = refs[: len(shapes)], refs[-3], refs[-2], refs[-1]
    loads = [
        pltpu.make_async_copy(block_of(ins[w], lead, c), packed.at[pl.ds(at, n), :], sems.at[i])
        for i, (at, w, lead, c, n) in enumerate(blocks(shapes))
    ]
    for load in loads:
        load.start()
    x = x_ref[...].astype(F32)
    latent, rot = x[:, :lat], x[:, lat:]
    norm = lax.rsqrt(jnp.mean(latent * latent, -1, keepdims=True) + 1e-06)
    out_ref[:, :lat] = (latent * norm * gain_ref[...]).astype(BF)
    row = lax.broadcasted_iota(jnp.int32, rot.shape, 0)
    cosine, sine = rope_factors(base_ref[0] + row // part * page_len + row % part)
    turned = rot * cosine + swap_halves(rot) * sine
    out_ref[:, lat:] = jnp.concatenate([turned, jnp.zeros_like(turned)], -1).astype(BF)
    for load in loads:
        load.wait()


def weight_loads(own, packed, dst, which, shapes, sems):
    loads = [(src, d.at[0]) for src, d in zip(own, dst)]
    for at, w, lead, c, n in blocks(shapes):
        if w in which:
            to = block_of(dst[which.index(w)].at[1], lead, c)
            loads.append((packed.at[pl.ds(at, n), :], to))
    return [pltpu.make_async_copy(src, to, sems.at[i]) for i, (src, to) in enumerate(loads)]


def load_count(which, shapes):
    return len(which) + sum(1 for b in blocks(shapes) if b[1] in which)


def query_where(idx, z, core, qrows, chips):
    blk = idx // qrows
    off = jnp.zeros_like(idx)
    for i, step in enumerate(STEPS):
        off = jnp.where(blk == i, step % chips, off)
    return lax.rem(z + off, chips) * (2 * qrows) + core * qrows + idx % qrows


def query_kernel(
    where_ref, g_ref, wq0, ak0, packed, out_ref, x_ref, wq_ref, ak_ref, sems,
    *, nope, rope, qrows, chips, shapes,
):
    loads = weight_loads((wq0, ak0), packed, (wq_ref, ak_ref), (0, 1), shapes, sems)
    for load in loads:
        load.start()
    chain, z, core = where_ref[0], where_ref[1], where_ref[2]
    for i, step in enumerate(STEPS):
        at = lax.rem(z + step % chips, chips)
        x_ref[i * qrows : (i + 1) * qrows, :] = g_ref[pl.ds(pl.multiple_of(at * qrows, qrows), qrows), :]
    x = x_ref[...]
    rows = x.shape[0]
    lat = ak_ref.shape[-1]
    idx = lax.broadcasted_iota(jnp.int32, (rows, rope), 0)
    place = chain * (chips * 2 * qrows) + query_where(idx, z, core, qrows, chips)
    cosine, sine = rope_factors(place)
    head = 0
    for load in loads:
        load.wait()
    for side in range(2):
        ak = ak_ref.at[side]
        q = jnp.dot(x, wq_ref[side], preferred_element_type=F32).astype(BF)
        for h in range(ak.shape[0]):
            base = h * (nope + rope)
            r0 = head * rows
            out_ref[r0 : r0 + rows, :lat] = jnp.dot(
                q[:, base : base + nope], ak[h], preferred_element_type=F32
            ).astype(BF)
            rot = q[:, base + nope : base + nope + rope].astype(F32)
            turned = rot * cosine + swap_halves(rot) * sine
            out_ref[r0 : r0 + rows, lat:] = jnp.concatenate(
                [turned, jnp.zeros_like(turned)], -1
            ).astype(BF)
            head += 1


def attend_kernel(
    where_ref, q_ref, ka_ref, kb_ref, av0, op0, packed, o0, o1, o2, o3, o4,
    s_ref, top_ref, l_ref, acc_ref, ho_ref, av_ref, op_ref, sems, *, rows, lat, scale, nch, chips, qrows, part, shapes,
):
    chain, z, core = where_ref[0], where_ref[1], where_ref[2]
    s2 = scale * LOG2E
    loads = weight_loads((av0, op0), packed, (av_ref, op_ref), (2, 3), shapes, sems)
    for load in loads:
        load.start()
    vh = av_ref.shape[-1]
    heads = q_ref.shape[0] // rows
    n = ka_ref.shape[0] // nch
    nt = (((1,), (1,)), ((), ()))

    def lanes(x, op):
        out = x[:, :128]
        for c in range(128, x.shape[1], 128):
            out = op(out, x[:, c : c + 128])
        return out

    def block(back):
        return pl.ds(pl.multiple_of(jnp.maximum(chain - back, 0) * n, n), n)

    def score(back):
        if back == 0:
            idx = lax.broadcasted_iota(jnp.int32, (rows, 1), 0)
            qpos = query_where(idx, z, core, qrows, chips)
            idx = lax.broadcasted_iota(jnp.int32, (1, n), 1)
            kpos = (idx % qrows) // part * (chips * 2 * part) + idx // qrows * (2 * part) + idx % part
            ok = [kpos + i * part <= qpos for i in (core, 1 - core)]
        for h in range(heads):
            q = q_ref[h * rows : (h + 1) * rows, :]
            for i, k_ref in enumerate((ka_ref, kb_ref)):
                s = lax.dot_general(q, k_ref[block(back), :], nt, preferred_element_type=F32)
                if back == 0:
                    s = jnp.where(ok[i], s, NEG)
                at = (2 * back + i) * n
                s_ref[h, :, at : at + n] = s
                top = lanes(s, jnp.maximum)
                if back or i:
                    top = jnp.maximum(top, top_ref[h])
                top_ref[h] = top

    def mix(back):
        for h in range(heads):
            m = top_ref[h][:, :1]
            pv = None
            for i, k_ref in enumerate((ka_ref, kb_ref)):
                at = (2 * back + i) * n
                p = jnp.exp2(s_ref[h, :, at : at + n] * s2 - m)
                total = lanes(p, jnp.add)
                if back or i:
                    total += l_ref[h]
                l_ref[h] = total
                part_pv = jnp.dot(
                    p.astype(BF), k_ref[block(back), :lat], preferred_element_type=F32
                )
                pv = part_pv if pv is None else pv + part_pv
            acc_ref[h] = acc_ref[h] + pv if back else pv

    score(0)
    for back in range(1, nch):
        pl.when(chain >= back)(functools.partial(score, back))
    for h in range(heads):
        m = jnp.max(top_ref[h], -1, keepdims=True) * s2
        top_ref[h] = jnp.broadcast_to(m, top_ref.shape[1:])
    mix(0)
    for back in range(1, nch):
        pl.when(chain >= back)(functools.partial(mix, back))
    for load in loads:
        load.wait()
    per = heads // 2
    for h in range(heads):
        total = jnp.sum(l_ref[h], -1, keepdims=True)
        mixed = (acc_ref[h] / total).astype(BF)
        av = av_ref[h // per, h % per]
        ho_ref[:, h * vh : (h + 1) * vh] = jnp.dot(mixed, av, preferred_element_type=F32).astype(BF)
    ho = ho_ref[...]
    k, width = op_ref.shape[1:]
    cut = 512 if width % 512 == 0 else width
    for c in range(0, width, cut):
        part_out = (
            jnp.dot(ho[:, :k], op_ref[0, :, c : c + cut], preferred_element_type=F32)
            + jnp.dot(ho[:, k:], op_ref[1, :, c : c + cut], preferred_element_type=F32)
        ).astype(BF)
        at = 0
        for out_ref in (o0, o1, o2, o3, o4):
            out_ref[:, c : c + cut] = part_out[at : at + out_ref.shape[0]]
            at += out_ref.shape[0]


def local(
    query_comp, latent_rows, rope_keys, latent_gain, query_up, absorb_key, absorb_value, out_proj,
    page_owner, page_slot,
):
    nzh, nzl, nch = lax.axis_size("zh"), lax.axis_size("zl"), lax.axis_size("chain")
    zh, zl, core = lax.axis_index("zh"), lax.axis_index("zl"), lax.axis_index("core")
    chain, dec = lax.axis_index("chain"), lax.axis_index("dec")
    pages, part, lat = latent_rows.shape[1:]
    rope = rope_keys.shape[3]
    heads_here, nope = absorb_key.shape[:2]
    vh = absorb_value.shape[2]
    qrows, ql = query_comp.shape[1:]
    width = out_proj.shape[1]
    tp_index = (zh * nzl + zl) * 2 + core
    tp_count = nzh * nzl * 2
    block_len = qrows * tp_count
    slots = 2 * pages
    smem = pl.BlockSpec(memory_space=pltpu.SMEM)
    vm = pl.BlockSpec(memory_space=pltpu.VMEM)
    hbm = pl.BlockSpec(memory_space=pltpu.HBM)

    def room(mib):
        return pltpu.CompilerParams(vmem_limit_bytes=mib * 1024 * 1024)

    raw = jnp.concatenate(
        [latent_rows[0].reshape(pages * part, lat), rope_keys[0].reshape(pages * part, rope)], -1
    )
    rows = qrows * nzh * nzl
    kw = lat + 2 * rope
    heads = 2 * heads_here
    z = zh * nzl + zl
    where = jnp.stack([chain, z, core]).astype(jnp.int32)
    weights = (query_up, absorb_key, absorb_value, out_proj)
    shapes = tuple(w.shape for w in weights)
    count = len(list(blocks(shapes)))
    keys, packed = pl.pallas_call(
        functools.partial(
            key_kernel, lat=lat, part=part, page_len=part * tp_count, shapes=shapes
        ),
        out_shape=(
            jax.ShapeDtypeStruct((pages * part, kw), BF),
            jax.ShapeDtypeStruct((packed_rows(shapes), 128), BF),
        ),
        in_specs=[smem, vm, vm] + [hbm] * 4,
        out_specs=(vm, hbm),
        scratch_shapes=[pltpu.SemaphoreType.DMA((count,))],
        compiler_params=room(56),
        name="keys",
    )(
        (chain * block_len + tp_index * part).astype(jnp.int32)[None], raw, latent_gain[None],
        *weights,
    )
    packed = swap_core(packed)

    own = lax.all_gather(keys, Z, axis=0, tiled=True)
    mine = spread(own, "chain").reshape(nch * rows, kw)
    held = lax.optimization_barrier((query_comp[0], own))[0]
    qg = lax.all_gather(held, Z, axis=0, tiled=True)
    page = lax.optimization_barrier((keys, own))[0]
    page = pl.pallas_call(
        functools.partial(page_kernel, lat=lat, part=part, slots=slots),
        out_shape=jax.ShapeDtypeStruct((lax.axis_size("dec"),) + keys.shape, BF),
        in_specs=[smem, smem, vm],
        out_specs=vm,
        compiler_params=room(4),
        name="pages",
    )(page_owner, page_slot, page)
    page = lax.all_to_all(page, "dec", 0, 0, tiled=True).reshape(-1, pages, part, kw)
    qg, mine, page = lax.optimization_barrier((qg, mine, page))
    other = swap_core(mine)

    q = pl.pallas_call(
        functools.partial(query_kernel, nope=nope, rope=rope, qrows=qrows, chips=nzh * nzl, shapes=shapes),
        out_shape=jax.ShapeDtypeStruct((heads * rows, kw), BF),
        in_specs=[smem, vm] + [hbm] * 3,
        out_specs=vm,
        scratch_shapes=[
            pltpu.VMEM((rows, ql), BF),
            pltpu.VMEM((2,) + query_up.shape, BF),
            pltpu.VMEM((2,) + absorb_key.shape, BF),
            pltpu.SemaphoreType.DMA((load_count((0, 1), shapes),)),
        ],
        compiler_params=room(12),
        cost_estimate=pl.CostEstimate(
            flops=2 * rows * heads * (nope + rope) * ql + 2 * rows * heads * nope * lat,
            bytes_accessed=6000000, transcendentals=0,
        ),
        name="queries",
    )(where, qg, query_up, absorb_key, packed)

    n = nzh * qrows
    sums = pl.pallas_call(
        functools.partial(
            attend_kernel, rows=rows, lat=lat, scale=(nope + rope) ** -0.5,
            nch=nch, chips=nzh * nzl, qrows=qrows, part=part, shapes=shapes,
        ),
        out_shape=[jax.ShapeDtypeStruct((r, width), BF) for r in (n, n, n, n // 2, n // 2)],
        in_specs=[smem] + [vm] * 3 + [hbm] * 3,
        out_specs=[vm] * 5,
        scratch_shapes=[
            pltpu.VMEM((heads, rows, nch * block_len), F32),
            pltpu.VMEM((heads, rows, 128), F32),
            pltpu.VMEM((heads, rows, 128), F32),
            pltpu.VMEM((heads, rows, lat), F32),
            pltpu.VMEM((rows, heads * vh), BF),
            pltpu.VMEM((2,) + absorb_value.shape, BF),
            pltpu.VMEM((2,) + out_proj.shape, BF),
            pltpu.SemaphoreType.DMA((load_count((2, 3), shapes),)),
        ],
        compiler_params=room(28),
        cost_estimate=pl.CostEstimate(
            flops=4 * rows * heads * nch * block_len * lat, bytes_accessed=9000000,
            transcendentals=rows * heads * nch * block_len,
        ),
        name="attend",
    )(where, q, mine, other, absorb_value, out_proj, packed)

    up = shift_z(sums[1], 1)
    down = shift_z(sums[2], -1)
    up2 = shift_z(sums[3], 2)
    down2 = shift_z(sums[4], -2)
    cut = width // 2

    def near(e, up, down):
        at = slice((e + 1) * qrows, (e + 2) * qrows)
        return sums[0][at].astype(F32) + up[at].astype(F32) + down[at].astype(F32)

    far = near(2, up, down).astype(BF)
    far, up, down = lax.optimization_barrier((far, up, down))
    left = shift_z(far[:, :cut], nzl).astype(F32)
    right = shift_z(far[:, cut:], -nzl).astype(F32)
    ahead = near(1, up, down) + up2[qrows:].astype(F32)
    ahead = jnp.concatenate([ahead[:, :cut] + left, ahead[:, cut:]], -1)
    ahead = shift_z(ahead.astype(BF), nzl)
    behind = near(-1, up, down) + down2[:qrows].astype(F32)
    behind = jnp.concatenate([behind[:, :cut], behind[:, cut:] + right], -1)
    behind = shift_z(behind.astype(BF), -nzl)
    total = near(0, up, down) + up2[:qrows].astype(F32) + down2[qrows:].astype(F32)
    total = total + ahead.astype(F32) + behind.astype(F32)
    layer_output = total.astype(BF)[None]

    came = page[:, :, 0, lat + rope].reshape(-1).astype(jnp.int32)
    take = (came[None, :] == dec * slots + jnp.arange(slots, dtype=jnp.int32)[:, None]).astype(BF)
    placed = jnp.einsum(
        "sp,pjc->sjc", take, page.reshape(-1, part, page.shape[-1]), preferred_element_type=F32
    ).astype(BF)
    cache_latent = placed[..., :lat][None, None]
    cache_rope = placed[..., lat : lat + rope][None, None]
    return (layer_output, cache_latent, cache_rope)


def solution(mesh):
    shape = mesh.shape
    chips = shape["tp"] // 2
    nzl = 4
    fine = Mesh(
        np.asarray(mesh.devices).reshape(shape["chain"], chips // nzl, nzl, 2, shape["dec"]),
        ("chain", "zh", "zl", "core", "dec"),
    )
    row = ("chain",) + TP
    return jax.shard_map(
        local,
        mesh=fine,
        in_specs=(
            P("dec", row, None),
            P("dec", "chain", TP, None),
            P("dec", "chain", TP, None),
            P(),
            P(None, TP),
            P(TP, None, None),
            P(TP, None, None),
            P(TP, None),
            P("dec", "chain"),
            P("dec", "chain"),
        ),
        out_specs=(
            P("dec", row, None),
            P("dec", "chain", None, TP, None),
            P("dec", "chain", None, TP, None),
        ),
        check_vma=False,
    )
```

```python
import functools

import jax
import jax.numpy as jnp
import numpy as np
from jax import lax
from jax.experimental import pallas as pl
from jax.experimental.pallas import tpu as pltpu
from jax.sharding import Mesh, PartitionSpec as P

BF = jnp.bfloat16
F32 = jnp.float32
LOG2E = 1.4426950408889634
Z = ("zh", "zl")
TP = ("zh", "zl", "core")
NEG = -1e30
STEPS = [4 * e + d for d in (0, 1, -1) for e in (-1, 0, 1, 2)] + [2, 6, -6, -2]


def swap_halves(v):
    half = v.shape[-1] // 2
    return jnp.concatenate([v[..., half:], v[..., :half]], -1)


def shift_z(x, step):
    n = lax.axis_size("zh") * lax.axis_size("zl")
    return lax.ppermute(x, Z, [(i, (i + step) % n) for i in range(n)])


def swap_core(x):
    return lax.ppermute(x, "core", [(0, 1), (1, 0)])


def spread(x, axis):
    n = lax.axis_size(axis)
    return lax.all_to_all(jnp.broadcast_to(x[None], (n,) + x.shape), axis, 0, 0, tiled=True)


def frequencies(width):
    half = width // 2
    lane = lax.broadcasted_iota(jnp.int32, (1, width), 1)
    out = jnp.ones((1, width), F32)
    for i in range(1, half):
        out = jnp.where(lane % half == i, np.float32(10000.0 ** (-2.0 * i / width)), out)
    return out


def rope_factors(where_at):
    width = where_at.shape[1]
    angle = where_at.astype(F32) * frequencies(width)
    lane = lax.broadcasted_iota(jnp.int32, where_at.shape, 1)
    sine = jnp.sin(angle)
    return jnp.cos(angle), jnp.where(lane < width // 2, -sine, sine)


def page_kernel(owner_ref, slot_ref, key_ref, out_ref, *, lat, part, slots):
    tail = key_ref[:, lat:].astype(F32)
    row = lax.broadcasted_iota(jnp.int32, tail.shape, 0)
    lane = lax.broadcasted_iota(jnp.int32, tail.shape, 1)
    code = jnp.zeros(tail.shape, F32)
    for p in range(tail.shape[0] // part):
        here = (owner_ref[0, p] * slots + slot_ref[0, p]).astype(F32)
        code = jnp.where(row // part == p, here, code)
    tail = jnp.where(lane < tail.shape[1] // 2, tail, code).astype(BF)
    for i in range(out_ref.shape[0]):
        out_ref[i, :, :lat] = key_ref[:, :lat]
        out_ref[i, :, lat:] = tail


def blocks(shapes):
    at = 0
    for w, shape in enumerate(shapes):
        for lead in range(int(np.prod(shape[:-2]))):
            for c in range(0, shape[-1], 128):
                yield at, w, lead, c, shape[-2]
                at += shape[-2]


def packed_rows(shapes):
    return sum(int(np.prod(shape)) for shape in shapes) // 128


def block_of(ref, lead, c):
    if len(ref.shape) == 3:
        return ref.at[lead, :, pl.ds(c, 128)]
    return ref.at[:, pl.ds(c, 128)]


def key_kernel(base_ref, x_ref, gain_ref, *refs, lat, part, page_len, shapes):
    ins, out_ref, packed = refs[: len(shapes)], refs[-2], refs[-1]
    x = x_ref[...].astype(F32)
    latent, rot = x[:, :lat], x[:, lat:]
    norm = lax.rsqrt(jnp.mean(latent * latent, -1, keepdims=True) + 1e-06)
    out_ref[:, :lat] = (latent * norm * gain_ref[...]).astype(BF)
    row = lax.broadcasted_iota(jnp.int32, rot.shape, 0)
    cosine, sine = rope_factors(base_ref[0] + row // part * page_len + row % part)
    turned = rot * cosine + swap_halves(rot) * sine
    out_ref[:, lat:] = jnp.concatenate([turned, jnp.zeros_like(turned)], -1).astype(BF)
    for at, w, lead, c, n in blocks(shapes):
        src = ins[w]
        if len(src.shape) == 3:
            packed[at : at + n, :] = src[lead, :, c : c + 128]
        else:
            packed[at : at + n, :] = src[:, c : c + 128]


def weight_loads(own, packed, dst, which, shapes, sems):
    loads = [(src, d.at[0]) for src, d in zip(own, dst)]
    for at, w, lead, c, n in blocks(shapes):
        if w in which:
            to = block_of(dst[which.index(w)].at[1], lead, c)
            loads.append((packed.at[pl.ds(at, n), :], to))
    return [pltpu.make_async_copy(src, to, sems.at[i]) for i, (src, to) in enumerate(loads)]


def load_count(which, shapes):
    return len(which) + sum(1 for b in blocks(shapes) if b[1] in which)


def query_where(idx, z, core, qrows, chips):
    blk = idx // qrows
    off = jnp.zeros_like(idx)
    for i, step in enumerate(STEPS):
        off = jnp.where(blk == i, step % chips, off)
    return lax.rem(z + off, chips) * (2 * qrows) + core * qrows + idx % qrows


def query_kernel(
    where_ref, g_ref, wq0, ak0, packed, out_ref, x_ref, wq_ref, ak_ref, sems,
    *, nope, rope, qrows, chips, shapes,
):
    loads = weight_loads((wq0, ak0), packed, (wq_ref, ak_ref), (0, 1), shapes, sems)
    for load in loads:
        load.start()
    chain, z, core = where_ref[0], where_ref[1], where_ref[2]
    for i, step in enumerate(STEPS):
        at = lax.rem(z + step % chips, chips)
        x_ref[i * qrows : (i + 1) * qrows, :] = g_ref[pl.ds(pl.multiple_of(at * qrows, qrows), qrows), :]
    x = x_ref[...]
    rows = x.shape[0]
    lat = ak_ref.shape[-1]
    idx = lax.broadcasted_iota(jnp.int32, (rows, rope), 0)
    place = chain * (chips * 2 * qrows) + query_where(idx, z, core, qrows, chips)
    cosine, sine = rope_factors(place)
    head = 0
    for load in loads:
        load.wait()
    for side in range(2):
        ak = ak_ref.at[side]
        q = jnp.dot(x, wq_ref[side], preferred_element_type=F32).astype(BF)
        for h in range(ak.shape[0]):
            base = h * (nope + rope)
            r0 = head * rows
            out_ref[r0 : r0 + rows, :lat] = jnp.dot(
                q[:, base : base + nope], ak[h], preferred_element_type=F32
            ).astype(BF)
            rot = q[:, base + nope : base + nope + rope].astype(F32)
            turned = rot * cosine + swap_halves(rot) * sine
            out_ref[r0 : r0 + rows, lat:] = jnp.concatenate(
                [turned, jnp.zeros_like(turned)], -1
            ).astype(BF)
            head += 1


def attend_kernel(
    where_ref, q_ref, ka_ref, kb_ref, av0, op0, packed, o0, o1, o2, o3, o4,
    s_ref, top_ref, l_ref, acc_ref, ho_ref, av_ref, op_ref, sems, *, rows, lat, scale, nch, chips, qrows, part, shapes,
):
    chain, z, core = where_ref[0], where_ref[1], where_ref[2]
    s2 = scale * LOG2E
    loads = weight_loads((av0, op0), packed, (av_ref, op_ref), (2, 3), shapes, sems)
    for load in loads:
        load.start()
    vh = av_ref.shape[-1]
    heads = q_ref.shape[0] // rows
    n = ka_ref.shape[0] // nch
    nt = (((1,), (1,)), ((), ()))

    def lanes(x, op):
        out = x[:, :128]
        for c in range(128, x.shape[1], 128):
            out = op(out, x[:, c : c + 128])
        return out

    def block(back):
        return pl.ds(pl.multiple_of(jnp.maximum(chain - back, 0) * n, n), n)

    def score(back):
        if back == 0:
            idx = lax.broadcasted_iota(jnp.int32, (rows, 1), 0)
            qpos = query_where(idx, z, core, qrows, chips)
            idx = lax.broadcasted_iota(jnp.int32, (1, n), 1)
            kpos = (idx % qrows) // part * (chips * 2 * part) + idx // qrows * (2 * part) + idx % part
            ok = [kpos + i * part <= qpos for i in (core, 1 - core)]
        for i, k_ref in enumerate((ka_ref, kb_ref)):
            at = (2 * back + i) * n
            all_heads = lax.dot_general(
                q_ref[...], k_ref[block(back), :], nt, preferred_element_type=F32
            )
            for h in range(heads):
                s = all_heads[h * rows : (h + 1) * rows]
                if back == 0:
                    s = jnp.where(ok[i], s, NEG)
                s_ref[h * rows : (h + 1) * rows, at : at + n] = s
                top = lanes(s, jnp.maximum)
                if back or i:
                    top = jnp.maximum(top, top_ref[h * rows : (h + 1) * rows])
                top_ref[h * rows : (h + 1) * rows] = top

    def mix(back):
        m = top_ref[:, :1]
        for i, k_ref in enumerate((ka_ref, kb_ref)):
            at = (2 * back + i) * n
            p = jnp.exp2(s_ref[:, at : at + n] * s2 - m)
            total = lanes(p, jnp.add)
            l_ref[...] = total + l_ref[...] if back or i else total
            pv = jnp.dot(p.astype(BF), k_ref[block(back), :lat], preferred_element_type=F32)
            acc_ref[...] = acc_ref[...] + pv if back or i else pv

    score(0)
    for back in range(1, nch):
        pl.when(chain >= back)(functools.partial(score, back))
    top_ref[...] = jnp.broadcast_to(
        jnp.max(top_ref[...], -1, keepdims=True) * s2, top_ref.shape
    )
    mix(0)
    for back in range(1, nch):
        pl.when(chain >= back)(functools.partial(mix, back))
    for load in loads:
        load.wait()
    per = heads // 2
    for h in range(heads):
        at = slice(h * rows, (h + 1) * rows)
        total = jnp.sum(l_ref[at], -1, keepdims=True)
        mixed = (acc_ref[at] / total).astype(BF)
        av = av_ref[h // per, h % per]
        ho_ref[:, h * vh : (h + 1) * vh] = jnp.dot(mixed, av, preferred_element_type=F32).astype(BF)
    ho = ho_ref[...]
    k, width = op_ref.shape[1:]
    cut = 512 if width % 512 == 0 else width
    for c in range(0, width, cut):
        part_out = (
            jnp.dot(ho[:, :k], op_ref[0, :, c : c + cut], preferred_element_type=F32)
            + jnp.dot(ho[:, k:], op_ref[1, :, c : c + cut], preferred_element_type=F32)
        ).astype(BF)
        at = 0
        for out_ref in (o0, o1, o2, o3, o4):
            out_ref[:, c : c + cut] = part_out[at : at + out_ref.shape[0]]
            at += out_ref.shape[0]


def local(
    query_comp, latent_rows, rope_keys, latent_gain, query_up, absorb_key, absorb_value, out_proj,
    page_owner, page_slot,
):
    nzh, nzl, nch = lax.axis_size("zh"), lax.axis_size("zl"), lax.axis_size("chain")
    zh, zl, core = lax.axis_index("zh"), lax.axis_index("zl"), lax.axis_index("core")
    chain, dec = lax.axis_index("chain"), lax.axis_index("dec")
    pages, part, lat = latent_rows.shape[1:]
    rope = rope_keys.shape[3]
    heads_here, nope = absorb_key.shape[:2]
    vh = absorb_value.shape[2]
    qrows, ql = query_comp.shape[1:]
    width = out_proj.shape[1]
    tp_index = (zh * nzl + zl) * 2 + core
    tp_count = nzh * nzl * 2
    block_len = qrows * tp_count
    slots = 2 * pages
    smem = pl.BlockSpec(memory_space=pltpu.SMEM)
    vm = pl.BlockSpec(memory_space=pltpu.VMEM)
    hbm = pl.BlockSpec(memory_space=pltpu.HBM)

    def room(mib):
        return pltpu.CompilerParams(vmem_limit_bytes=mib * 1024 * 1024)

    raw = jnp.concatenate(
        [latent_rows[0].reshape(pages * part, lat), rope_keys[0].reshape(pages * part, rope)], -1
    )
    rows = qrows * nzh * nzl
    kw = lat + 2 * rope
    heads = 2 * heads_here
    z = zh * nzl + zl
    where = jnp.stack([chain, z, core]).astype(jnp.int32)
    weights = (query_up, absorb_key, absorb_value, out_proj)
    shapes = tuple(w.shape for w in weights)
    keys, packed = pl.pallas_call(
        functools.partial(
            key_kernel, lat=lat, part=part, page_len=part * tp_count, shapes=shapes
        ),
        out_shape=(
            jax.ShapeDtypeStruct((pages * part, kw), BF),
            jax.ShapeDtypeStruct((packed_rows(shapes), 128), BF),
        ),
        in_specs=[smem] + [vm] * 6,
        out_specs=(vm, vm),
        compiler_params=room(56),
        name="keys",
    )(
        (chain * block_len + tp_index * part).astype(jnp.int32)[None], raw, latent_gain[None],
        *weights,
    )
    packed = swap_core(packed)

    own = lax.all_gather(keys, Z, axis=0, tiled=True)
    mine = spread(own, "chain").reshape(nch * rows, kw)
    held = lax.optimization_barrier((query_comp[0], own))[0]
    qg = lax.all_gather(held, Z, axis=0, tiled=True)
    qg, mine = lax.optimization_barrier((qg, mine))
    other = swap_core(mine)

    q = pl.pallas_call(
        functools.partial(query_kernel, nope=nope, rope=rope, qrows=qrows, chips=nzh * nzl, shapes=shapes),
        out_shape=jax.ShapeDtypeStruct((heads * rows, kw), BF),
        in_specs=[smem, vm] + [hbm] * 3,
        out_specs=vm,
        scratch_shapes=[
            pltpu.VMEM((rows, ql), BF),
            pltpu.VMEM((2,) + query_up.shape, BF),
            pltpu.VMEM((2,) + absorb_key.shape, BF),
            pltpu.SemaphoreType.DMA((load_count((0, 1), shapes),)),
        ],
        compiler_params=room(12),
        cost_estimate=pl.CostEstimate(
            flops=2 * rows * heads * (nope + rope) * ql + 2 * rows * heads * nope * lat,
            bytes_accessed=6000000, transcendentals=0,
        ),
        name="queries",
    )(where, qg, query_up, absorb_key, packed)

    n = nzh * qrows
    sums = pl.pallas_call(
        functools.partial(
            attend_kernel, rows=rows, lat=lat, scale=(nope + rope) ** -0.5,
            nch=nch, chips=nzh * nzl, qrows=qrows, part=part, shapes=shapes,
        ),
        out_shape=[jax.ShapeDtypeStruct((r, width), BF) for r in (n, n, n, n // 2, n // 2)],
        in_specs=[smem] + [vm] * 3 + [hbm] * 3,
        out_specs=[vm] * 5,
        scratch_shapes=[
            pltpu.VMEM((heads * rows, nch * block_len), F32),
            pltpu.VMEM((heads * rows, 128), F32),
            pltpu.VMEM((heads * rows, 128), F32),
            pltpu.VMEM((heads * rows, lat), F32),
            pltpu.VMEM((rows, heads * vh), BF),
            pltpu.VMEM((2,) + absorb_value.shape, BF),
            pltpu.VMEM((2,) + out_proj.shape, BF),
            pltpu.SemaphoreType.DMA((load_count((2, 3), shapes),)),
        ],
        compiler_params=room(28),
        cost_estimate=pl.CostEstimate(
            flops=4 * rows * heads * nch * block_len * lat, bytes_accessed=9000000,
            transcendentals=rows * heads * nch * block_len,
        ),
        name="attend",
    )(where, q, mine, other, absorb_value, out_proj, packed)

    up = shift_z(sums[1], 1)
    down = shift_z(sums[2], -1)
    up2 = shift_z(sums[3], 2)
    down2 = shift_z(sums[4], -2)
    cut = width // 2

    def near(e, up, down):
        at = slice((e + 1) * qrows, (e + 2) * qrows)
        return sums[0][at].astype(F32) + up[at].astype(F32) + down[at].astype(F32)

    far = near(2, up, down).astype(BF)
    far, up, down = lax.optimization_barrier((far, up, down))
    left = shift_z(far[:, :cut], nzl).astype(F32)
    right = shift_z(far[:, cut:], -nzl).astype(F32)
    ahead = near(1, up, down) + up2[qrows:].astype(F32)
    ahead = jnp.concatenate([ahead[:, :cut] + left, ahead[:, cut:]], -1)
    ahead = ahead.astype(BF)
    behind = near(-1, up, down) + down2[:qrows].astype(F32)
    behind = jnp.concatenate([behind[:, :cut], behind[:, cut:] + right], -1)
    behind = behind.astype(BF)
    total = near(0, up, down) + up2[:qrows].astype(F32) + down2[qrows:].astype(F32)
    total = total + shift_z(ahead, nzl).astype(F32) + shift_z(behind, -nzl).astype(F32)
    layer_output = total.astype(BF)[None]

    page = lax.optimization_barrier((keys, ahead, behind))[0]
    page = pl.pallas_call(
        functools.partial(page_kernel, lat=lat, part=part, slots=slots),
        out_shape=jax.ShapeDtypeStruct((lax.axis_size("dec"),) + keys.shape, BF),
        in_specs=[smem, smem, vm],
        out_specs=vm,
        compiler_params=room(4),
        cost_estimate=pl.CostEstimate(flops=0, bytes_accessed=4000000, transcendentals=0),
        name="pages",
    )(page_owner, page_slot, page)
    page = lax.all_to_all(page, "dec", 0, 0, tiled=True).reshape(-1, pages, part, kw)
    came = page[:, :, 0, lat + rope].reshape(-1).astype(jnp.int32)
    take = (came[None, :] == dec * slots + jnp.arange(slots, dtype=jnp.int32)[:, None]).astype(BF)
    placed = jnp.einsum(
        "sp,pjc->sjc", take, page.reshape(-1, part, page.shape[-1]), preferred_element_type=F32
    ).astype(BF)
    cache_latent = placed[..., :lat][None, None]
    cache_rope = placed[..., lat : lat + rope][None, None]
    return (layer_output, cache_latent, cache_rope)


def solution(mesh):
    shape = mesh.shape
    chips = shape["tp"] // 2
    nzl = 4
    fine = Mesh(
        np.asarray(mesh.devices).reshape(shape["chain"], chips // nzl, nzl, 2, shape["dec"]),
        ("chain", "zh", "zl", "core", "dec"),
    )
    row = ("chain",) + TP
    return jax.shard_map(
        local,
        mesh=fine,
        in_specs=(
            P("dec", row, None),
            P("dec", "chain", TP, None),
            P("dec", "chain", TP, None),
            P(),
            P(None, TP),
            P(TP, None, None),
            P(TP, None, None),
            P(TP, None),
            P("dec", "chain"),
            P("dec", "chain"),
        ),
        out_specs=(
            P("dec", row, None),
            P("dec", "chain", None, TP, None),
            P("dec", "chain", None, TP, None),
        ),
        check_vma=False,
    )
```

```python
import functools

import jax
import jax.numpy as jnp
import numpy as np
from jax import lax
from jax.experimental import pallas as pl
from jax.experimental.pallas import tpu as pltpu
from jax.sharding import Mesh, PartitionSpec as P

BF = jnp.bfloat16
F32 = jnp.float32
LOG2E = 1.4426950408889634
Z = ("zh", "zl")
TP = ("zh", "zl", "core")
NEG = -1e30
STEPS = [4 * e + d for d in (0, 1, -1) for e in (-1, 0, 1, 2)] + [2, 6, -6, -2]


def swap_halves(v):
    half = v.shape[-1] // 2
    return jnp.concatenate([v[..., half:], v[..., :half]], -1)


def shift_z(x, step):
    n = lax.axis_size("zh") * lax.axis_size("zl")
    return lax.ppermute(x, Z, [(i, (i + step) % n) for i in range(n)])


def swap_core(x):
    return lax.ppermute(x, "core", [(0, 1), (1, 0)])


def spread(x, axis):
    n = lax.axis_size(axis)
    return lax.all_to_all(jnp.broadcast_to(x[None], (n,) + x.shape), axis, 0, 0, tiled=True)


def frequencies(width):
    half = width // 2
    lane = lax.broadcasted_iota(jnp.int32, (1, width), 1)
    out = jnp.ones((1, width), F32)
    for i in range(1, half):
        out = jnp.where(lane % half == i, np.float32(10000.0 ** (-2.0 * i / width)), out)
    return out


def rope_factors(where_at):
    width = where_at.shape[1]
    angle = where_at.astype(F32) * frequencies(width)
    lane = lax.broadcasted_iota(jnp.int32, where_at.shape, 1)
    sine = jnp.sin(angle)
    return jnp.cos(angle), jnp.where(lane < width // 2, -sine, sine)


def page_kernel(owner_ref, slot_ref, key_ref, out_ref, *, lat, part, slots):
    tail = key_ref[:, lat:].astype(F32)
    row = lax.broadcasted_iota(jnp.int32, tail.shape, 0)
    lane = lax.broadcasted_iota(jnp.int32, tail.shape, 1)
    code = jnp.zeros(tail.shape, F32)
    for p in range(tail.shape[0] // part):
        here = (owner_ref[0, p] * slots + slot_ref[0, p]).astype(F32)
        code = jnp.where(row // part == p, here, code)
    tail = jnp.where(lane < tail.shape[1] // 2, tail, code).astype(BF)
    for i in range(out_ref.shape[0]):
        out_ref[i, :, :lat] = key_ref[:, :lat]
        out_ref[i, :, lat:] = tail


def blocks(shapes):
    at = 0
    for w, shape in enumerate(shapes):
        for lead in range(int(np.prod(shape[:-2]))):
            for c in range(0, shape[-1], 128):
                yield at, w, lead, c, shape[-2]
                at += shape[-2]


def packed_rows(shapes):
    return sum(int(np.prod(shape)) for shape in shapes) // 128


def block_of(ref, lead, c):
    if len(ref.shape) == 3:
        return ref.at[lead, :, pl.ds(c, 128)]
    return ref.at[:, pl.ds(c, 128)]


def key_kernel(base_ref, x_ref, gain_ref, *refs, lat, part, page_len, shapes):
    ins, out_ref, packed = refs[: len(shapes)], refs[-2], refs[-1]
    x = x_ref[...].astype(F32)
    latent, rot = x[:, :lat], x[:, lat:]
    norm = lax.rsqrt(jnp.mean(latent * latent, -1, keepdims=True) + 1e-06)
    out_ref[:, :lat] = (latent * norm * gain_ref[...]).astype(BF)
    row = lax.broadcasted_iota(jnp.int32, rot.shape, 0)
    cosine, sine = rope_factors(base_ref[0] + row // part * page_len + row % part)
    turned = rot * cosine + swap_halves(rot) * sine
    out_ref[:, lat:] = jnp.concatenate([turned, jnp.zeros_like(turned)], -1).astype(BF)
    for at, w, lead, c, n in blocks(shapes):
        src = ins[w]
        if len(src.shape) == 3:
            packed[at : at + n, :] = src[lead, :, c : c + 128]
        else:
            packed[at : at + n, :] = src[:, c : c + 128]


def weight_loads(own, packed, dst, which, shapes, sems):
    loads = [(src, d.at[0]) for src, d in zip(own, dst)]
    for at, w, lead, c, n in blocks(shapes):
        if w in which:
            to = block_of(dst[which.index(w)].at[1], lead, c)
            loads.append((packed.at[pl.ds(at, n), :], to))
    return [pltpu.make_async_copy(src, to, sems.at[i]) for i, (src, to) in enumerate(loads)]


def load_count(which, shapes):
    return len(which) + sum(1 for b in blocks(shapes) if b[1] in which)


def query_where(idx, z, core, qrows, chips):
    blk = idx // qrows
    off = jnp.zeros_like(idx)
    for i, step in enumerate(STEPS):
        off = jnp.where(blk == i, step % chips, off)
    return lax.rem(z + off, chips) * (2 * qrows) + core * qrows + idx % qrows


def query_kernel(
    where_ref, g_ref, wq0, ak0, packed, out_ref, x_ref, wq_ref, ak_ref, sems,
    *, nope, rope, qrows, chips, shapes,
):
    loads = weight_loads((wq0, ak0), packed, (wq_ref, ak_ref), (0, 1), shapes, sems)
    for load in loads:
        load.start()
    chain, z, core = where_ref[0], where_ref[1], where_ref[2]
    for i, step in enumerate(STEPS):
        at = lax.rem(z + step % chips, chips)
        x_ref[i * qrows : (i + 1) * qrows, :] = g_ref[pl.ds(pl.multiple_of(at * qrows, qrows), qrows), :]
    x = x_ref[...]
    rows = x.shape[0]
    lat = ak_ref.shape[-1]
    idx = lax.broadcasted_iota(jnp.int32, (rows, rope), 0)
    place = chain * (chips * 2 * qrows) + query_where(idx, z, core, qrows, chips)
    cosine, sine = rope_factors(place)
    head = 0
    for load in loads:
        load.wait()
    for side in range(2):
        ak = ak_ref.at[side]
        q = jnp.dot(x, wq_ref[side], preferred_element_type=F32).astype(BF)
        for h in range(ak.shape[0]):
            base = h * (nope + rope)
            r0 = head * rows
            out_ref[r0 : r0 + rows, :lat] = jnp.dot(
                q[:, base : base + nope], ak[h], preferred_element_type=F32
            ).astype(BF)
            rot = q[:, base + nope : base + nope + rope].astype(F32)
            turned = rot * cosine + swap_halves(rot) * sine
            out_ref[r0 : r0 + rows, lat:] = jnp.concatenate(
                [turned, jnp.zeros_like(turned)], -1
            ).astype(BF)
            head += 1


def attend_kernel(
    where_ref, q_ref, ka_ref, kb_ref, av0, op0, packed, o0, o1, o2, o3, o4,
    acc_ref, ho_ref, av_ref, op_ref, sems, *, rows, lat, scale, nch, chips, qrows, part, shapes,
):
    chain, z, core = where_ref[0], where_ref[1], where_ref[2]
    s2 = scale * LOG2E
    loads = weight_loads((av0, op0), packed, (av_ref, op_ref), (2, 3), shapes, sems)
    for load in loads:
        load.start()
    vh = av_ref.shape[-1]
    heads = q_ref.shape[0] // rows
    n = ka_ref.shape[0] // nch
    nt = (((1,), (1,)), ((), ()))

    def attend(blocks_seen):
        count = blocks_seen * n
        idx = lax.broadcasted_iota(jnp.int32, (rows, 1), 0)
        qpos = query_where(idx, z, core, qrows, chips)
        idx = lax.broadcasted_iota(jnp.int32, (1, n), 1)
        kpos = (idx % qrows) // part * (chips * 2 * part) + idx // qrows * (2 * part) + idx % part
        ok = [kpos + i * part <= qpos for i in (core, 1 - core)]
        for h in range(heads):
            q = q_ref[h * rows : (h + 1) * rows, :]
            scores = []
            for i, k_ref in enumerate((ka_ref, kb_ref)):
                s = lax.dot_general(q, k_ref[:count, :], nt, preferred_element_type=F32)
                own = jnp.where(ok[i], s[:, count - n :], NEG)
                scores.append(own if count == n else jnp.concatenate([s[:, : count - n], own], -1))
            m = jnp.maximum(*[jnp.max(s, -1, keepdims=True) for s in scores]) * s2
            total, mixed = 0.0, 0.0
            for s, k_ref in zip(scores, (ka_ref, kb_ref)):
                p = jnp.exp2(s * s2 - m)
                total = total + jnp.sum(p, -1, keepdims=True)
                mixed = mixed + jnp.dot(p.astype(BF), k_ref[:count, :lat], preferred_element_type=F32)
            acc_ref[h * rows : (h + 1) * rows, :] = (mixed / total).astype(BF)

    for seen in range(1, nch + 1):
        pl.when(chain == seen - 1)(functools.partial(attend, seen))
    for load in loads:
        load.wait()
    per = heads // 2
    for h in range(heads):
        av = av_ref[h // per, h % per]
        ho_ref[:, h * vh : (h + 1) * vh] = jnp.dot(
            acc_ref[h * rows : (h + 1) * rows, :], av, preferred_element_type=F32
        ).astype(BF)
    ho = ho_ref[...]
    k, width = op_ref.shape[1:]
    cut = 512 if width % 512 == 0 else width
    for c in range(0, width, cut):
        part_out = (
            jnp.dot(ho[:, :k], op_ref[0, :, c : c + cut], preferred_element_type=F32)
            + jnp.dot(ho[:, k:], op_ref[1, :, c : c + cut], preferred_element_type=F32)
        ).astype(BF)
        at = 0
        for out_ref in (o0, o1, o2, o3, o4):
            out_ref[:, c : c + cut] = part_out[at : at + out_ref.shape[0]]
            at += out_ref.shape[0]


def local(
    query_comp, latent_rows, rope_keys, latent_gain, query_up, absorb_key, absorb_value, out_proj,
    page_owner, page_slot,
):
    nzh, nzl, nch = lax.axis_size("zh"), lax.axis_size("zl"), lax.axis_size("chain")
    zh, zl, core = lax.axis_index("zh"), lax.axis_index("zl"), lax.axis_index("core")
    chain, dec = lax.axis_index("chain"), lax.axis_index("dec")
    pages, part, lat = latent_rows.shape[1:]
    rope = rope_keys.shape[3]
    heads_here, nope = absorb_key.shape[:2]
    vh = absorb_value.shape[2]
    qrows, ql = query_comp.shape[1:]
    width = out_proj.shape[1]
    tp_index = (zh * nzl + zl) * 2 + core
    tp_count = nzh * nzl * 2
    block_len = qrows * tp_count
    slots = 2 * pages
    smem = pl.BlockSpec(memory_space=pltpu.SMEM)
    vm = pl.BlockSpec(memory_space=pltpu.VMEM)
    hbm = pl.BlockSpec(memory_space=pltpu.HBM)

    def room(mib):
        return pltpu.CompilerParams(vmem_limit_bytes=mib * 1024 * 1024)

    raw = jnp.concatenate(
        [latent_rows[0].reshape(pages * part, lat), rope_keys[0].reshape(pages * part, rope)], -1
    )
    rows = qrows * nzh * nzl
    kw = lat + 2 * rope
    heads = 2 * heads_here
    z = zh * nzl + zl
    where = jnp.stack([chain, z, core]).astype(jnp.int32)
    weights = (query_up, absorb_key, absorb_value, out_proj)
    shapes = tuple(w.shape for w in weights)
    keys, packed = pl.pallas_call(
        functools.partial(
            key_kernel, lat=lat, part=part, page_len=part * tp_count, shapes=shapes
        ),
        out_shape=(
            jax.ShapeDtypeStruct((pages * part, kw), BF),
            jax.ShapeDtypeStruct((packed_rows(shapes), 128), BF),
        ),
        in_specs=[smem] + [vm] * 6,
        out_specs=(vm, vm),
        compiler_params=room(56),
        name="keys",
    )(
        (chain * block_len + tp_index * part).astype(jnp.int32)[None], raw, latent_gain[None],
        *weights,
    )
    packed = swap_core(packed)

    own = lax.all_gather(keys, Z, axis=0, tiled=True)
    mine = spread(own, "chain").reshape(nch * rows, kw)
    held = lax.optimization_barrier((query_comp[0], own))[0]
    qg = lax.all_gather(held, Z, axis=0, tiled=True)
    qg, mine = lax.optimization_barrier((qg, mine))
    other = swap_core(mine)

    q = pl.pallas_call(
        functools.partial(query_kernel, nope=nope, rope=rope, qrows=qrows, chips=nzh * nzl, shapes=shapes),
        out_shape=jax.ShapeDtypeStruct((heads * rows, kw), BF),
        in_specs=[smem, vm] + [hbm] * 3,
        out_specs=vm,
        scratch_shapes=[
            pltpu.VMEM((rows, ql), BF),
            pltpu.VMEM((2,) + query_up.shape, BF),
            pltpu.VMEM((2,) + absorb_key.shape, BF),
            pltpu.SemaphoreType.DMA((load_count((0, 1), shapes),)),
        ],
        compiler_params=room(12),
        cost_estimate=pl.CostEstimate(
            flops=2 * rows * heads * (nope + rope) * ql + 2 * rows * heads * nope * lat,
            bytes_accessed=6000000, transcendentals=0,
        ),
        name="queries",
    )(where, qg, query_up, absorb_key, packed)

    n = nzh * qrows
    sums = pl.pallas_call(
        functools.partial(
            attend_kernel, rows=rows, lat=lat, scale=(nope + rope) ** -0.5,
            nch=nch, chips=nzh * nzl, qrows=qrows, part=part, shapes=shapes,
        ),
        out_shape=[jax.ShapeDtypeStruct((r, width), BF) for r in (n, n, n, n // 2, n // 2)],
        in_specs=[smem] + [vm] * 3 + [hbm] * 3,
        out_specs=[vm] * 5,
        scratch_shapes=[
            pltpu.VMEM((heads * rows, lat), BF),
            pltpu.VMEM((rows, heads * vh), BF),
            pltpu.VMEM((2,) + absorb_value.shape, BF),
            pltpu.VMEM((2,) + out_proj.shape, BF),
            pltpu.SemaphoreType.DMA((load_count((2, 3), shapes),)),
        ],
        compiler_params=room(28),
        cost_estimate=pl.CostEstimate(
            flops=4 * rows * heads * nch * block_len * lat, bytes_accessed=9000000,
            transcendentals=rows * heads * nch * block_len,
        ),
        name="attend",
    )(where, q, mine, other, absorb_value, out_proj, packed)

    up = shift_z(sums[1], 1)
    down = shift_z(sums[2], -1)
    up2 = shift_z(sums[3], 2)
    down2 = shift_z(sums[4], -2)
    cut = width // 2

    def near(e, up, down):
        at = slice((e + 1) * qrows, (e + 2) * qrows)
        return sums[0][at].astype(F32) + up[at].astype(F32) + down[at].astype(F32)

    far = near(2, up, down).astype(BF)
    far, up, down = lax.optimization_barrier((far, up, down))
    left = shift_z(far[:, :cut], nzl).astype(F32)
    right = shift_z(far[:, cut:], -nzl).astype(F32)
    ahead = near(1, up, down) + up2[qrows:].astype(F32)
    ahead = jnp.concatenate([ahead[:, :cut] + left, ahead[:, cut:]], -1)
    ahead = shift_z(ahead.astype(BF), nzl)
    behind = near(-1, up, down) + down2[:qrows].astype(F32)
    behind = jnp.concatenate([behind[:, :cut], behind[:, cut:] + right], -1)
    behind = shift_z(behind.astype(BF), -nzl)
    total = near(0, up, down) + up2[:qrows].astype(F32) + down2[qrows:].astype(F32)
    total = total + ahead.astype(F32) + behind.astype(F32)
    layer_output = total.astype(BF)[None]

    page = lax.optimization_barrier((keys, sums[0]))[0]
    page = pl.pallas_call(
        functools.partial(page_kernel, lat=lat, part=part, slots=slots),
        out_shape=jax.ShapeDtypeStruct((lax.axis_size("dec"),) + keys.shape, BF),
        in_specs=[smem, smem, vm],
        out_specs=vm,
        compiler_params=room(4),
        cost_estimate=pl.CostEstimate(flops=10**10, bytes_accessed=400000, transcendentals=0),
        name="pages",
    )(page_owner, page_slot, page)
    page = lax.all_to_all(page, "dec", 0, 0, tiled=True).reshape(-1, pages, part, kw)
    came = page[:, :, 0, lat + rope].reshape(-1).astype(jnp.int32)
    take = (came[None, :] == dec * slots + jnp.arange(slots, dtype=jnp.int32)[:, None]).astype(BF)
    placed = jnp.einsum(
        "sp,pjc->sjc", take, page.reshape(-1, part, page.shape[-1]), preferred_element_type=F32
    ).astype(BF)
    cache_latent = placed[..., :lat][None, None]
    cache_rope = placed[..., lat : lat + rope][None, None]
    return (layer_output, cache_latent, cache_rope)


def solution(mesh):
    shape = mesh.shape
    chips = shape["tp"] // 2
    nzl = 4
    fine = Mesh(
        np.asarray(mesh.devices).reshape(shape["chain"], chips // nzl, nzl, 2, shape["dec"]),
        ("chain", "zh", "zl", "core", "dec"),
    )
    row = ("chain",) + TP
    return jax.shard_map(
        local,
        mesh=fine,
        in_specs=(
            P("dec", row, None),
            P("dec", "chain", TP, None),
            P("dec", "chain", TP, None),
            P(),
            P(None, TP),
            P(TP, None, None),
            P(TP, None, None),
            P(TP, None),
            P("dec", "chain"),
            P("dec", "chain"),
        ),
        out_specs=(
            P("dec", row, None),
            P("dec", "chain", None, TP, None),
            P("dec", "chain", None, TP, None),
        ),
        check_vma=False,
    )
```

```python
import functools

import jax
import jax.numpy as jnp
import numpy as np
from jax import lax
from jax.experimental import pallas as pl
from jax.experimental.pallas import tpu as pltpu
from jax.sharding import Mesh, PartitionSpec as P

BF = jnp.bfloat16
F32 = jnp.float32
LOG2E = 1.4426950408889634
Z = ("zh", "zl")
TP = ("zh", "zl", "core")
NEG = -1e30
STEPS = [4 * e + d for d in (0, 1, -1) for e in (-1, 0, 1, 2)] + [2, 6, -6, -2]


def swap_halves(v):
    half = v.shape[-1] // 2
    return jnp.concatenate([v[..., half:], v[..., :half]], -1)


def shift_z(x, step):
    n = lax.axis_size("zh") * lax.axis_size("zl")
    return lax.ppermute(x, Z, [(i, (i + step) % n) for i in range(n)])


def swap_core(x):
    return lax.ppermute(x, "core", [(0, 1), (1, 0)])


def spread(x, axis):
    n = lax.axis_size(axis)
    return lax.all_to_all(jnp.broadcast_to(x[None], (n,) + x.shape), axis, 0, 0, tiled=True)


def frequencies(width):
    half = width // 2
    lane = lax.broadcasted_iota(jnp.int32, (1, width), 1)
    out = jnp.ones((1, width), F32)
    for i in range(1, half):
        out = jnp.where(lane % half == i, np.float32(10000.0 ** (-2.0 * i / width)), out)
    return out


def rope_factors(where_at):
    width = where_at.shape[1]
    angle = where_at.astype(F32) * frequencies(width)
    lane = lax.broadcasted_iota(jnp.int32, where_at.shape, 1)
    sine = jnp.sin(angle)
    return jnp.cos(angle), jnp.where(lane < width // 2, -sine, sine)


def blocks(shapes):
    at = 0
    for w, shape in enumerate(shapes):
        for lead in range(int(np.prod(shape[:-2]))):
            for c in range(0, shape[-1], 128):
                yield at, w, lead, c, shape[-2]
                at += shape[-2]


def packed_rows(shapes):
    return sum(int(np.prod(shape)) for shape in shapes) // 128


def block_of(ref, lead, c):
    if len(ref.shape) == 3:
        return ref.at[lead, :, pl.ds(c, 128)]
    return ref.at[:, pl.ds(c, 128)]


def key_kernel(
    where_ref, owner_ref, slot_ref, lat_ref, rope_ref, gain_ref, *refs, slots, page_len, shapes
):
    ins, out_ref, page_ref, packed = refs[: len(shapes)], refs[-3], refs[-2], refs[-1]
    pages, part, lat = lat_ref.shape[1:]
    latent = jnp.concatenate([lat_ref[0, p].astype(F32) for p in range(pages)], 0)
    rot = jnp.concatenate([rope_ref[0, p].astype(F32) for p in range(pages)], 0)
    norm = lax.rsqrt(jnp.mean(latent * latent, -1, keepdims=True) + 1e-06)
    normed = (latent * norm * gain_ref[...]).astype(BF)
    row = lax.broadcasted_iota(jnp.int32, rot.shape, 0)
    cosine, sine = rope_factors(where_ref[0] + row // part * page_len + row % part)
    turned = rot * cosine + swap_halves(rot) * sine
    code = jnp.zeros_like(turned)
    for p in range(pages):
        here = (owner_ref[0, p] * slots + slot_ref[0, p]).astype(F32)
        code = jnp.where(row // part == p, here, code)
    out_ref[:, :lat] = normed
    out_ref[:, lat:] = jnp.concatenate([turned, jnp.zeros_like(turned)], -1).astype(BF)
    tail = jnp.concatenate([turned, code], -1).astype(BF)
    for i in range(page_ref.shape[0]):
        page_ref[i, :, :lat] = normed
        page_ref[i, :, lat:] = tail
    for at, w, lead, c, n in blocks(shapes):
        src = ins[w]
        if len(src.shape) == 3:
            packed[at : at + n, :] = src[lead, :, c : c + 128]
        else:
            packed[at : at + n, :] = src[:, c : c + 128]


def weight_loads(own, packed, dst, which, shapes, sems):
    loads = [(src, d.at[0]) for src, d in zip(own, dst)]
    for at, w, lead, c, n in blocks(shapes):
        if w in which:
            to = block_of(dst[which.index(w)].at[1], lead, c)
            loads.append((packed.at[pl.ds(at, n), :], to))
    return [pltpu.make_async_copy(src, to, sems.at[i]) for i, (src, to) in enumerate(loads)]


def load_count(which, shapes):
    return len(which) + sum(1 for b in blocks(shapes) if b[1] in which)


def query_where(idx, z, core, qrows, chips):
    blk = idx // qrows
    off = jnp.zeros_like(idx)
    for i, step in enumerate(STEPS):
        off = jnp.where(blk == i, step % chips, off)
    return lax.rem(z + off, chips) * (2 * qrows) + core * qrows + idx % qrows


def query_kernel(
    where_ref, g_ref, wq0, ak0, packed, out_ref, x_ref, wq_ref, ak_ref, sems,
    *, nope, rope, qrows, chips, shapes,
):
    loads = weight_loads((wq0, ak0), packed, (wq_ref, ak_ref), (0, 1), shapes, sems)
    for load in loads:
        load.start()
    chain, z, core = where_ref[0], where_ref[1], where_ref[2]
    for i, step in enumerate(STEPS):
        at = lax.rem(z + step % chips, chips)
        x_ref[i * qrows : (i + 1) * qrows, :] = g_ref[pl.ds(pl.multiple_of(at * qrows, qrows), qrows), :]
    x = x_ref[...]
    rows = x.shape[0]
    lat = ak_ref.shape[-1]
    idx = lax.broadcasted_iota(jnp.int32, (rows, rope), 0)
    place = chain * (chips * 2 * qrows) + query_where(idx, z, core, qrows, chips)
    cosine, sine = rope_factors(place)
    head = 0
    for side in range(2):
        for load in loads[2:] if side else loads[:2]:
            load.wait()
        ak = ak_ref.at[side]
        q = jnp.dot(x, wq_ref[side], preferred_element_type=F32).astype(BF)
        for h in range(ak.shape[0]):
            base = h * (nope + rope)
            r0 = head * rows
            out_ref[r0 : r0 + rows, :lat] = jnp.dot(
                q[:, base : base + nope], ak[h], preferred_element_type=F32
            ).astype(BF)
            rot = q[:, base + nope : base + nope + rope].astype(F32)
            turned = rot * cosine + swap_halves(rot) * sine
            out_ref[r0 : r0 + rows, lat:] = jnp.concatenate(
                [turned, jnp.zeros_like(turned)], -1
            ).astype(BF)
            head += 1


def attend_kernel(
    where_ref, q_ref, ka_ref, kb_ref, av0, op0, packed, o0, o1, o2, o3, o4,
    acc_ref, ho_ref, av_ref, op_ref, sems, *, rows, lat, scale, nch, chips, qrows, part, shapes,
):
    chain, z, core = where_ref[0], where_ref[1], where_ref[2]
    s2 = scale * LOG2E
    loads = weight_loads((av0, op0), packed, (av_ref, op_ref), (2, 3), shapes, sems)
    for load in loads:
        load.start()
    vh = av_ref.shape[-1]
    heads = q_ref.shape[0] // rows
    n = ka_ref.shape[0] // nch
    nt = (((1,), (1,)), ((), ()))

    def attend(blocks_seen):
        count = blocks_seen * n
        idx = lax.broadcasted_iota(jnp.int32, (rows, 1), 0)
        qpos = query_where(idx, z, core, qrows, chips)
        idx = lax.broadcasted_iota(jnp.int32, (1, n), 1)
        kpos = (idx % qrows) // part * (chips * 2 * part) + idx // qrows * (2 * part) + idx % part
        ok = [kpos + i * part <= qpos for i in (core, 1 - core)]
        for h in range(heads):
            q = q_ref[h * rows : (h + 1) * rows, :]
            scores = []
            for i, k_ref in enumerate((ka_ref, kb_ref)):
                s = lax.dot_general(q, k_ref[:count, :], nt, preferred_element_type=F32)
                own = jnp.where(ok[i], s[:, count - n :], NEG)
                scores.append(own if count == n else jnp.concatenate([s[:, : count - n], own], -1))
            m = jnp.maximum(*[jnp.max(s, -1, keepdims=True) for s in scores]) * s2
            total, mixed = 0.0, 0.0
            for s, k_ref in zip(scores, (ka_ref, kb_ref)):
                p = jnp.exp2(s * s2 - m)
                total = total + jnp.sum(p, -1, keepdims=True)
                mixed = mixed + jnp.dot(p.astype(BF), k_ref[:count, :lat], preferred_element_type=F32)
            acc_ref[h * rows : (h + 1) * rows, :] = (mixed / total).astype(BF)

    for seen in range(1, nch + 1):
        pl.when(chain == seen - 1)(functools.partial(attend, seen))
    for load in loads:
        load.wait()
    per = heads // 2
    for h in range(heads):
        av = av_ref[h // per, h % per]
        ho_ref[:, h * vh : (h + 1) * vh] = jnp.dot(
            acc_ref[h * rows : (h + 1) * rows, :], av, preferred_element_type=F32
        ).astype(BF)
    ho = ho_ref[...]
    k, width = op_ref.shape[1:]
    cut = 512 if width % 512 == 0 else width
    for c in range(0, width, cut):
        part_out = (
            jnp.dot(ho[:, :k], op_ref[0, :, c : c + cut], preferred_element_type=F32)
            + jnp.dot(ho[:, k:], op_ref[1, :, c : c + cut], preferred_element_type=F32)
        ).astype(BF)
        at = 0
        for out_ref in (o0, o1, o2, o3, o4):
            out_ref[:, c : c + cut] = part_out[at : at + out_ref.shape[0]]
            at += out_ref.shape[0]


def local(
    query_comp, latent_rows, rope_keys, latent_gain, query_up, absorb_key, absorb_value, out_proj,
    page_owner, page_slot,
):
    nzh, nzl, nch = lax.axis_size("zh"), lax.axis_size("zl"), lax.axis_size("chain")
    zh, zl, core = lax.axis_index("zh"), lax.axis_index("zl"), lax.axis_index("core")
    chain, dec = lax.axis_index("chain"), lax.axis_index("dec")
    pages, part, lat = latent_rows.shape[1:]
    rope = rope_keys.shape[3]
    heads_here, nope = absorb_key.shape[:2]
    vh = absorb_value.shape[2]
    qrows, ql = query_comp.shape[1:]
    width = out_proj.shape[1]
    tp_index = (zh * nzl + zl) * 2 + core
    tp_count = nzh * nzl * 2
    block_len = qrows * tp_count
    slots = 2 * pages
    smem = pl.BlockSpec(memory_space=pltpu.SMEM)
    vm = pl.BlockSpec(memory_space=pltpu.VMEM)
    hbm = pl.BlockSpec(memory_space=pltpu.HBM)

    def room(mib):
        return pltpu.CompilerParams(vmem_limit_bytes=mib * 1024 * 1024)

    rows = qrows * nzh * nzl
    kw = lat + 2 * rope
    heads = 2 * heads_here
    z = zh * nzl + zl
    where = jnp.stack([chain, z, core]).astype(jnp.int32)
    weights = (query_up, absorb_key, absorb_value, out_proj)
    shapes = tuple(w.shape for w in weights)
    keys, page, packed = pl.pallas_call(
        functools.partial(key_kernel, slots=slots, page_len=part * tp_count, shapes=shapes),
        out_shape=(
            jax.ShapeDtypeStruct((pages * part, kw), BF),
            jax.ShapeDtypeStruct((lax.axis_size("dec"), pages * part, kw), BF),
            jax.ShapeDtypeStruct((packed_rows(shapes), 128), BF),
        ),
        in_specs=[smem] * 3 + [vm] * 7,
        out_specs=(vm, vm, vm),
        compiler_params=room(56),
        name="keys",
    )(
        (chain * block_len + tp_index * part).astype(jnp.int32)[None], page_owner, page_slot,
        latent_rows, rope_keys, latent_gain[None], *weights,
    )
    packed = swap_core(packed)

    own = lax.all_gather(keys, Z, axis=0, tiled=True)
    mine = spread(own, "chain").reshape(nch * rows, kw)
    held = lax.optimization_barrier((query_comp[0], own))[0]
    qg = lax.all_gather(held, Z, axis=0, tiled=True)
    qg, mine = lax.optimization_barrier((qg, mine))
    other = swap_core(mine)

    q = pl.pallas_call(
        functools.partial(query_kernel, nope=nope, rope=rope, qrows=qrows, chips=nzh * nzl, shapes=shapes),
        out_shape=jax.ShapeDtypeStruct((heads * rows, kw), BF),
        in_specs=[smem, vm] + [hbm] * 3,
        out_specs=vm,
        scratch_shapes=[
            pltpu.VMEM((rows, ql), BF),
            pltpu.VMEM((2,) + query_up.shape, BF),
            pltpu.VMEM((2,) + absorb_key.shape, BF),
            pltpu.SemaphoreType.DMA((load_count((0, 1), shapes),)),
        ],
        compiler_params=room(12),
        cost_estimate=pl.CostEstimate(
            flops=2 * rows * heads * (nope + rope) * ql + 2 * rows * heads * nope * lat,
            bytes_accessed=6000000, transcendentals=0,
        ),
        name="queries",
    )(where, qg, query_up, absorb_key, packed)

    n = nzh * qrows
    sums = pl.pallas_call(
        functools.partial(
            attend_kernel, rows=rows, lat=lat, scale=(nope + rope) ** -0.5,
            nch=nch, chips=nzh * nzl, qrows=qrows, part=part, shapes=shapes,
        ),
        out_shape=[jax.ShapeDtypeStruct((r, width), BF) for r in (n, n, n, n // 2, n // 2)],
        in_specs=[smem] + [vm] * 3 + [hbm] * 3,
        out_specs=[vm] * 5,
        scratch_shapes=[
            pltpu.VMEM((heads * rows, lat), BF),
            pltpu.VMEM((rows, heads * vh), BF),
            pltpu.VMEM((2,) + absorb_value.shape, BF),
            pltpu.VMEM((2,) + out_proj.shape, BF),
            pltpu.SemaphoreType.DMA((load_count((2, 3), shapes),)),
        ],
        compiler_params=room(28),
        cost_estimate=pl.CostEstimate(
            flops=4 * rows * heads * nch * block_len * lat, bytes_accessed=9000000,
            transcendentals=rows * heads * nch * block_len,
        ),
        name="attend",
    )(where, q, mine, other, absorb_value, out_proj, packed)

    up = shift_z(sums[1], 1)
    down = shift_z(sums[2], -1)
    up2 = shift_z(sums[3], 2)
    down2 = shift_z(sums[4], -2)
    cut = width // 2

    def near(e, up, down):
        at = slice((e + 1) * qrows, (e + 2) * qrows)
        return sums[0][at].astype(F32) + up[at].astype(F32) + down[at].astype(F32)

    far = near(2, up, down).astype(BF)
    far, up, down = lax.optimization_barrier((far, up, down))
    left, right = lax.optimization_barrier((shift_z(far[:, :cut], nzl), shift_z(far[:, cut:], -nzl)))
    ahead = near(1, up, down) + up2[qrows:].astype(F32)
    ahead = jnp.concatenate([ahead[:, :cut] + left.astype(F32), ahead[:, cut:]], -1)
    ahead = shift_z(ahead.astype(BF), nzl)
    behind = near(-1, up, down) + down2[:qrows].astype(F32)
    behind = jnp.concatenate([behind[:, :cut], behind[:, cut:] + right.astype(F32)], -1)
    behind = shift_z(behind.astype(BF), -nzl)
    total = near(0, up, down) + up2[:qrows].astype(F32) + down2[qrows:].astype(F32)
    total = total + ahead.astype(F32) + behind.astype(F32)
    layer_output = total.astype(BF)[None]

    page = lax.optimization_barrier((page, ahead))[0]
    page = lax.all_to_all(page, "dec", 0, 0, tiled=True).reshape(-1, pages, part, kw)
    came = page[:, :, 0, lat + rope].reshape(-1).astype(jnp.int32)
    take = (came[None, :] == dec * slots + jnp.arange(slots, dtype=jnp.int32)[:, None]).astype(BF)
    placed = jnp.einsum(
        "sp,pjc->sjc", take, page.reshape(-1, part, page.shape[-1]), preferred_element_type=F32
    ).astype(BF)
    cache_latent = placed[..., :lat][None, None]
    cache_rope = placed[..., lat : lat + rope][None, None]
    return (layer_output, cache_latent, cache_rope)


def solution(mesh):
    shape = mesh.shape
    chips = shape["tp"] // 2
    nzl = 4
    fine = Mesh(
        np.asarray(mesh.devices).reshape(shape["chain"], chips // nzl, nzl, 2, shape["dec"]),
        ("chain", "zh", "zl", "core", "dec"),
    )
    row = ("chain",) + TP
    return jax.shard_map(
        local,
        mesh=fine,
        in_specs=(
            P("dec", row, None),
            P("dec", "chain", TP, None),
            P("dec", "chain", TP, None),
            P(),
            P(None, TP),
            P(TP, None, None),
            P(TP, None, None),
            P(TP, None),
            P("dec", "chain"),
            P("dec", "chain"),
        ),
        out_specs=(
            P("dec", row, None),
            P("dec", "chain", None, TP, None),
            P("dec", "chain", None, TP, None),
        ),
        check_vma=False,
    )
```

```python
import functools

import jax
import jax.numpy as jnp
import numpy as np
from jax import lax
from jax.experimental import pallas as pl
from jax.experimental.pallas import tpu as pltpu
from jax.sharding import Mesh, PartitionSpec as P

BF = jnp.bfloat16
F32 = jnp.float32
LOG2E = 1.4426950408889634
Z = ("zh", "zl")
TP = ("zh", "zl", "core")
NEG = -1e30
STEPS = [4 * e + d for d in (0, 1, -1) for e in (-1, 0, 1, 2)] + [2, 6, -6, -2]


def swap_halves(v):
    half = v.shape[-1] // 2
    return jnp.concatenate([v[..., half:], v[..., :half]], -1)


def shift_z(x, step):
    n = lax.axis_size("zh") * lax.axis_size("zl")
    return lax.ppermute(x, Z, [(i, (i + step) % n) for i in range(n)])


def swap_core(x):
    return lax.ppermute(x, "core", [(0, 1), (1, 0)])


def spread(x, axis):
    n = lax.axis_size(axis)
    return lax.all_to_all(jnp.broadcast_to(x[None], (n,) + x.shape), axis, 0, 0, tiled=True)


def frequencies(width):
    half = width // 2
    lane = lax.broadcasted_iota(jnp.int32, (1, width), 1)
    out = jnp.ones((1, width), F32)
    for i in range(1, half):
        out = jnp.where(lane % half == i, np.float32(10000.0 ** (-2.0 * i / width)), out)
    return out


def rope_factors(where_at):
    width = where_at.shape[1]
    angle = where_at.astype(F32) * frequencies(width)
    lane = lax.broadcasted_iota(jnp.int32, where_at.shape, 1)
    sine = jnp.sin(angle)
    return jnp.cos(angle), jnp.where(lane < width // 2, -sine, sine)


def blocks(shapes):
    at = 0
    for w, shape in enumerate(shapes):
        for lead in range(int(np.prod(shape[:-2]))):
            for c in range(0, shape[-1], 128):
                yield at, w, lead, c, shape[-2]
                at += shape[-2]


def packed_rows(shapes):
    return sum(int(np.prod(shape)) for shape in shapes) // 128


def block_of(ref, lead, c):
    if len(ref.shape) == 3:
        return ref.at[lead, :, pl.ds(c, 128)]
    return ref.at[:, pl.ds(c, 128)]


def key_kernel(
    where_ref, owner_ref, slot_ref, lat_ref, rope_ref, gain_ref, *refs, slots, page_len, shapes
):
    ins, out_ref, page_ref, packed = refs[: len(shapes)], refs[-3], refs[-2], refs[-1]
    pages, part, lat = lat_ref.shape[1:]
    latent = jnp.concatenate([lat_ref[0, p].astype(F32) for p in range(pages)], 0)
    rot = jnp.concatenate([rope_ref[0, p].astype(F32) for p in range(pages)], 0)
    norm = lax.rsqrt(jnp.mean(latent * latent, -1, keepdims=True) + 1e-06)
    normed = (latent * norm * gain_ref[...]).astype(BF)
    row = lax.broadcasted_iota(jnp.int32, rot.shape, 0)
    cosine, sine = rope_factors(where_ref[0] + row // part * page_len + row % part)
    turned = rot * cosine + swap_halves(rot) * sine
    code = jnp.zeros_like(turned)
    for p in range(pages):
        here = (owner_ref[0, p] * slots + slot_ref[0, p]).astype(F32)
        code = jnp.where(row // part == p, here, code)
    out_ref[:, :lat] = normed
    out_ref[:, lat:] = jnp.concatenate([turned, jnp.zeros_like(turned)], -1).astype(BF)
    tail = jnp.concatenate([turned, code], -1).astype(BF)
    for i in range(page_ref.shape[0]):
        page_ref[i, :, :lat] = normed
        page_ref[i, :, lat:] = tail
    for at, w, lead, c, n in blocks(shapes):
        src = ins[w]
        if len(src.shape) == 3:
            packed[at : at + n, :] = src[lead, :, c : c + 128]
        else:
            packed[at : at + n, :] = src[:, c : c + 128]


def weight_loads(own, packed, dst, which, shapes, sems):
    loads = [(src, d.at[0]) for src, d in zip(own, dst)]
    for at, w, lead, c, n in blocks(shapes):
        if w in which:
            to = block_of(dst[which.index(w)].at[1], lead, c)
            loads.append((packed.at[pl.ds(at, n), :], to))
    return [pltpu.make_async_copy(src, to, sems.at[i]) for i, (src, to) in enumerate(loads)]


def load_count(which, shapes):
    return len(which) + sum(1 for b in blocks(shapes) if b[1] in which)


def query_where(idx, z, core, qrows, chips):
    blk = idx // qrows
    off = jnp.zeros_like(idx)
    for i, step in enumerate(STEPS):
        off = jnp.where(blk == i, step % chips, off)
    return lax.rem(z + off, chips) * (2 * qrows) + core * qrows + idx % qrows


def query_kernel(
    where_ref, g_ref, wq0, ak0, packed, out_ref, x_ref, wq_ref, ak_ref, sems,
    *, nope, rope, qrows, chips, shapes,
):
    loads = weight_loads((wq0, ak0), packed, (wq_ref, ak_ref), (0, 1), shapes, sems)
    for load in loads:
        load.start()
    chain, z, core = where_ref[0], where_ref[1], where_ref[2]
    for i, step in enumerate(STEPS):
        at = lax.rem(z + step % chips, chips)
        x_ref[i * qrows : (i + 1) * qrows, :] = g_ref[pl.ds(pl.multiple_of(at * qrows, qrows), qrows), :]
    x = x_ref[...]
    rows = x.shape[0]
    lat = ak_ref.shape[-1]
    idx = lax.broadcasted_iota(jnp.int32, (rows, rope), 0)
    place = chain * (chips * 2 * qrows) + query_where(idx, z, core, qrows, chips)
    cosine, sine = rope_factors(place)
    head = 0
    for side in range(2):
        for load in loads[2:] if side else loads[:2]:
            load.wait()
        ak = ak_ref.at[side]
        q = jnp.dot(x, wq_ref[side], preferred_element_type=F32).astype(BF)
        for h in range(ak.shape[0]):
            base = h * (nope + rope)
            r0 = head * rows
            out_ref[r0 : r0 + rows, :lat] = jnp.dot(
                q[:, base : base + nope], ak[h], preferred_element_type=F32
            ).astype(BF)
            rot = q[:, base + nope : base + nope + rope].astype(F32)
            turned = rot * cosine + swap_halves(rot) * sine
            out_ref[r0 : r0 + rows, lat:] = jnp.concatenate(
                [turned, jnp.zeros_like(turned)], -1
            ).astype(BF)
            head += 1


def attend_kernel(
    where_ref, q_ref, ka_ref, kb_ref, av0, op0, packed, o0, o1, o2, o3, o4,
    acc_ref, ho_ref, av_ref, op_ref, sems, *, rows, lat, scale, nch, chips, qrows, part, shapes,
):
    chain, z, core = where_ref[0], where_ref[1], where_ref[2]
    s2 = scale * LOG2E
    loads = weight_loads((av0, op0), packed, (av_ref, op_ref), (2, 3), shapes, sems)
    for load in loads:
        load.start()
    vh = av_ref.shape[-1]
    heads = q_ref.shape[0] // rows
    n = ka_ref.shape[0] // nch
    nt = (((1,), (1,)), ((), ()))

    def attend(blocks_seen):
        count = blocks_seen * n
        idx = lax.broadcasted_iota(jnp.int32, (rows, 1), 0)
        qpos = query_where(idx, z, core, qrows, chips)
        idx = lax.broadcasted_iota(jnp.int32, (1, n), 1)
        kpos = (idx % qrows) // part * (chips * 2 * part) + idx // qrows * (2 * part) + idx % part
        ok = [kpos + i * part <= qpos for i in (core, 1 - core)]
        for h in range(heads):
            q = q_ref[h * rows : (h + 1) * rows, :]
            scores = []
            for i, k_ref in enumerate((ka_ref, kb_ref)):
                s = lax.dot_general(q, k_ref[:count, :], nt, preferred_element_type=F32)
                own = jnp.where(ok[i], s[:, count - n :], NEG)
                scores.append(own if count == n else jnp.concatenate([s[:, : count - n], own], -1))
            m = jnp.maximum(*[jnp.max(s, -1, keepdims=True) for s in scores]) * s2
            total, mixed = 0.0, 0.0
            for s, k_ref in zip(scores, (ka_ref, kb_ref)):
                p = jnp.exp2(s * s2 - m)
                total = total + jnp.sum(p, -1, keepdims=True)
                mixed = mixed + jnp.dot(p.astype(BF), k_ref[:count, :lat], preferred_element_type=F32)
            acc_ref[h * rows : (h + 1) * rows, :] = (mixed / total).astype(BF)

    for seen in range(1, nch + 1):
        pl.when(chain == seen - 1)(functools.partial(attend, seen))
    for load in loads:
        load.wait()
    per = heads // 2
    for h in range(heads):
        av = av_ref[h // per, h % per]
        ho_ref[:, h * vh : (h + 1) * vh] = jnp.dot(
            acc_ref[h * rows : (h + 1) * rows, :], av, preferred_element_type=F32
        ).astype(BF)
    ho = ho_ref[...]
    k, width = op_ref.shape[1:]
    cut = 512 if width % 512 == 0 else width
    for c in range(0, width, cut):
        part_out = (
            jnp.dot(ho[:, :k], op_ref[0, :, c : c + cut], preferred_element_type=F32)
            + jnp.dot(ho[:, k:], op_ref[1, :, c : c + cut], preferred_element_type=F32)
        ).astype(BF)
        at = 0
        for out_ref in (o0, o1, o2, o3, o4):
            out_ref[:, c : c + cut] = part_out[at : at + out_ref.shape[0]]
            at += out_ref.shape[0]


def local(
    query_comp, latent_rows, rope_keys, latent_gain, query_up, absorb_key, absorb_value, out_proj,
    page_owner, page_slot,
):
    nzh, nzl, nch = lax.axis_size("zh"), lax.axis_size("zl"), lax.axis_size("chain")
    zh, zl, core = lax.axis_index("zh"), lax.axis_index("zl"), lax.axis_index("core")
    chain, dec = lax.axis_index("chain"), lax.axis_index("dec")
    pages, part, lat = latent_rows.shape[1:]
    rope = rope_keys.shape[3]
    heads_here, nope = absorb_key.shape[:2]
    vh = absorb_value.shape[2]
    qrows, ql = query_comp.shape[1:]
    width = out_proj.shape[1]
    tp_index = (zh * nzl + zl) * 2 + core
    tp_count = nzh * nzl * 2
    block_len = qrows * tp_count
    slots = 2 * pages
    smem = pl.BlockSpec(memory_space=pltpu.SMEM)
    vm = pl.BlockSpec(memory_space=pltpu.VMEM)
    hbm = pl.BlockSpec(memory_space=pltpu.HBM)

    def room(mib):
        return pltpu.CompilerParams(vmem_limit_bytes=mib * 1024 * 1024)

    rows = qrows * nzh * nzl
    kw = lat + 2 * rope
    heads = 2 * heads_here
    z = zh * nzl + zl
    where = jnp.stack([chain, z, core]).astype(jnp.int32)
    weights = (query_up, absorb_key, absorb_value, out_proj)
    shapes = tuple(w.shape for w in weights)
    keys, page, packed = pl.pallas_call(
        functools.partial(key_kernel, slots=slots, page_len=part * tp_count, shapes=shapes),
        out_shape=(
            jax.ShapeDtypeStruct((pages * part, kw), BF),
            jax.ShapeDtypeStruct((lax.axis_size("dec"), pages * part, kw), BF),
            jax.ShapeDtypeStruct((packed_rows(shapes), 128), BF),
        ),
        in_specs=[smem] * 3 + [vm] * 7,
        out_specs=(vm, vm, vm),
        compiler_params=room(56),
        name="keys",
    )(
        (chain * block_len + tp_index * part).astype(jnp.int32)[None], page_owner, page_slot,
        latent_rows, rope_keys, latent_gain[None], *weights,
    )
    packed = swap_core(packed)

    own = lax.all_gather(keys, Z, axis=0, tiled=True)
    mine = spread(own, "chain").reshape(nch * rows, kw)
    held = lax.optimization_barrier((query_comp[0], own))[0]
    qg = lax.all_gather(held, Z, axis=0, tiled=True)
    qg, mine = lax.optimization_barrier((qg, mine))
    other = swap_core(mine)

    q = pl.pallas_call(
        functools.partial(query_kernel, nope=nope, rope=rope, qrows=qrows, chips=nzh * nzl, shapes=shapes),
        out_shape=jax.ShapeDtypeStruct((heads * rows, kw), BF),
        in_specs=[smem, vm] + [hbm] * 3,
        out_specs=vm,
        scratch_shapes=[
            pltpu.VMEM((rows, ql), BF),
            pltpu.VMEM((2,) + query_up.shape, BF),
            pltpu.VMEM((2,) + absorb_key.shape, BF),
            pltpu.SemaphoreType.DMA((load_count((0, 1), shapes),)),
        ],
        compiler_params=room(12),
        cost_estimate=pl.CostEstimate(
            flops=2 * rows * heads * (nope + rope) * ql + 2 * rows * heads * nope * lat,
            bytes_accessed=6000000, transcendentals=0,
        ),
        name="queries",
    )(where, qg, query_up, absorb_key, packed)

    n = nzh * qrows
    sums = pl.pallas_call(
        functools.partial(
            attend_kernel, rows=rows, lat=lat, scale=(nope + rope) ** -0.5,
            nch=nch, chips=nzh * nzl, qrows=qrows, part=part, shapes=shapes,
        ),
        out_shape=[jax.ShapeDtypeStruct((r, width), BF) for r in (n, n, n, n // 2, n // 2)],
        in_specs=[smem] + [vm] * 3 + [hbm] * 3,
        out_specs=[vm] * 5,
        scratch_shapes=[
            pltpu.VMEM((heads * rows, lat), BF),
            pltpu.VMEM((rows, heads * vh), BF),
            pltpu.VMEM((2,) + absorb_value.shape, BF),
            pltpu.VMEM((2,) + out_proj.shape, BF),
            pltpu.SemaphoreType.DMA((load_count((2, 3), shapes),)),
        ],
        compiler_params=room(28),
        cost_estimate=pl.CostEstimate(
            flops=4 * rows * heads * nch * block_len * lat, bytes_accessed=9000000,
            transcendentals=rows * heads * nch * block_len,
        ),
        name="attend",
    )(where, q, mine, other, absorb_value, out_proj, packed)

    up = shift_z(sums[1], 1)
    down = shift_z(sums[2], -1)
    up2 = shift_z(sums[3], 2)
    down2 = shift_z(sums[4], -2)
    cut = width // 2

    def near(e, up, down):
        at = slice((e + 1) * qrows, (e + 2) * qrows)
        return sums[0][at].astype(F32) + up[at].astype(F32) + down[at].astype(F32)

    far = near(2, up, down).astype(BF)
    far, up, down = lax.optimization_barrier((far, up, down))
    left, right = lax.optimization_barrier((shift_z(far[:, :cut], nzl), shift_z(far[:, cut:], -nzl)))
    ahead = near(1, up, down) + up2[qrows:].astype(F32)
    ahead = jnp.concatenate([ahead[:, :cut] + left.astype(F32), ahead[:, cut:]], -1)
    ahead = shift_z(ahead.astype(BF), nzl)
    behind = near(-1, up, down) + down2[:qrows].astype(F32)
    behind = jnp.concatenate([behind[:, :cut], behind[:, cut:] + right.astype(F32)], -1)
    behind = shift_z(behind.astype(BF), -nzl)
    total = near(0, up, down) + up2[:qrows].astype(F32) + down2[qrows:].astype(F32)
    total = total + ahead.astype(F32) + behind.astype(F32)
    layer_output = total.astype(BF)[None]

    page = lax.optimization_barrier((page, down2))[0]
    page = lax.all_to_all(page, "dec", 0, 0, tiled=True).reshape(-1, pages, part, kw)
    came = page[:, :, 0, lat + rope].reshape(-1).astype(jnp.int32)
    take = (came[None, :] == dec * slots + jnp.arange(slots, dtype=jnp.int32)[:, None]).astype(BF)
    placed = jnp.einsum(
        "sp,pjc->sjc", take, page.reshape(-1, part, page.shape[-1]), preferred_element_type=F32
    ).astype(BF)
    cache_latent = placed[..., :lat][None, None]
    cache_rope = placed[..., lat : lat + rope][None, None]
    return (layer_output, cache_latent, cache_rope)


def solution(mesh):
    shape = mesh.shape
    chips = shape["tp"] // 2
    nzl = 4
    fine = Mesh(
        np.asarray(mesh.devices).reshape(shape["chain"], chips // nzl, nzl, 2, shape["dec"]),
        ("chain", "zh", "zl", "core", "dec"),
    )
    row = ("chain",) + TP
    return jax.shard_map(
        local,
        mesh=fine,
        in_specs=(
            P("dec", row, None),
            P("dec", "chain", TP, None),
            P("dec", "chain", TP, None),
            P(),
            P(None, TP),
            P(TP, None, None),
            P(TP, None, None),
            P(TP, None),
            P("dec", "chain"),
            P("dec", "chain"),
        ),
        out_specs=(
            P("dec", row, None),
            P("dec", "chain", None, TP, None),
            P("dec", "chain", None, TP, None),
        ),
        check_vma=False,
    )
```

```python
import functools

import jax
import jax.numpy as jnp
import numpy as np
from jax import lax
from jax.experimental import pallas as pl
from jax.experimental.pallas import tpu as pltpu
from jax.sharding import Mesh, PartitionSpec as P

BF = jnp.bfloat16
F32 = jnp.float32
LOG2E = 1.4426950408889634
Z = ("zh", "zl")
TP = ("zh", "zl", "core")
NEG = -1e30
STEPS = [4 * e + d for d in (0, 1, -1) for e in (-1, 0, 1, 2)] + [2, 6, -6, -2]


def swap_halves(v):
    half = v.shape[-1] // 2
    return jnp.concatenate([v[..., half:], v[..., :half]], -1)


def shift_z(x, step):
    n = lax.axis_size("zh") * lax.axis_size("zl")
    return lax.ppermute(x, Z, [(i, (i + step) % n) for i in range(n)])


def swap_core(x):
    return lax.ppermute(x, "core", [(0, 1), (1, 0)])


def spread(x, axis):
    n = lax.axis_size(axis)
    return lax.all_to_all(jnp.broadcast_to(x[None], (n,) + x.shape), axis, 0, 0, tiled=True)


def frequencies(width):
    half = width // 2
    lane = lax.broadcasted_iota(jnp.int32, (1, width), 1)
    out = jnp.ones((1, width), F32)
    for i in range(1, half):
        out = jnp.where(lane % half == i, np.float32(10000.0 ** (-2.0 * i / width)), out)
    return out


def rope_factors(where_at):
    width = where_at.shape[1]
    angle = where_at.astype(F32) * frequencies(width)
    lane = lax.broadcasted_iota(jnp.int32, where_at.shape, 1)
    sine = jnp.sin(angle)
    return jnp.cos(angle), jnp.where(lane < width // 2, -sine, sine)


def blocks(shapes):
    at = 0
    for w, shape in enumerate(shapes):
        for lead in range(int(np.prod(shape[:-2]))):
            for c in range(0, shape[-1], 128):
                yield at, w, lead, c, shape[-2]
                at += shape[-2]


def packed_rows(shapes):
    return sum(int(np.prod(shape)) for shape in shapes) // 128


def block_of(ref, lead, c):
    if len(ref.shape) == 3:
        return ref.at[lead, :, pl.ds(c, 128)]
    return ref.at[:, pl.ds(c, 128)]


def key_kernel(
    where_ref, owner_ref, slot_ref, lat_ref, rope_ref, gain_ref, *refs, slots, page_len, shapes
):
    ins, out_ref, page_ref, packed = refs[: len(shapes)], refs[-3], refs[-2], refs[-1]
    pages, part, lat = lat_ref.shape[1:]
    latent = jnp.concatenate([lat_ref[0, p].astype(F32) for p in range(pages)], 0)
    rot = jnp.concatenate([rope_ref[0, p].astype(F32) for p in range(pages)], 0)
    norm = lax.rsqrt(jnp.mean(latent * latent, -1, keepdims=True) + 1e-06)
    normed = (latent * norm * gain_ref[...]).astype(BF)
    row = lax.broadcasted_iota(jnp.int32, rot.shape, 0)
    cosine, sine = rope_factors(where_ref[0] + row // part * page_len + row % part)
    turned = rot * cosine + swap_halves(rot) * sine
    code = jnp.zeros_like(turned)
    for p in range(pages):
        here = (owner_ref[0, p] * slots + slot_ref[0, p]).astype(F32)
        code = jnp.where(row // part == p, here, code)
    out_ref[:, :lat] = normed
    out_ref[:, lat:] = jnp.concatenate([turned, jnp.zeros_like(turned)], -1).astype(BF)
    tail = jnp.concatenate([turned, code], -1).astype(BF)
    for i in range(page_ref.shape[0]):
        page_ref[i, :, :lat] = normed
        page_ref[i, :, lat:] = tail
    for at, w, lead, c, n in blocks(shapes):
        src = ins[w]
        if len(src.shape) == 3:
            packed[at : at + n, :] = src[lead, :, c : c + 128]
        else:
            packed[at : at + n, :] = src[:, c : c + 128]


def weight_loads(own, packed, dst, which, shapes, sems):
    loads = [(src, d.at[0]) for src, d in zip(own, dst)]
    for at, w, lead, c, n in blocks(shapes):
        if w in which:
            to = block_of(dst[which.index(w)].at[1], lead, c)
            loads.append((packed.at[pl.ds(at, n), :], to))
    return [pltpu.make_async_copy(src, to, sems.at[i]) for i, (src, to) in enumerate(loads)]


def load_count(which, shapes):
    return len(which) + sum(1 for b in blocks(shapes) if b[1] in which)


def query_where(idx, z, core, qrows, chips):
    blk = idx // qrows
    off = jnp.zeros_like(idx)
    for i, step in enumerate(STEPS):
        off = jnp.where(blk == i, step % chips, off)
    return lax.rem(z + off, chips) * (2 * qrows) + core * qrows + idx % qrows


def query_kernel(
    where_ref, g_ref, wq0, ak0, packed, out_ref, x_ref, wq_ref, ak_ref, sems,
    *, nope, rope, qrows, chips, shapes,
):
    loads = weight_loads((wq0, ak0), packed, (wq_ref, ak_ref), (0, 1), shapes, sems)
    for load in loads:
        load.start()
    chain, z, core = where_ref[0], where_ref[1], where_ref[2]
    for i, step in enumerate(STEPS):
        at = lax.rem(z + step % chips, chips)
        x_ref[i * qrows : (i + 1) * qrows, :] = g_ref[pl.ds(pl.multiple_of(at * qrows, qrows), qrows), :]
    x = x_ref[...]
    rows = x.shape[0]
    lat = ak_ref.shape[-1]
    idx = lax.broadcasted_iota(jnp.int32, (rows, rope), 0)
    place = chain * (chips * 2 * qrows) + query_where(idx, z, core, qrows, chips)
    cosine, sine = rope_factors(place)
    head = 0
    for side in range(2):
        for load in loads[2:] if side else loads[:2]:
            load.wait()
        ak = ak_ref.at[side]
        q = jnp.dot(x, wq_ref[side], preferred_element_type=F32).astype(BF)
        for h in range(ak.shape[0]):
            base = h * (nope + rope)
            r0 = head * rows
            out_ref[r0 : r0 + rows, :lat] = jnp.dot(
                q[:, base : base + nope], ak[h], preferred_element_type=F32
            ).astype(BF)
            rot = q[:, base + nope : base + nope + rope].astype(F32)
            turned = rot * cosine + swap_halves(rot) * sine
            out_ref[r0 : r0 + rows, lat:] = jnp.concatenate(
                [turned, jnp.zeros_like(turned)], -1
            ).astype(BF)
            head += 1


def attend_kernel(
    where_ref, q_ref, ka_ref, kb_ref, av0, op0, packed, o0, o1, o2, o3, o4,
    acc_ref, ho_ref, av_ref, op_ref, sems, *, rows, lat, scale, nch, chips, qrows, part, shapes,
):
    chain, z, core = where_ref[0], where_ref[1], where_ref[2]
    s2 = scale * LOG2E
    loads = weight_loads((av0, op0), packed, (av_ref, op_ref), (2, 3), shapes, sems)
    for load in loads:
        load.start()
    vh = av_ref.shape[-1]
    heads = q_ref.shape[0] // rows
    n = ka_ref.shape[0] // nch
    nt = (((1,), (1,)), ((), ()))

    def attend(blocks_seen):
        count = blocks_seen * n
        idx = lax.broadcasted_iota(jnp.int32, (rows, 1), 0)
        qpos = query_where(idx, z, core, qrows, chips)
        idx = lax.broadcasted_iota(jnp.int32, (1, n), 1)
        kpos = (idx % qrows) // part * (chips * 2 * part) + idx // qrows * (2 * part) + idx % part
        ok = [kpos + i * part <= qpos for i in (core, 1 - core)]
        for h in range(heads):
            q = q_ref[h * rows : (h + 1) * rows, :]
            scores = []
            for i, k_ref in enumerate((ka_ref, kb_ref)):
                for part_keys in (slice(0, count - n), slice(count - n, count)):
                    if part_keys.start == part_keys.stop:
                        continue
                    s = lax.dot_general(q, k_ref[part_keys, :], nt, preferred_element_type=F32)
                    if part_keys.stop == count:
                        s = jnp.where(ok[i], s, NEG)
                    scores.append((s, k_ref, part_keys))
            m = functools.reduce(jnp.maximum, [jnp.max(s, -1, keepdims=True) for s, _, _ in scores])
            m = m * s2
            total, mixed = 0.0, 0.0
            for s, k_ref, part_keys in scores:
                p = jnp.exp2(s * s2 - m)
                total = total + jnp.sum(p, -1, keepdims=True)
                mixed = mixed + jnp.dot(
                    p.astype(BF), k_ref[part_keys, :lat], preferred_element_type=F32
                )
            acc_ref[h * rows : (h + 1) * rows, :] = (mixed / total).astype(BF)

    for seen in range(1, nch + 1):
        pl.when(chain == seen - 1)(functools.partial(attend, seen))
    for load in loads:
        load.wait()
    per = heads // 2
    for h in range(heads):
        av = av_ref[h // per, h % per]
        ho_ref[:, h * vh : (h + 1) * vh] = jnp.dot(
            acc_ref[h * rows : (h + 1) * rows, :], av, preferred_element_type=F32
        ).astype(BF)
    ho = ho_ref[...]
    k, width = op_ref.shape[1:]
    cut = 512 if width % 512 == 0 else width
    for c in range(0, width, cut):
        part_out = (
            jnp.dot(ho[:, :k], op_ref[0, :, c : c + cut], preferred_element_type=F32)
            + jnp.dot(ho[:, k:], op_ref[1, :, c : c + cut], preferred_element_type=F32)
        ).astype(BF)
        at = 0
        for out_ref in (o0, o1, o2, o3, o4):
            out_ref[:, c : c + cut] = part_out[at : at + out_ref.shape[0]]
            at += out_ref.shape[0]


def local(
    query_comp, latent_rows, rope_keys, latent_gain, query_up, absorb_key, absorb_value, out_proj,
    page_owner, page_slot,
):
    nzh, nzl, nch = lax.axis_size("zh"), lax.axis_size("zl"), lax.axis_size("chain")
    zh, zl, core = lax.axis_index("zh"), lax.axis_index("zl"), lax.axis_index("core")
    chain, dec = lax.axis_index("chain"), lax.axis_index("dec")
    pages, part, lat = latent_rows.shape[1:]
    rope = rope_keys.shape[3]
    heads_here, nope = absorb_key.shape[:2]
    vh = absorb_value.shape[2]
    qrows, ql = query_comp.shape[1:]
    width = out_proj.shape[1]
    tp_index = (zh * nzl + zl) * 2 + core
    tp_count = nzh * nzl * 2
    block_len = qrows * tp_count
    slots = 2 * pages
    smem = pl.BlockSpec(memory_space=pltpu.SMEM)
    vm = pl.BlockSpec(memory_space=pltpu.VMEM)
    hbm = pl.BlockSpec(memory_space=pltpu.HBM)

    def room(mib):
        return pltpu.CompilerParams(vmem_limit_bytes=mib * 1024 * 1024)

    rows = qrows * nzh * nzl
    kw = lat + 2 * rope
    heads = 2 * heads_here
    z = zh * nzl + zl
    where = jnp.stack([chain, z, core]).astype(jnp.int32)
    weights = (query_up, absorb_key, absorb_value, out_proj)
    shapes = tuple(w.shape for w in weights)
    keys, page, packed = pl.pallas_call(
        functools.partial(key_kernel, slots=slots, page_len=part * tp_count, shapes=shapes),
        out_shape=(
            jax.ShapeDtypeStruct((pages * part, kw), BF),
            jax.ShapeDtypeStruct((lax.axis_size("dec"), pages * part, kw), BF),
            jax.ShapeDtypeStruct((packed_rows(shapes), 128), BF),
        ),
        in_specs=[smem] * 3 + [vm] * 7,
        out_specs=(vm, vm, vm),
        compiler_params=room(56),
        name="keys",
    )(
        (chain * block_len + tp_index * part).astype(jnp.int32)[None], page_owner, page_slot,
        latent_rows, rope_keys, latent_gain[None], *weights,
    )
    packed = swap_core(packed)

    own = lax.all_gather(keys, Z, axis=0, tiled=True)
    mine = spread(own, "chain").reshape(nch * rows, kw)
    held = lax.optimization_barrier((query_comp[0], own))[0]
    qg = lax.all_gather(held, Z, axis=0, tiled=True)
    qg, mine = lax.optimization_barrier((qg, mine))
    other = swap_core(mine)

    q = pl.pallas_call(
        functools.partial(query_kernel, nope=nope, rope=rope, qrows=qrows, chips=nzh * nzl, shapes=shapes),
        out_shape=jax.ShapeDtypeStruct((heads * rows, kw), BF),
        in_specs=[smem, vm] + [hbm] * 3,
        out_specs=vm,
        scratch_shapes=[
            pltpu.VMEM((rows, ql), BF),
            pltpu.VMEM((2,) + query_up.shape, BF),
            pltpu.VMEM((2,) + absorb_key.shape, BF),
            pltpu.SemaphoreType.DMA((load_count((0, 1), shapes),)),
        ],
        compiler_params=room(12),
        cost_estimate=pl.CostEstimate(
            flops=2 * rows * heads * (nope + rope) * ql + 2 * rows * heads * nope * lat,
            bytes_accessed=6000000, transcendentals=0,
        ),
        name="queries",
    )(where, qg, query_up, absorb_key, packed)

    n = nzh * qrows
    sums = pl.pallas_call(
        functools.partial(
            attend_kernel, rows=rows, lat=lat, scale=(nope + rope) ** -0.5,
            nch=nch, chips=nzh * nzl, qrows=qrows, part=part, shapes=shapes,
        ),
        out_shape=[jax.ShapeDtypeStruct((r, width), BF) for r in (n, n, n, n // 2, n // 2)],
        in_specs=[smem] + [vm] * 3 + [hbm] * 3,
        out_specs=[vm] * 5,
        scratch_shapes=[
            pltpu.VMEM((heads * rows, lat), BF),
            pltpu.VMEM((rows, heads * vh), BF),
            pltpu.VMEM((2,) + absorb_value.shape, BF),
            pltpu.VMEM((2,) + out_proj.shape, BF),
            pltpu.SemaphoreType.DMA((load_count((2, 3), shapes),)),
        ],
        compiler_params=room(28),
        cost_estimate=pl.CostEstimate(
            flops=4 * rows * heads * nch * block_len * lat, bytes_accessed=9000000,
            transcendentals=rows * heads * nch * block_len,
        ),
        name="attend",
    )(where, q, mine, other, absorb_value, out_proj, packed)

    up = shift_z(sums[1], 1)
    down = shift_z(sums[2], -1)
    up2 = shift_z(sums[3], 2)
    down2 = shift_z(sums[4], -2)
    cut = width // 2

    def near(e, up, down):
        at = slice((e + 1) * qrows, (e + 2) * qrows)
        return sums[0][at].astype(F32) + up[at].astype(F32) + down[at].astype(F32)

    far = near(2, up, down).astype(BF)
    far, up, down = lax.optimization_barrier((far, up, down))
    first = shift_z(far[:, :cut], nzl)
    left, right = lax.optimization_barrier((first, shift_z(far[:, cut:], -nzl)))
    ahead = near(1, up, down) + up2[qrows:].astype(F32)
    ahead = jnp.concatenate([ahead[:, :cut] + left.astype(F32), ahead[:, cut:]], -1)
    ahead = shift_z(ahead.astype(BF), nzl)
    behind = near(-1, up, down) + down2[:qrows].astype(F32)
    behind = jnp.concatenate([behind[:, :cut], behind[:, cut:] + right.astype(F32)], -1)
    behind = shift_z(behind.astype(BF), -nzl)
    total = near(0, up, down) + up2[:qrows].astype(F32) + down2[qrows:].astype(F32)
    total = total + ahead.astype(F32) + behind.astype(F32)
    layer_output = total.astype(BF)[None]

    page = lax.optimization_barrier((page, first))[0]
    page = lax.all_to_all(page, "dec", 0, 0, tiled=True).reshape(-1, pages, part, kw)
    came = page[:, :, 0, lat + rope].reshape(-1).astype(jnp.int32)
    take = (came[None, :] == dec * slots + jnp.arange(slots, dtype=jnp.int32)[:, None]).astype(BF)
    placed = jnp.einsum(
        "sp,pjc->sjc", take, page.reshape(-1, part, page.shape[-1]), preferred_element_type=F32
    ).astype(BF)
    cache_latent = placed[..., :lat][None, None]
    cache_rope = placed[..., lat : lat + rope][None, None]
    return (layer_output, cache_latent, cache_rope)


def solution(mesh):
    shape = mesh.shape
    chips = shape["tp"] // 2
    nzl = 4
    fine = Mesh(
        np.asarray(mesh.devices).reshape(shape["chain"], chips // nzl, nzl, 2, shape["dec"]),
        ("chain", "zh", "zl", "core", "dec"),
    )
    row = ("chain",) + TP
    return jax.shard_map(
        local,
        mesh=fine,
        in_specs=(
            P("dec", row, None),
            P("dec", "chain", TP, None),
            P("dec", "chain", TP, None),
            P(),
            P(None, TP),
            P(TP, None, None),
            P(TP, None, None),
            P(TP, None),
            P("dec", "chain"),
            P("dec", "chain"),
        ),
        out_specs=(
            P("dec", row, None),
            P("dec", "chain", None, TP, None),
            P("dec", "chain", None, TP, None),
        ),
        check_vma=False,
    )
```

```python
import functools

import jax
import jax.numpy as jnp
import numpy as np
from jax import lax
from jax.experimental import pallas as pl
from jax.experimental.pallas import tpu as pltpu
from jax.sharding import Mesh, PartitionSpec as P

BF = jnp.bfloat16
F32 = jnp.float32
LOG2E = 1.4426950408889634
Z = ("zh", "zl")
TP = ("zh", "zl", "core")
NEG = -1e30
STEPS = [4 * e + d for d in (0, 1, -1) for e in (-1, 0, 1, 2)] + [2, 6, -6, -2]


def swap_halves(v):
    half = v.shape[-1] // 2
    return jnp.concatenate([v[..., half:], v[..., :half]], -1)


def shift_z(x, step):
    n = lax.axis_size("zh") * lax.axis_size("zl")
    return lax.ppermute(x, Z, [(i, (i + step) % n) for i in range(n)])


def swap_core(x):
    return lax.ppermute(x, "core", [(0, 1), (1, 0)])


def spread(x, axis):
    n = lax.axis_size(axis)
    return lax.all_to_all(jnp.broadcast_to(x[None], (n,) + x.shape), axis, 0, 0, tiled=True)


def frequencies(width):
    half = width // 2
    lane = lax.broadcasted_iota(jnp.int32, (1, width), 1)
    out = jnp.ones((1, width), F32)
    for i in range(1, half):
        out = jnp.where(lane % half == i, np.float32(10000.0 ** (-2.0 * i / width)), out)
    return out


def rope_factors(where_at):
    width = where_at.shape[1]
    angle = where_at.astype(F32) * frequencies(width)
    lane = lax.broadcasted_iota(jnp.int32, where_at.shape, 1)
    sine = jnp.sin(angle)
    return jnp.cos(angle), jnp.where(lane < width // 2, -sine, sine)


def blocks(shapes):
    at = 0
    for w, shape in enumerate(shapes):
        for lead in range(int(np.prod(shape[:-2]))):
            for c in range(0, shape[-1], 128):
                yield at, w, lead, c, shape[-2]
                at += shape[-2]


def packed_rows(shapes):
    return sum(int(np.prod(shape)) for shape in shapes) // 128


def block_of(ref, lead, c):
    if len(ref.shape) == 3:
        return ref.at[lead, :, pl.ds(c, 128)]
    return ref.at[:, pl.ds(c, 128)]


def key_kernel(
    where_ref, owner_ref, slot_ref, lat_ref, rope_ref, gain_ref, *refs, slots, page_len, shapes
):
    ins, out_ref, page_ref, packed = refs[: len(shapes)], refs[-3], refs[-2], refs[-1]
    pages, part, lat = lat_ref.shape[1:]
    latent = jnp.concatenate([lat_ref[0, p].astype(F32) for p in range(pages)], 0)
    rot = jnp.concatenate([rope_ref[0, p].astype(F32) for p in range(pages)], 0)
    norm = lax.rsqrt(jnp.mean(latent * latent, -1, keepdims=True) + 1e-06)
    normed = (latent * norm * gain_ref[...]).astype(BF)
    row = lax.broadcasted_iota(jnp.int32, rot.shape, 0)
    cosine, sine = rope_factors(where_ref[0] + row // part * page_len + row % part)
    turned = rot * cosine + swap_halves(rot) * sine
    code = jnp.zeros_like(turned)
    for p in range(pages):
        here = (owner_ref[0, p] * slots + slot_ref[0, p]).astype(F32)
        code = jnp.where(row // part == p, here, code)
    out_ref[:, :lat] = normed
    out_ref[:, lat:] = jnp.concatenate([turned, jnp.zeros_like(turned)], -1).astype(BF)
    tail = jnp.concatenate([turned, code], -1).astype(BF)
    for i in range(page_ref.shape[0]):
        page_ref[i, :, :lat] = normed
        page_ref[i, :, lat:] = tail
    for at, w, lead, c, n in blocks(shapes):
        src = ins[w]
        if len(src.shape) == 3:
            packed[at : at + n, :] = src[lead, :, c : c + 128]
        else:
            packed[at : at + n, :] = src[:, c : c + 128]


def weight_loads(own, packed, dst, which, shapes, sems):
    loads = [(src, d.at[0]) for src, d in zip(own, dst)]
    for at, w, lead, c, n in blocks(shapes):
        if w in which:
            to = block_of(dst[which.index(w)].at[1], lead, c)
            loads.append((packed.at[pl.ds(at, n), :], to))
    return [pltpu.make_async_copy(src, to, sems.at[i]) for i, (src, to) in enumerate(loads)]


def load_count(which, shapes):
    return len(which) + sum(1 for b in blocks(shapes) if b[1] in which)


def query_where(idx, z, core, qrows, chips):
    blk = idx // qrows
    off = jnp.zeros_like(idx)
    for i, step in enumerate(STEPS):
        off = jnp.where(blk == i, step % chips, off)
    return lax.rem(z + off, chips) * (2 * qrows) + core * qrows + idx % qrows


def query_kernel(
    where_ref, g_ref, wq0, ak0, packed, out_ref, x_ref, wq_ref, ak_ref, sems,
    *, nope, rope, qrows, chips, shapes,
):
    loads = weight_loads((wq0, ak0), packed, (wq_ref, ak_ref), (0, 1), shapes, sems)
    for load in loads:
        load.start()
    chain, z, core = where_ref[0], where_ref[1], where_ref[2]
    for i, step in enumerate(STEPS):
        at = lax.rem(z + step % chips, chips)
        x_ref[i * qrows : (i + 1) * qrows, :] = g_ref[pl.ds(pl.multiple_of(at * qrows, qrows), qrows), :]
    x = x_ref[...]
    rows = x.shape[0]
    lat = ak_ref.shape[-1]
    idx = lax.broadcasted_iota(jnp.int32, (rows, rope), 0)
    place = chain * (chips * 2 * qrows) + query_where(idx, z, core, qrows, chips)
    cosine, sine = rope_factors(place)
    head = 0
    for side in range(2):
        for load in loads[2:] if side else loads[:2]:
            load.wait()
        ak = ak_ref.at[side]
        q = jnp.dot(x, wq_ref[side], preferred_element_type=F32).astype(BF)
        for h in range(ak.shape[0]):
            base = h * (nope + rope)
            r0 = head * rows
            out_ref[r0 : r0 + rows, :lat] = jnp.dot(
                q[:, base : base + nope], ak[h], preferred_element_type=F32
            ).astype(BF)
            rot = q[:, base + nope : base + nope + rope].astype(F32)
            turned = rot * cosine + swap_halves(rot) * sine
            out_ref[r0 : r0 + rows, lat:] = jnp.concatenate(
                [turned, jnp.zeros_like(turned)], -1
            ).astype(BF)
            head += 1


def attend_kernel(
    where_ref, q_ref, ka_ref, kb_ref, av0, op0, packed, o0, o1, o2, o3, o4,
    acc_ref, ho_ref, av_ref, op_ref, sems, *, rows, lat, scale, nch, chips, qrows, part, shapes,
):
    chain, z, core = where_ref[0], where_ref[1], where_ref[2]
    s2 = scale * LOG2E
    loads = weight_loads((av0, op0), packed, (av_ref, op_ref), (2, 3), shapes, sems)
    for load in loads:
        load.start()
    vh = av_ref.shape[-1]
    heads = q_ref.shape[0] // rows
    n = ka_ref.shape[0] // nch
    nt = (((1,), (1,)), ((), ()))

    def attend(blocks_seen):
        count = blocks_seen * n
        idx = lax.broadcasted_iota(jnp.int32, (2 * rows, 1), 0) % rows
        qpos = query_where(idx, z, core, qrows, chips)
        idx = lax.broadcasted_iota(jnp.int32, (1, n), 1)
        kpos = (idx % qrows) // part * (chips * 2 * part) + idx // qrows * (2 * part) + idx % part
        ok = [kpos + i * part <= qpos for i in (core, 1 - core)]
        for h in range(0, heads, 2):
            q = q_ref[h * rows : (h + 2) * rows, :]
            scores = []
            for i, k_ref in enumerate((ka_ref, kb_ref)):
                for part_keys in (slice(0, count - n), slice(count - n, count)):
                    if part_keys.start == part_keys.stop:
                        continue
                    s = lax.dot_general(q, k_ref[part_keys, :], nt, preferred_element_type=F32)
                    if part_keys.stop == count:
                        s = jnp.where(ok[i], s, NEG)
                    scores.append((s, k_ref, part_keys))
            m = functools.reduce(jnp.maximum, [jnp.max(s, -1, keepdims=True) for s, _, _ in scores])
            m = m * s2
            total, mixed = 0.0, 0.0
            for s, k_ref, part_keys in scores:
                p = jnp.exp2(s * s2 - m)
                total = total + jnp.sum(p, -1, keepdims=True)
                mixed = mixed + jnp.dot(
                    p.astype(BF), k_ref[part_keys, :lat], preferred_element_type=F32
                )
            acc_ref[h * rows : (h + 2) * rows, :] = (mixed / total).astype(BF)

    for seen in range(1, nch + 1):
        pl.when(chain == seen - 1)(functools.partial(attend, seen))
    for load in loads:
        load.wait()
    per = heads // 2
    for h in range(heads):
        av = av_ref[h // per, h % per]
        ho_ref[:, h * vh : (h + 1) * vh] = jnp.dot(
            acc_ref[h * rows : (h + 1) * rows, :], av, preferred_element_type=F32
        ).astype(BF)
    ho = ho_ref[...]
    k, width = op_ref.shape[1:]
    cut = 512 if width % 512 == 0 else width
    for c in range(0, width, cut):
        part_out = (
            jnp.dot(ho[:, :k], op_ref[0, :, c : c + cut], preferred_element_type=F32)
            + jnp.dot(ho[:, k:], op_ref[1, :, c : c + cut], preferred_element_type=F32)
        ).astype(BF)
        at = 0
        for out_ref in (o0, o1, o2, o3, o4):
            out_ref[:, c : c + cut] = part_out[at : at + out_ref.shape[0]]
            at += out_ref.shape[0]


def local(
    query_comp, latent_rows, rope_keys, latent_gain, query_up, absorb_key, absorb_value, out_proj,
    page_owner, page_slot,
):
    nzh, nzl, nch = lax.axis_size("zh"), lax.axis_size("zl"), lax.axis_size("chain")
    zh, zl, core = lax.axis_index("zh"), lax.axis_index("zl"), lax.axis_index("core")
    chain, dec = lax.axis_index("chain"), lax.axis_index("dec")
    pages, part, lat = latent_rows.shape[1:]
    rope = rope_keys.shape[3]
    heads_here, nope = absorb_key.shape[:2]
    vh = absorb_value.shape[2]
    qrows, ql = query_comp.shape[1:]
    width = out_proj.shape[1]
    tp_index = (zh * nzl + zl) * 2 + core
    tp_count = nzh * nzl * 2
    block_len = qrows * tp_count
    slots = 2 * pages
    smem = pl.BlockSpec(memory_space=pltpu.SMEM)
    vm = pl.BlockSpec(memory_space=pltpu.VMEM)
    hbm = pl.BlockSpec(memory_space=pltpu.HBM)

    def room(mib):
        return pltpu.CompilerParams(vmem_limit_bytes=mib * 1024 * 1024)

    rows = qrows * nzh * nzl
    kw = lat + 2 * rope
    heads = 2 * heads_here
    z = zh * nzl + zl
    where = jnp.stack([chain, z, core]).astype(jnp.int32)
    weights = (query_up, absorb_key, absorb_value, out_proj)
    shapes = tuple(w.shape for w in weights)
    keys, page, packed = pl.pallas_call(
        functools.partial(key_kernel, slots=slots, page_len=part * tp_count, shapes=shapes),
        out_shape=(
            jax.ShapeDtypeStruct((pages * part, kw), BF),
            jax.ShapeDtypeStruct((lax.axis_size("dec"), pages * part, kw), BF),
            jax.ShapeDtypeStruct((packed_rows(shapes), 128), BF),
        ),
        in_specs=[smem] * 3 + [vm] * 7,
        out_specs=(vm, vm, vm),
        compiler_params=room(56),
        name="keys",
    )(
        (chain * block_len + tp_index * part).astype(jnp.int32)[None], page_owner, page_slot,
        latent_rows, rope_keys, latent_gain[None], *weights,
    )
    packed = swap_core(packed)

    own = lax.all_gather(keys, Z, axis=0, tiled=True)
    mine = spread(own, "chain").reshape(nch * rows, kw)
    held = lax.optimization_barrier((query_comp[0], own))[0]
    qg = lax.all_gather(held, Z, axis=0, tiled=True)
    qg, mine = lax.optimization_barrier((qg, mine))
    other = swap_core(mine)

    q = pl.pallas_call(
        functools.partial(query_kernel, nope=nope, rope=rope, qrows=qrows, chips=nzh * nzl, shapes=shapes),
        out_shape=jax.ShapeDtypeStruct((heads * rows, kw), BF),
        in_specs=[smem, vm] + [hbm] * 3,
        out_specs=vm,
        scratch_shapes=[
            pltpu.VMEM((rows, ql), BF),
            pltpu.VMEM((2,) + query_up.shape, BF),
            pltpu.VMEM((2,) + absorb_key.shape, BF),
            pltpu.SemaphoreType.DMA((load_count((0, 1), shapes),)),
        ],
        compiler_params=room(12),
        cost_estimate=pl.CostEstimate(
            flops=2 * rows * heads * (nope + rope) * ql + 2 * rows * heads * nope * lat,
            bytes_accessed=6000000, transcendentals=0,
        ),
        name="queries",
    )(where, qg, query_up, absorb_key, packed)

    n = nzh * qrows
    sums = pl.pallas_call(
        functools.partial(
            attend_kernel, rows=rows, lat=lat, scale=(nope + rope) ** -0.5,
            nch=nch, chips=nzh * nzl, qrows=qrows, part=part, shapes=shapes,
        ),
        out_shape=[jax.ShapeDtypeStruct((r, width), BF) for r in (n, n, n, n // 2, n // 2)],
        in_specs=[smem] + [vm] * 3 + [hbm] * 3,
        out_specs=[vm] * 5,
        scratch_shapes=[
            pltpu.VMEM((heads * rows, lat), BF),
            pltpu.VMEM((rows, heads * vh), BF),
            pltpu.VMEM((2,) + absorb_value.shape, BF),
            pltpu.VMEM((2,) + out_proj.shape, BF),
            pltpu.SemaphoreType.DMA((load_count((2, 3), shapes),)),
        ],
        compiler_params=room(28),
        cost_estimate=pl.CostEstimate(
            flops=4 * rows * heads * nch * block_len * lat, bytes_accessed=9000000,
            transcendentals=rows * heads * nch * block_len,
        ),
        name="attend",
    )(where, q, mine, other, absorb_value, out_proj, packed)

    up = shift_z(sums[1], 1)
    down = shift_z(sums[2], -1)
    up2 = shift_z(sums[3], 2)
    down2 = shift_z(sums[4], -2)
    cut = width // 2

    def near(e, up, down):
        at = slice((e + 1) * qrows, (e + 2) * qrows)
        return sums[0][at].astype(F32) + up[at].astype(F32) + down[at].astype(F32)

    far = near(2, up, down).astype(BF)
    far, up, down = lax.optimization_barrier((far, up, down))
    first = shift_z(far[:, :cut], nzl)
    left, right = lax.optimization_barrier((first, shift_z(far[:, cut:], -nzl)))
    ahead = near(1, up, down) + up2[qrows:].astype(F32)
    ahead = jnp.concatenate([ahead[:, :cut] + left.astype(F32), ahead[:, cut:]], -1)
    ahead = shift_z(ahead.astype(BF), nzl)
    behind = near(-1, up, down) + down2[:qrows].astype(F32)
    behind = jnp.concatenate([behind[:, :cut], behind[:, cut:] + right.astype(F32)], -1)
    behind = shift_z(behind.astype(BF), -nzl)
    total = near(0, up, down) + up2[:qrows].astype(F32) + down2[qrows:].astype(F32)
    total = total + ahead.astype(F32) + behind.astype(F32)
    layer_output = total.astype(BF)[None]

    page = lax.optimization_barrier((page, first))[0]
    page = lax.all_to_all(page, "dec", 0, 0, tiled=True).reshape(-1, pages, part, kw)
    came = page[:, :, 0, lat + rope].reshape(-1).astype(jnp.int32)
    take = (came[None, :] == dec * slots + jnp.arange(slots, dtype=jnp.int32)[:, None]).astype(BF)
    placed = jnp.einsum(
        "sp,pjc->sjc", take, page.reshape(-1, part, page.shape[-1]), preferred_element_type=F32
    ).astype(BF)
    cache_latent = placed[..., :lat][None, None]
    cache_rope = placed[..., lat : lat + rope][None, None]
    return (layer_output, cache_latent, cache_rope)


def solution(mesh):
    shape = mesh.shape
    chips = shape["tp"] // 2
    nzl = 4
    fine = Mesh(
        np.asarray(mesh.devices).reshape(shape["chain"], chips // nzl, nzl, 2, shape["dec"]),
        ("chain", "zh", "zl", "core", "dec"),
    )
    row = ("chain",) + TP
    return jax.shard_map(
        local,
        mesh=fine,
        in_specs=(
            P("dec", row, None),
            P("dec", "chain", TP, None),
            P("dec", "chain", TP, None),
            P(),
            P(None, TP),
            P(TP, None, None),
            P(TP, None, None),
            P(TP, None),
            P("dec", "chain"),
            P("dec", "chain"),
        ),
        out_specs=(
            P("dec", row, None),
            P("dec", "chain", None, TP, None),
            P("dec", "chain", None, TP, None),
        ),
        check_vma=False,
    )
```
